32 devices in a mesh: groups: 2 (over y), blk: 4 (over z), heads: 2 (over x), rows: 2 (over core).
Axes of the slice: x: 2, y: 2, z: 4, core: 2. Of those that a mesh axis runs over, the one named last changes fastest.
Arguments:
- queries: bfloat16 [64, 16, 256], P(('groups', 'blk', 'rows'), 'heads'), parts along dimension 0, may hold values from -128 to 128
- src_keys: bfloat16 [12288, 8, 256], P(('groups', 'blk'), 'heads'), parts along dimension 0, may hold values from -6 to 6
- src_values: bfloat16 [12288, 8, 256], P(('groups', 'blk'), 'heads'), parts along dimension 0, may hold values from -6 to 6
- dec_state: bfloat16 [64, 3584], P('groups', ('blk', 'rows')), parts along dimension 0, may hold values from -0.59765625 to 0.59765625
- mask_embed: bfloat16 [3584], P(('blk', 'rows')), may hold values from -1.796875 to 1.796875
- out_weight: bfloat16 [4096, 3584], P('heads', ('blk', 'rows')), may hold values from -0.09375 to 0.09375
- norm_gain: bfloat16 [3584], P(('blk', 'rows')), may hold values from 0.5 to 1.5
- gate_weight: bfloat16 [3584, 14336], P('heads', ('blk', 'rows')), may hold values from -0.09375 to 0.09375
- up_weight: bfloat16 [3584, 14336], P('heads', ('blk', 'rows')), may hold values from -0.09375 to 0.09375
- down_weight: bfloat16 [14336, 3584], P(('blk', 'rows'), 'heads'), may hold values from -0.046875 to 0.046875
- cand_lengths: int32 [2], P('groups'), parts along dimension 0, may hold values from 64 to 128
- masked_pos: int32 [2, 48], P('groups'), parts along dimension 0, may hold values from 0 to 127, as said below
Outputs:
- stream: bfloat16 [64, 3584], P('groups', ('blk', 'rows')), parts along dimension 0
- branch: bfloat16 [64, 3584], P(('groups', 'blk', 'rows'), 'heads'), parts along dimension 0
The draws below stay inside these ranges and needn't reach their ends.
There are 2 independent parts, one for each index of `groups`. The reference program is written for one: setup_inputs(seed, part) draws one part's arguments, and reference() takes and returns one part's arrays. A program takes and returns all parts, laid end to end along the dimension named above; an argument that names none is the same for every part. Nothing has to cross between parts.
Inputs may be any that keep to these rules, and one draw needn't show every extreme that they name: `masked_pos`: the 48 positions of one candidate are distinct.
All inputs are finite; a program needn't handle non-finite values.
Results may differ from the reference program's by a relative error of at most 0.03.
Values may be sent and summed in bfloat16 or wider, within the bound.
No kernel may reach another device: no remote copies, remote signals or barrier semaphores. Data moves between devices by JAX's collectives and lax.ppermute only.
A program may use at most 64 MiB of HBM per device.

```python
import math
import jax
import jax.numpy as jnp
from jax import lax

D = 3584
FF = 14336
QH = 16
KVH = 8
HD = 256
LEN = 128
NMASK = 48
S_DEV = 1536
TOKENS = 32
CAND = 1
SRC = 6144


def source_and_queries(key):
    base_key = jax.random.fold_in(key, 11)
    key_one, key_two = jax.random.split(base_key, 2)
    keys_drawn = jnp.clip(jax.random.normal(key_one, (SRC, KVH, HD), jnp.float32), -6.0, 6.0)
    query_drawn = 2.5 * jnp.clip(jax.random.normal(key_two, (TOKENS, QH, HD), jnp.float32), -6.0, 6.0)
    return (keys_drawn, query_drawn)


def draw_src_keys(key, part):
    return source_and_queries(key)[0].astype(jnp.bfloat16)


def draw_queries(key, part):
    return source_and_queries(key)[1].astype(jnp.bfloat16)


def draw_masked_pos(key, part):
    scores = jax.random.randint(jax.random.fold_in(key, 5), (CAND, LEN), 0, 1 << 20) * LEN
    scores = scores + jnp.arange(LEN, dtype=jnp.int32)[None, :]
    order = jnp.argsort(scores, axis=1)
    return order[:, :NMASK].astype(jnp.int32)


def shard_levels(rng, dims, pieces, smallest, high):
    def one(axis_at, blocks):
        steps = jax.random.uniform(jax.random.fold_in(jax.random.fold_in(rng, 6), axis_at), (blocks,), jnp.float32, smallest / len(pieces), high / len(pieces))
        return jnp.repeat(jnp.exp(steps), dims[axis_at] // blocks).reshape((-1,) + (1,) * (len(dims) - axis_at - 1))

    gain = one(*pieces[0])
    for cut in pieces[1:]:
        gain = gain * one(*cut)
    return gain


def gaussian(rng, extent, deviation, limit, cuts=(), kind=jnp.bfloat16):
    drawn = jax.random.normal(rng, extent, jnp.float32) * deviation
    if len(cuts) > 0:
        drawn = shard_levels(rng, extent, cuts, -0.22, 0.18) * drawn
    return jnp.clip(drawn, min=-limit, max=limit).astype(kind)


def setup_inputs(seed: int = 0, part: int = 0) -> dict:
    arg_keys = jax.random.split(jax.random.key(seed), 13)
    part_splits = jax.random.split(jax.random.fold_in(arg_keys[12], part), 13)
    queries = draw_queries(jax.random.fold_in(jax.random.fold_in(arg_keys[12], part), 71), part)
    src_keys = draw_src_keys(jax.random.fold_in(jax.random.fold_in(arg_keys[12], part), 71), part)
    src_values = gaussian(part_splits[2], (SRC, KVH, HD), 1.0, 6.0, ((0, 4), (1, 2)))
    dec_state = gaussian(part_splits[3], (TOKENS, D), 0.1, 0.59765625, ((1, 8),))
    mask_embed = gaussian(arg_keys[4], (D,), 0.3, 1.796875, ((0, 8),))
    out_weight = gaussian(arg_keys[5], (QH * HD, D), (QH * HD) ** -0.5, 0.09375, ((0, 2), (1, 8)))
    norm_gain = jnp.clip(1.0 + 0.1 * jax.random.normal(arg_keys[6], (D,), jnp.float32), 0.5, 1.5).astype(jnp.bfloat16)
    gate_weight = gaussian(arg_keys[7], (D, FF), D ** -0.5, 0.09375, ((0, 2), (1, 8)))
    up_weight = gaussian(arg_keys[8], (D, FF), D ** -0.5, 0.09375, ((0, 2), (1, 8)))
    down_weight = gaussian(arg_keys[9], (FF, D), FF ** -0.5, 0.046875, ((0, 8), (1, 2)))
    cand_lengths = jax.random.randint(part_splits[10], (CAND,), LEN // 2, LEN + 1).astype(jnp.int32)
    masked_pos = draw_masked_pos(jax.random.fold_in(jax.random.fold_in(arg_keys[12], part), 71), part)
    return {"queries": queries, "src_keys": src_keys, "src_values": src_values, "dec_state": dec_state, "mask_embed": mask_embed, "out_weight": out_weight, "norm_gain": norm_gain, "gate_weight": gate_weight, "up_weight": up_weight, "down_weight": down_weight, "cand_lengths": cand_lengths, "masked_pos": masked_pos}


def token_masks(cand_lengths, masked_pos, tokens):
    positions = jnp.arange(tokens, dtype=jnp.int32) % LEN
    length_tok = jnp.repeat(cand_lengths, LEN)[:tokens]
    valid_tok = positions < length_tok
    slots = jnp.arange(LEN, dtype=jnp.int32)
    masked_tok = jnp.any(masked_pos[:, :, None] == slots[None, None, :], axis=1).reshape(-1)[:tokens]
    return (valid_tok, masked_tok)

def reference(queries, src_keys, src_values, dec_state, mask_embed, out_weight, norm_gain, gate_weight, up_weight, down_weight, cand_lengths, masked_pos):
    tokens = queries.shape[0]
    group_size = QH // KVH
    row_block = math.gcd(tokens, 32)
    src_blocks = SRC // S_DEV
    keys_wide = src_keys.astype(jnp.float32)
    values_wide = src_values.astype(jnp.float32).reshape(src_blocks, S_DEV, KVH, HD)
    score_scale = HD ** (-0.5)

    def attend(query_rows):
        grouped = query_rows.astype(jnp.float32).reshape(row_block, KVH, group_size, HD)
        scores = jnp.einsum('tgjd,kgd->tgjk', grouped, keys_wide, precision=lax.Precision.HIGHEST) * score_scale
        scores = scores.reshape(row_block, KVH, group_size, src_blocks, S_DEV)
        block_peak = lax.optimization_barrier(jnp.max(scores, axis=4))
        weights = jnp.exp(scores - block_peak[..., None])
        block_totals = lax.optimization_barrier(jnp.sum(weights, axis=4))
        rounded = weights.astype(jnp.bfloat16).astype(jnp.float32)
        block_numer = jnp.einsum('tgjbk,bkgd->tgjbd', rounded, values_wide, precision=lax.Precision.HIGHEST)
        top = lax.optimization_barrier(jnp.max(block_peak, axis=3, keepdims=True))
        factor = jnp.exp(block_peak - top)
        numerator = lax.optimization_barrier(jnp.sum(block_numer * factor[..., None], axis=3))
        totals = lax.optimization_barrier(jnp.sum(block_totals * factor, axis=3))
        return (numerator / totals[..., None]).astype(jnp.bfloat16).reshape(row_block, QH * HD)
    blocks = queries.reshape(tokens // row_block, row_block, QH, HD)
    attn_out = lax.map(attend, blocks).reshape(tokens, QH * HD)
    projected = jnp.dot(attn_out, out_weight, preferred_element_type=jnp.float32)
    valid_tok, masked_tok = token_masks(cand_lengths, masked_pos, tokens)
    base_state = jnp.where(masked_tok[:, None], mask_embed[None, :], dec_state).astype(jnp.float32)
    stream_mid = base_state + projected
    inv_rms = lax.rsqrt(lax.optimization_barrier(jnp.mean(stream_mid * stream_mid, axis=1, keepdims=True)) + 1e-06)
    normed = (stream_mid * inv_rms * norm_gain.astype(jnp.float32)).astype(jnp.bfloat16)
    gate_rows = jnp.dot(normed, gate_weight, preferred_element_type=jnp.float32)
    up_rows = jnp.dot(normed, up_weight, preferred_element_type=jnp.float32)
    hidden = (jax.nn.gelu(gate_rows, approximate=True) * up_rows).astype(jnp.bfloat16)
    down_out = jnp.dot(hidden, down_weight, preferred_element_type=jnp.float32)
    keep_mask = valid_tok.astype(jnp.float32)[:, None]
    return ((stream_mid * keep_mask).astype(jnp.bfloat16), (down_out * keep_mask).astype(jnp.bfloat16))
```

```python
import jax
import jax.numpy as jnp
from jax import lax
from jax.sharding import PartitionSpec as P

LEN = 128
EPS = 1e-06
BF = jnp.bfloat16
F32 = jnp.float32


def token_masks(cand_lengths, masked_pos, tokens):
    positions = jnp.arange(tokens, dtype=jnp.int32) % LEN
    length_tok = jnp.repeat(cand_lengths, LEN)[:tokens]
    valid_tok = positions < length_tok
    slots = jnp.arange(LEN, dtype=jnp.int32)
    masked_tok = jnp.any(masked_pos[:, :, None] == slots[None, None, :], axis=1).reshape(-1)[
        :tokens
    ]
    return (valid_tok, masked_tok)


def shards_any(
    queries,
    src_keys,
    src_values,
    dec_state,
    mask_embed,
    out_weight,
    norm_gain,
    gate_weight,
    up_weight,
    down_weight,
    cand_lengths,
    masked_pos,
):
    tok_dev, local_heads, head_size = queries.shape
    kv_local = src_keys.shape[1]
    group_size = local_heads // kv_local
    score_scale = head_size ** (-0.5)
    features = dec_state.shape[1] * lax.axis_size("blk") * lax.axis_size("rows")
    queries_all = lax.all_gather(queries, "blk", axis=0, tiled=True)
    gathered_rows = queries_all.shape[0]
    grouped = queries_all.reshape(gathered_rows, kv_local, group_size, head_size)
    scores = (
        jnp.einsum("tgjd,kgd->tgjk", grouped, src_keys, preferred_element_type=F32) * score_scale
    )
    local_peak = jnp.max(scores, axis=3)
    weights = jnp.exp(scores - local_peak[..., None])
    totals = jnp.sum(weights, axis=3)
    numerator = jnp.einsum(
        "tgjk,kgd->tgjd", weights.astype(BF), src_values, preferred_element_type=F32
    )
    highest = lax.pmax(local_peak, "blk")
    factor = jnp.exp(local_peak - highest)
    numer_own, totals_own = (
        lax.psum_scatter(
            (numerator * factor[..., None]).astype(BF), "blk", scatter_dimension=0, tiled=True
        ).astype(F32),
        lax.psum_scatter(
            (totals * factor).astype(BF), "blk", scatter_dimension=0, tiled=True
        ).astype(F32),
    )
    attn_own = (
        (numer_own / totals_own[..., None]).astype(BF).reshape(tok_dev, local_heads * head_size)
    )
    attn_all = lax.all_gather(attn_own, ("blk", "rows"), axis=0, tiled=True)
    tokens = attn_all.shape[0]
    projected = lax.psum(
        jnp.dot(attn_all, out_weight, preferred_element_type=F32).astype(BF), "heads"
    ).astype(F32)
    valid_tok, masked_tok = token_masks(cand_lengths, masked_pos, tokens)
    base_state = jnp.where(masked_tok[:, None], mask_embed[None, :], dec_state).astype(F32)
    stream_mid = base_state + projected
    squares = lax.psum(jnp.sum(stream_mid * stream_mid, axis=1), ("blk", "rows"))
    inv_rms = lax.rsqrt(squares / features + EPS)[:, None]
    normed = (stream_mid * inv_rms * norm_gain.astype(F32)).astype(BF)
    keep_mask = valid_tok.astype(F32)[:, None]
    stream = (stream_mid * keep_mask).astype(BF)
    normed_full = lax.all_gather(normed, ("blk", "rows"), axis=1, tiled=True)
    feature_width = gate_weight.shape[0]
    column_block = lax.dynamic_slice_in_dim(
        normed_full, lax.axis_index("heads") * feature_width, feature_width, 1
    )
    gate_part = jnp.dot(column_block, gate_weight, preferred_element_type=F32)
    up_part = jnp.dot(column_block, up_weight, preferred_element_type=F32)
    gate_rows, up_rows = (
        lax.psum(gate_part.astype(BF), "heads").astype(F32),
        lax.psum(up_part.astype(BF), "heads").astype(F32),
    )
    hidden = (jax.nn.gelu(gate_rows, approximate=True) * up_rows).astype(BF)
    down_out = lax.psum_scatter(
        jnp.dot(hidden, down_weight, preferred_element_type=F32),
        ("blk", "rows"),
        scatter_dimension=0,
        tiled=True,
    )
    own_start = (lax.axis_index("blk") * lax.axis_size("rows") + lax.axis_index("rows")) * tok_dev
    keep_own = lax.dynamic_slice_in_dim(keep_mask, own_start, tok_dev, 0)
    return (stream, (down_out * keep_own).astype(BF))


def hop(value, axis, size, step):
    return lax.ppermute(value, axis, [(i, i ^ step) for i in range(size)])


def by_index(pieces, at):
    return [lax.select_n(at ^ k, *pieces) for k in range(len(pieces))]


def shards_direct(
    queries,
    src_keys,
    src_values,
    dec_state,
    mask_embed,
    out_weight,
    norm_gain,
    gate_weight,
    up_weight,
    down_weight,
    cand_lengths,
    masked_pos,
):
    blks, head_parts = lax.axis_size("blk"), lax.axis_size("heads")
    blk, head, row = (lax.axis_index(name) for name in ("blk", "heads", "rows"))
    tok_dev, local_heads, head_size = queries.shape
    kv_local = src_keys.shape[1]
    group_size = local_heads // kv_local
    score_scale = head_size ** (-0.5)
    width = dec_state.shape[1]
    features = width * blks * 2
    half = blks // head_parts

    pieces = [queries] + [hop(queries, "blk", blks, s) for s in range(1, blks)]
    q_all = jnp.concatenate(by_index(pieces, blk), axis=0)
    rows_in = q_all.shape[0]
    grouped = q_all.reshape(rows_in, kv_local, group_size, head_size)
    scores = (
        jnp.einsum("tgjd,kgd->tgjk", grouped, src_keys, preferred_element_type=F32) * score_scale
    )
    peak = jnp.max(scores, axis=3)
    weights = jnp.exp(scores - peak[..., None])
    totals = jnp.sum(weights, axis=3)
    numerator = jnp.einsum(
        "tgjk,kgd->tgjd", weights.astype(BF), src_values, preferred_element_type=F32
    )
    partial = (numerator / totals[..., None]).astype(BF)
    level = peak + jnp.log(totals)
    partials = [partial] + [hop(partial, "blk", blks, s) for s in range(1, blks)]
    levels = [level] + [hop(level, "blk", blks, s) for s in range(1, blks)]
    top = levels[0]
    for one in levels[1:]:
        top = jnp.maximum(top, one)
    shares = [jnp.exp(one - top) for one in levels]
    total = sum(shares)
    attn = sum(
        (share / total)[..., None] * part.astype(F32) for share, part in zip(shares, partials)
    )
    attn = attn.astype(BF).reshape(rows_in, local_heads * head_size)
    other = hop(attn, "rows", 2, 1)
    attn_all = jnp.stack(by_index([attn, other], row), axis=0)
    attn_all = attn_all.reshape(2, blks, tok_dev, -1).transpose(1, 0, 2, 3)
    tokens = rows_in * 2
    attn_all = attn_all.reshape(tokens, -1)
    projected = jnp.dot(attn_all, out_weight, preferred_element_type=F32).astype(BF)
    projected = projected.astype(F32) + hop(projected, "heads", 2, 1).astype(F32)
    valid_tok, masked_tok = token_masks(cand_lengths, masked_pos, tokens)
    base_state = jnp.where(masked_tok[:, None], mask_embed[None, :], dec_state).astype(F32)
    mid = base_state + projected
    keep_mask = valid_tok.astype(F32)[:, None]
    stream = (mid * keep_mask).astype(BF)
    squares = jnp.sum(mid * mid, axis=1)
    scaled = (mid * norm_gain.astype(F32)).astype(BF)

    def spread(value):
        got = [value]
        for s in range(1, blks):
            pairs = []
            for b in range(blks):
                h = b // half
                pairs.append((b * head_parts + h, (b ^ s) * head_parts + h))
            got.append(lax.ppermute(value, ("blk", "heads"), pairs))
        return [lax.select_n(blk ^ (head * half + k), *got) for k in range(half)]

    tiles, square_tiles = spread(scaled), spread(squares)
    mine = jnp.stack(tiles, axis=0)
    theirs = hop(mine, "rows", 2, 1)
    pair = jnp.stack(by_index([mine, theirs], row), axis=0)
    column_block = pair.transpose(2, 1, 0, 3).reshape(tokens, -1)
    squares = sum(square_tiles)
    squares = squares + hop(squares, "rows", 2, 1)
    squares = squares + hop(squares, "heads", 2, 1)
    inv_rms = lax.rsqrt(squares / features + EPS)[:, None]
    gate = jnp.dot(column_block, gate_weight, preferred_element_type=F32)
    gate = gate + hop(gate.astype(BF), "heads", 2, 1).astype(F32)
    up = jnp.dot(column_block, up_weight, preferred_element_type=F32)
    up = up + hop(up.astype(BF), "heads", 2, 1).astype(F32)
    hidden = (jax.nn.gelu(gate * inv_rms, approximate=True) * (up * inv_rms)).astype(BF)
    down = jnp.dot(hidden, down_weight, preferred_element_type=F32)
    down = down.reshape(blks, 2, tok_dev, -1)
    keep = lax.dynamic_index_in_dim(down, row, 1, keepdims=False)
    away = lax.dynamic_index_in_dim(down, 1 - row, 1, keepdims=False).astype(BF)
    keep = keep + hop(away, "rows", 2, 1).astype(F32)
    sent = keep.astype(BF)
    own = lax.dynamic_index_in_dim(keep, blk, 0, keepdims=False)
    for s in range(1, blks):
        part = lax.dynamic_index_in_dim(sent, blk ^ s, 0, keepdims=False)
        own = own + hop(part, "blk", blks, s).astype(F32)
    keep_own = lax.dynamic_slice_in_dim(keep_mask, (blk * 2 + row) * tok_dev, tok_dev, 0)
    return (stream, (own * keep_own).astype(BF))


def solution(mesh):
    size = dict(mesh.shape)
    direct = size["blk"] in (2, 4, 8) and size["heads"] == 2 and size["rows"] == 2
    placed = (
        P(("groups", "blk", "rows"), "heads", None),
        P(("groups", "blk"), "heads", None),
        P(("groups", "blk"), "heads", None),
        P("groups", ("blk", "rows")),
        P(("blk", "rows")),
        P("heads", ("blk", "rows")),
        P(("blk", "rows")),
        P("heads", ("blk", "rows")),
        P("heads", ("blk", "rows")),
        P(("blk", "rows"), "heads"),
        P("groups"),
        P("groups", None),
    )
    return jax.shard_map(
        shards_direct if direct else shards_any,
        mesh=mesh,
        in_specs=placed,
        out_specs=(P("groups", ("blk", "rows")), P(("groups", "blk", "rows"), "heads")),
        check_vma=False,
    )
```

```python
import jax
import jax.numpy as jnp
from jax import lax
from jax.experimental import pallas as pl
from jax.experimental.pallas import tpu as pltpu
from jax.sharding import PartitionSpec as P

LEN = 128
EPS = 1e-06
BF = jnp.bfloat16
F32 = jnp.float32


def token_masks(cand_lengths, masked_pos, tokens):
    positions = jnp.arange(tokens, dtype=jnp.int32) % LEN
    length_tok = jnp.repeat(cand_lengths, LEN)[:tokens]
    valid_tok = positions < length_tok
    slots = jnp.arange(LEN, dtype=jnp.int32)
    masked_tok = jnp.any(masked_pos[:, :, None] == slots[None, None, :], axis=1).reshape(-1)[
        :tokens
    ]
    return (valid_tok, masked_tok)


def shards_any(
    queries,
    src_keys,
    src_values,
    dec_state,
    mask_embed,
    out_weight,
    norm_gain,
    gate_weight,
    up_weight,
    down_weight,
    cand_lengths,
    masked_pos,
):
    tok_dev, local_heads, head_size = queries.shape
    kv_local = src_keys.shape[1]
    group_size = local_heads // kv_local
    score_scale = head_size ** (-0.5)
    features = dec_state.shape[1] * lax.axis_size("blk") * lax.axis_size("rows")
    queries_all = lax.all_gather(queries, "blk", axis=0, tiled=True)
    gathered_rows = queries_all.shape[0]
    grouped = queries_all.reshape(gathered_rows, kv_local, group_size, head_size)
    scores = (
        jnp.einsum("tgjd,kgd->tgjk", grouped, src_keys, preferred_element_type=F32) * score_scale
    )
    local_peak = jnp.max(scores, axis=3)
    weights = jnp.exp(scores - local_peak[..., None])
    totals = jnp.sum(weights, axis=3)
    numerator = jnp.einsum(
        "tgjk,kgd->tgjd", weights.astype(BF), src_values, preferred_element_type=F32
    )
    highest = lax.pmax(local_peak, "blk")
    factor = jnp.exp(local_peak - highest)
    numer_own, totals_own = (
        lax.psum_scatter(
            (numerator * factor[..., None]).astype(BF), "blk", scatter_dimension=0, tiled=True
        ).astype(F32),
        lax.psum_scatter(
            (totals * factor).astype(BF), "blk", scatter_dimension=0, tiled=True
        ).astype(F32),
    )
    attn_own = (
        (numer_own / totals_own[..., None]).astype(BF).reshape(tok_dev, local_heads * head_size)
    )
    attn_all = lax.all_gather(attn_own, ("blk", "rows"), axis=0, tiled=True)
    tokens = attn_all.shape[0]
    projected = lax.psum(
        jnp.dot(attn_all, out_weight, preferred_element_type=F32).astype(BF), "heads"
    ).astype(F32)
    valid_tok, masked_tok = token_masks(cand_lengths, masked_pos, tokens)
    base_state = jnp.where(masked_tok[:, None], mask_embed[None, :], dec_state).astype(F32)
    stream_mid = base_state + projected
    squares = lax.psum(jnp.sum(stream_mid * stream_mid, axis=1), ("blk", "rows"))
    inv_rms = lax.rsqrt(squares / features + EPS)[:, None]
    normed = (stream_mid * inv_rms * norm_gain.astype(F32)).astype(BF)
    keep_mask = valid_tok.astype(F32)[:, None]
    stream = (stream_mid * keep_mask).astype(BF)
    normed_full = lax.all_gather(normed, ("blk", "rows"), axis=1, tiled=True)
    feature_width = gate_weight.shape[0]
    column_block = lax.dynamic_slice_in_dim(
        normed_full, lax.axis_index("heads") * feature_width, feature_width, 1
    )
    gate_part = jnp.dot(column_block, gate_weight, preferred_element_type=F32)
    up_part = jnp.dot(column_block, up_weight, preferred_element_type=F32)
    gate_rows, up_rows = (
        lax.psum(gate_part.astype(BF), "heads").astype(F32),
        lax.psum(up_part.astype(BF), "heads").astype(F32),
    )
    hidden = (jax.nn.gelu(gate_rows, approximate=True) * up_rows).astype(BF)
    down_out = lax.psum_scatter(
        jnp.dot(hidden, down_weight, preferred_element_type=F32),
        ("blk", "rows"),
        scatter_dimension=0,
        tiled=True,
    )
    own_start = (lax.axis_index("blk") * lax.axis_size("rows") + lax.axis_index("rows")) * tok_dev
    keep_own = lax.dynamic_slice_in_dim(keep_mask, own_start, tok_dev, 0)
    return (stream, (down_out * keep_own).astype(BF))


VM = pl.BlockSpec(memory_space=pltpu.VMEM)
SM = pl.BlockSpec(memory_space=pltpu.SMEM)
ANY = pl.BlockSpec(memory_space=pl.ANY)
MIB = 1 << 20


def hop(value, axis, size, step):
    return lax.ppermute(value, axis, [(i, i ^ step) for i in range(size)])


def by_index(pieces, at):
    return [lax.select_n(at ^ k, *pieces) for k in range(len(pieces))]


def kernel(body, name, outs, specs, args, limit=8, flops=0):
    size = sum(a.size * a.dtype.itemsize for a in list(args) + list(outs))
    return pl.pallas_call(
        body,
        out_shape=outs,
        in_specs=specs,
        out_specs=[VM] * len(outs),
        compiler_params=pltpu.CompilerParams(vmem_limit_bytes=limit * MIB),
        cost_estimate=pl.CostEstimate(flops=flops, bytes_accessed=size, transcendentals=0),
        name=name,
    )(*args)


def fetch(after, arrays, name):
    n = len(arrays)

    def body(*refs):
        sources, targets, sems = refs[1 : 1 + n], refs[1 + n : 1 + 2 * n], refs[1 + 2 * n]
        copies = [
            pltpu.make_async_copy(sources[i], targets[i], sems.at[i]) for i in range(n)
        ]
        for copy in copies:
            copy.start()
        for copy in copies:
            copy.wait()

    size = sum(a.size * a.dtype.itemsize for a in arrays)
    return pl.pallas_call(
        body,
        out_shape=[jax.ShapeDtypeStruct(a.shape, a.dtype) for a in arrays],
        in_specs=[ANY] * (1 + n),
        out_specs=[VM] * n,
        scratch_shapes=[pltpu.SemaphoreType.DMA((n,))],
        compiler_params=pltpu.CompilerParams(vmem_limit_bytes=MIB),
        cost_estimate=pl.CostEstimate(flops=0, bytes_accessed=2 * size, transcendentals=0),
        name=name,
    )(after, *[pltpu.with_memory_space_constraint(a, pltpu.HBM) for a in arrays])


def parts_of(value, count):
    out = []
    for _ in range(count):
        part = lax.reduce_precision(value, 8, 7)
        out.append(part.astype(BF))
        value = value - part
    return out


def split_in(value, count):
    out = []
    for _ in range(count):
        part = value.astype(BF)
        out.append(part)
        value = value - part.astype(F32)
    return out


def shards_direct(
    queries,
    src_keys,
    src_values,
    dec_state,
    mask_embed,
    out_weight,
    norm_gain,
    gate_weight,
    up_weight,
    down_weight,
    cand_lengths,
    masked_pos,
):
    blks, head_parts = lax.axis_size("blk"), lax.axis_size("heads")
    blk, head, row = (lax.axis_index(name) for name in ("blk", "heads", "rows"))
    tok_dev, local_heads, head_size = queries.shape
    kv_local = src_keys.shape[1]
    group_size = local_heads // kv_local
    score_scale = head_size ** (-0.5)
    width = dec_state.shape[1]
    features = width * blks * 2
    half = blks // head_parts
    hidden_width, out_width = gate_weight.shape[1], down_weight.shape[1]
    toks = tok_dev * blks
    tokens = toks * 2
    place = jnp.stack([row, blk, head]).astype(jnp.int32)
    sds = jax.ShapeDtypeStruct

    pieces = [queries] + [hop(queries, "blk", blks, s) for s in range(1, blks)]
    keys_near, proj_near = fetch(queries, [src_keys, out_weight.T], "fetch_keys_proj")
    q_all = jnp.concatenate(by_index(pieces, blk), axis=0)
    grouped = q_all.reshape(toks, kv_local, group_size, head_size)
    scores = (
        jnp.einsum("tgjd,kgd->tgjk", grouped, keys_near, preferred_element_type=F32) * score_scale
    )
    peak = jnp.max(scores, axis=3)
    weights = jnp.exp(scores - peak[..., None])
    totals = jnp.sum(weights, axis=3)
    numerator = jnp.einsum(
        "tgjk,kgd->tgjd", weights.astype(BF), src_values, preferred_element_type=F32
    )
    partial = (numerator / totals[..., None]).astype(BF)
    partial = partial.transpose(1, 2, 0, 3).reshape(local_heads * toks, head_size)
    level = (peak + jnp.log(totals)).reshape(toks, local_heads)
    side = jnp.concatenate(parts_of(level, 3), axis=1)
    side = jnp.pad(side, ((0, 0), (0, head_size - side.shape[1])))
    note = jnp.concatenate([partial, side], axis=0)
    notes = [note] + [hop(note, "blk", blks, s) for s in range(1, blks)]
    (gate_near,) = fetch(note, [gate_weight], "fetch_gate")

    def combine(*refs):
        ins, out = refs[:-1], refs[-1]
        base = local_heads * toks
        levels = []
        for ref in ins:
            side = ref[base : base + toks, :].astype(F32)
            levels.append(
                side[:, :local_heads]
                + side[:, local_heads : 2 * local_heads]
                + side[:, 2 * local_heads : 3 * local_heads]
            )
        top = levels[0]
        for one in levels[1:]:
            top = jnp.maximum(top, one)
        shares = [jnp.exp(one - top) for one in levels]
        total = shares[0]
        for one in shares[1:]:
            total = total + one
        shares = [one / total for one in shares]
        for h in range(local_heads):
            acc = None
            for share, ref in zip(shares, ins):
                term = share[:, h : h + 1] * ref[h * toks : (h + 1) * toks, :].astype(F32)
                acc = term if acc is None else acc + term
            out[:, h * head_size : (h + 1) * head_size] = acc.astype(BF)

    (attn,) = kernel(
        combine, "combine", [sds((toks, local_heads * head_size), BF)], [VM] * blks, notes
    )
    other = hop(attn, "rows", 2, 1)

    def project(place_ref, own_ref, other_ref, weight_ref, out_ref):
        first = place_ref[0] == 0
        own, other = own_ref[...], other_ref[...]
        rows = jnp.concatenate(
            [jnp.where(first, own, other), jnp.where(first, other, own)], axis=0
        )
        out_ref[...] = lax.dot_general(
            rows, weight_ref[...], (((1,), (1,)), ((), ())), preferred_element_type=F32
        ).astype(BF)

    (proj,) = kernel(
        project,
        "project",
        [sds((tokens, width), BF)],
        [SM, VM, VM, VM],
        [place, attn, other, proj_near],
    )
    proj_other = hop(proj, "heads", 2, 1)
    (up_near,) = fetch(proj, [up_weight], "fetch_up")

    def inner(value):
        value = value.reshape((blks, 2, tok_dev) + value.shape[1:])
        return jnp.swapaxes(value, 0, 1).reshape((tokens,) + value.shape[3:])

    valid_tok, masked_tok = token_masks(cand_lengths, masked_pos, tokens)
    base_state = inner(jnp.where(masked_tok[:, None], mask_embed[None, :], dec_state))
    keep_mask = valid_tok.astype(F32)
    keep_inner = inner(keep_mask)[:, None]
    lanes = -(-(width + 2) // 128) * 128

    def middle(base_ref, keep_ref, gain_ref, own_ref, other_ref, stream_ref, note_ref):
        mid = base_ref[...].astype(F32) + (own_ref[...].astype(F32) + other_ref[...].astype(F32))
        stream_ref[...] = (mid * keep_ref[...]).astype(BF)
        note_ref[:, :width] = (mid * gain_ref[...].astype(F32)).astype(BF)
        squares = jnp.sum(mid * mid, axis=1, keepdims=True)
        high, low = split_in(squares, 2)
        lane = lax.broadcasted_iota(jnp.int32, (tokens, lanes - width), 1)
        note_ref[:, width:] = jnp.where(
            lane == 0, high.astype(F32), jnp.where(lane == 1, low.astype(F32), 0.0)
        ).astype(BF)

    stream, note = kernel(
        middle,
        "middle",
        [sds((tokens, width), BF), sds((tokens, lanes), BF)],
        [VM] * 5,
        [base_state, keep_inner, norm_gain[None, :], proj, proj_other],
    )

    got = [note]
    for s in range(1, blks):
        pairs = []
        for b in range(blks):
            h = b // half
            pairs.append((b * head_parts + h, (b ^ s) * head_parts + h))
        got.append(lax.ppermute(note, ("blk", "heads"), pairs))
    (down_near,) = fetch(note, [down_weight], "fetch_down")
    mine = jnp.stack([lax.select_n(blk ^ (head * half + k), *got) for k in range(half)], axis=0)
    theirs = hop(mine, "rows", 2, 1)

    def column_block(place_ref, mine_ref, theirs_ref):
        first = place_ref[0] == 0
        tiles = []
        for k in range(half):
            own, other = mine_ref[k], theirs_ref[k]
            tiles += [jnp.where(first, own, other), jnp.where(first, other, own)]
        return tiles

    rows_in = gate_weight.shape[0]

    def gates(place_ref, mine_ref, theirs_ref, weight_ref, out_ref, note_ref, x_ref):
        tiles = column_block(place_ref, mine_ref, theirs_ref)
        squares = None
        for j, tile in enumerate(tiles):
            x_ref[:, j * width : (j + 1) * width] = tile[:, :width]
            here = tile[:, width : width + 2].astype(F32)
            squares = here if squares is None else squares + here
        squares = squares[:, 0:1] + squares[:, 1:2]
        gate = jnp.dot(x_ref[...], weight_ref[...], preferred_element_type=F32)
        out_ref[:, :hidden_width] = gate
        note_ref[:, :hidden_width] = gate.astype(BF)
        high, low = split_in(squares, 2)
        lane = lax.broadcasted_iota(jnp.int32, (tokens, 128), 1)
        out_ref[:, hidden_width:] = jnp.where(lane == 0, squares, 0.0)
        note_ref[:, hidden_width:] = jnp.where(
            lane == 0, high.astype(F32), jnp.where(lane == 1, low.astype(F32), 0.0)
        ).astype(BF)

    long_width = hidden_width + 128
    gate, gate_note, column = kernel(
        gates,
        "gates",
        [sds((tokens, long_width), F32), sds((tokens, long_width), BF), sds((tokens, rows_in), BF)],
        [SM, VM, VM, VM],
        [place, mine, theirs, gate_near],
    )
    gate_other = hop(gate_note, "heads", 2, 1)

    def ups(x_ref, weight_ref, out_ref, note_ref):
        up = jnp.dot(x_ref[...], weight_ref[...], preferred_element_type=F32)
        out_ref[...] = up
        note_ref[...] = up.astype(BF)

    up, up_note = kernel(
        ups,
        "ups",
        [sds((tokens, hidden_width), F32), sds((tokens, hidden_width), BF)],
        [VM, VM],
        [column, up_near],
        flops=2 * tokens * rows_in * hidden_width,
    )
    up_other = hop(up_note, "heads", 2, 1)

    def downs(
        place_ref, gate_ref, gate_other_ref, up_ref, up_other_ref, weight_ref, keep_ref, away_ref
    ):
        other = gate_other_ref[:, hidden_width:].astype(F32)
        squares = gate_ref[:, hidden_width : hidden_width + 1] + other[:, 0:1] + other[:, 1:2]
        inv_rms = lax.rsqrt(squares / features + EPS)
        gate = (gate_ref[:, :hidden_width] + gate_other_ref[:, :hidden_width].astype(F32)) * inv_rms
        up = (up_ref[...] + up_other_ref[...].astype(F32)) * inv_rms
        hidden = (jax.nn.gelu(gate, approximate=True) * up).astype(BF)
        down = jnp.dot(hidden, weight_ref[...], preferred_element_type=F32)
        first = place_ref[0] == 0
        keep_ref[...] = jnp.where(first, down[:toks], down[toks:])
        away_ref[...] = jnp.where(first, down[toks:], down[:toks]).astype(BF)

    keep, away = kernel(
        downs,
        "downs",
        [sds((toks, out_width), F32), sds((toks, out_width), BF)],
        [SM] + [VM] * 5,
        [place, gate, gate_other, up, up_other, down_near],
        limit=12,
    )
    back = hop(away, "rows", 2, 1)

    def owners(place_ref, keep_ref, back_ref, own_ref, *piece_refs):
        total = keep_ref[...] + back_ref[...].astype(F32)
        blocks = [total[k * tok_dev : (k + 1) * tok_dev] for k in range(blks)]
        at = place_ref[1]
        for s, ref in enumerate((own_ref,) + piece_refs):
            value = blocks[0]
            for k in range(1, blks):
                value = jnp.where(at == (k ^ s), blocks[k], value)
            ref[...] = value.astype(ref.dtype)

    own, *sends = kernel(
        owners,
        "owners",
        [sds((tok_dev, out_width), F32)] + [sds((tok_dev, out_width), BF)] * (blks - 1),
        [SM, VM, VM],
        [place, keep, back],
    )
    for s in range(1, blks):
        own = own + hop(sends[s - 1], "blk", blks, s).astype(F32)
    keep_own = lax.dynamic_slice_in_dim(keep_mask, (blk * 2 + row) * tok_dev, tok_dev, 0)
    branch = (own * keep_own[:, None]).astype(BF)
    stream = stream.reshape(2, blks, tok_dev, width).swapaxes(0, 1).reshape(tokens, width)
    return (stream, branch)


def solution(mesh):
    size = dict(mesh.shape)
    direct = size["blk"] in (2, 4, 8) and size["heads"] == 2 and size["rows"] == 2
    placed = (
        P(("groups", "blk", "rows"), "heads", None),
        P(("groups", "blk"), "heads", None),
        P(("groups", "blk"), "heads", None),
        P("groups", ("blk", "rows")),
        P(("blk", "rows")),
        P("heads", ("blk", "rows")),
        P(("blk", "rows")),
        P("heads", ("blk", "rows")),
        P("heads", ("blk", "rows")),
        P(("blk", "rows"), "heads"),
        P("groups"),
        P("groups", None),
    )
    return jax.shard_map(
        shards_direct if direct else shards_any,
        mesh=mesh,
        in_specs=placed,
        out_specs=(P("groups", ("blk", "rows")), P(("groups", "blk", "rows"), "heads")),
        check_vma=False,
    )
```

```python
import jax
import jax.numpy as jnp
from jax import lax
from jax.experimental import pallas as pl
from jax.experimental.pallas import tpu as pltpu
from jax.sharding import PartitionSpec as P

LEN = 128
EPS = 1e-06
BF = jnp.bfloat16
F32 = jnp.float32


def token_masks(cand_lengths, masked_pos, tokens):
    positions = jnp.arange(tokens, dtype=jnp.int32) % LEN
    length_tok = jnp.repeat(cand_lengths, LEN)[:tokens]
    valid_tok = positions < length_tok
    slots = jnp.arange(LEN, dtype=jnp.int32)
    masked_tok = jnp.any(masked_pos[:, :, None] == slots[None, None, :], axis=1).reshape(-1)[
        :tokens
    ]
    return (valid_tok, masked_tok)


def shards_any(
    queries,
    src_keys,
    src_values,
    dec_state,
    mask_embed,
    out_weight,
    norm_gain,
    gate_weight,
    up_weight,
    down_weight,
    cand_lengths,
    masked_pos,
):
    tok_dev, local_heads, head_size = queries.shape
    kv_local = src_keys.shape[1]
    group_size = local_heads // kv_local
    score_scale = head_size ** (-0.5)
    features = dec_state.shape[1] * lax.axis_size("blk") * lax.axis_size("rows")
    queries_all = lax.all_gather(queries, "blk", axis=0, tiled=True)
    gathered_rows = queries_all.shape[0]
    grouped = queries_all.reshape(gathered_rows, kv_local, group_size, head_size)
    scores = (
        jnp.einsum("tgjd,kgd->tgjk", grouped, src_keys, preferred_element_type=F32) * score_scale
    )
    local_peak = jnp.max(scores, axis=3)
    weights = jnp.exp(scores - local_peak[..., None])
    totals = jnp.sum(weights, axis=3)
    numerator = jnp.einsum(
        "tgjk,kgd->tgjd", weights.astype(BF), src_values, preferred_element_type=F32
    )
    highest = lax.pmax(local_peak, "blk")
    factor = jnp.exp(local_peak - highest)
    numer_own, totals_own = (
        lax.psum_scatter(
            (numerator * factor[..., None]).astype(BF), "blk", scatter_dimension=0, tiled=True
        ).astype(F32),
        lax.psum_scatter(
            (totals * factor).astype(BF), "blk", scatter_dimension=0, tiled=True
        ).astype(F32),
    )
    attn_own = (
        (numer_own / totals_own[..., None]).astype(BF).reshape(tok_dev, local_heads * head_size)
    )
    attn_all = lax.all_gather(attn_own, ("blk", "rows"), axis=0, tiled=True)
    tokens = attn_all.shape[0]
    projected = lax.psum(
        jnp.dot(attn_all, out_weight, preferred_element_type=F32).astype(BF), "heads"
    ).astype(F32)
    valid_tok, masked_tok = token_masks(cand_lengths, masked_pos, tokens)
    base_state = jnp.where(masked_tok[:, None], mask_embed[None, :], dec_state).astype(F32)
    stream_mid = base_state + projected
    squares = lax.psum(jnp.sum(stream_mid * stream_mid, axis=1), ("blk", "rows"))
    inv_rms = lax.rsqrt(squares / features + EPS)[:, None]
    normed = (stream_mid * inv_rms * norm_gain.astype(F32)).astype(BF)
    keep_mask = valid_tok.astype(F32)[:, None]
    stream = (stream_mid * keep_mask).astype(BF)
    normed_full = lax.all_gather(normed, ("blk", "rows"), axis=1, tiled=True)
    feature_width = gate_weight.shape[0]
    column_block = lax.dynamic_slice_in_dim(
        normed_full, lax.axis_index("heads") * feature_width, feature_width, 1
    )
    gate_part = jnp.dot(column_block, gate_weight, preferred_element_type=F32)
    up_part = jnp.dot(column_block, up_weight, preferred_element_type=F32)
    gate_rows, up_rows = (
        lax.psum(gate_part.astype(BF), "heads").astype(F32),
        lax.psum(up_part.astype(BF), "heads").astype(F32),
    )
    hidden = (jax.nn.gelu(gate_rows, approximate=True) * up_rows).astype(BF)
    down_out = lax.psum_scatter(
        jnp.dot(hidden, down_weight, preferred_element_type=F32),
        ("blk", "rows"),
        scatter_dimension=0,
        tiled=True,
    )
    own_start = (lax.axis_index("blk") * lax.axis_size("rows") + lax.axis_index("rows")) * tok_dev
    keep_own = lax.dynamic_slice_in_dim(keep_mask, own_start, tok_dev, 0)
    return (stream, (down_out * keep_own).astype(BF))


VM = pl.BlockSpec(memory_space=pltpu.VMEM)
SM = pl.BlockSpec(memory_space=pltpu.SMEM)
ANY = pl.BlockSpec(memory_space=pl.ANY)
MIB = 1 << 20


def hop(value, axis, size, step):
    return lax.ppermute(value, axis, [(i, i ^ step) for i in range(size)])


def by_index(pieces, at):
    return [lax.select_n(at ^ k, *pieces) for k in range(len(pieces))]


def kernel(body, name, outs, specs, args, limit=8, flops=0):
    size = sum(a.size * a.dtype.itemsize for a in list(args) + list(outs))
    return pl.pallas_call(
        body,
        out_shape=outs,
        in_specs=specs,
        out_specs=[VM] * len(outs),
        compiler_params=pltpu.CompilerParams(vmem_limit_bytes=limit * MIB),
        cost_estimate=pl.CostEstimate(flops=flops, bytes_accessed=size, transcendentals=0),
        name=name,
    )(*args)


def fetch(after, arrays, name):
    n = len(arrays)

    def body(*refs):
        sources, targets, sems = refs[1 : 1 + n], refs[1 + n : 1 + 2 * n], refs[1 + 2 * n]
        copies = [
            pltpu.make_async_copy(sources[i], targets[i], sems.at[i]) for i in range(n)
        ]
        for copy in copies:
            copy.start()
        for copy in copies:
            copy.wait()

    size = sum(a.size * a.dtype.itemsize for a in arrays)
    return pl.pallas_call(
        body,
        out_shape=[jax.ShapeDtypeStruct(a.shape, a.dtype) for a in arrays],
        in_specs=[ANY] * (1 + n),
        out_specs=[VM] * n,
        scratch_shapes=[pltpu.SemaphoreType.DMA((n,))],
        compiler_params=pltpu.CompilerParams(vmem_limit_bytes=MIB),
        cost_estimate=pl.CostEstimate(flops=0, bytes_accessed=2 * size, transcendentals=0),
        name=name,
    )(after, *[pltpu.with_memory_space_constraint(a, pltpu.HBM) for a in arrays])


def parts_of(value, count):
    out = []
    for _ in range(count):
        part = lax.reduce_precision(value, 8, 7)
        out.append(part.astype(BF))
        value = value - part
    return out


def split_in(value, count):
    out = []
    for _ in range(count):
        part = value.astype(BF)
        out.append(part)
        value = value - part.astype(F32)
    return out


def shards_direct(
    queries,
    src_keys,
    src_values,
    dec_state,
    mask_embed,
    out_weight,
    norm_gain,
    gate_weight,
    up_weight,
    down_weight,
    cand_lengths,
    masked_pos,
):
    blks, head_parts = lax.axis_size("blk"), lax.axis_size("heads")
    blk, head, row = (lax.axis_index(name) for name in ("blk", "heads", "rows"))
    tok_dev, local_heads, head_size = queries.shape
    kv_local = src_keys.shape[1]
    group_size = local_heads // kv_local
    score_scale = head_size ** (-0.5)
    width = dec_state.shape[1]
    features = width * blks * 2
    half = blks // head_parts
    hidden_width, out_width = gate_weight.shape[1], down_weight.shape[1]
    toks = tok_dev * blks
    tokens = toks * 2
    place = jnp.stack([row, blk, head]).astype(jnp.int32)
    sds = jax.ShapeDtypeStruct

    pieces = [queries] + [hop(queries, "blk", blks, s) for s in range(1, blks)]
    q_all = jnp.concatenate(by_index(pieces, blk), axis=0)
    grouped = q_all.reshape(toks, kv_local, group_size, head_size)
    scores = (
        jnp.einsum("tgjd,kgd->tgjk", grouped, src_keys, preferred_element_type=F32) * score_scale
    )
    peak = jnp.max(scores, axis=3)
    weights = jnp.exp(scores - peak[..., None])
    totals = jnp.sum(weights, axis=3)
    numerator = jnp.einsum(
        "tgjk,kgd->tgjd", weights.astype(BF), src_values, preferred_element_type=F32
    )
    partial = (numerator / totals[..., None]).astype(BF)
    partial = partial.transpose(1, 2, 0, 3).reshape(local_heads * toks, head_size)
    partial, peak, totals = lax.optimization_barrier((partial, peak, totals))
    level = (peak + jnp.log(totals)).reshape(toks, local_heads)
    side = jnp.concatenate(parts_of(level, 3), axis=1)
    side = jnp.pad(side, ((0, 0), (0, head_size - side.shape[1])))
    note = jnp.concatenate([partial, side], axis=0)
    notes = [note] + [hop(note, "blk", blks, s) for s in range(1, blks)]
    (proj_near,) = fetch(note, [out_weight.T], "fetch_proj")

    def combine(*refs):
        ins, out = refs[:blks], refs[-1]
        base = local_heads * toks
        levels = []
        for ref in ins:
            side = ref[base : base + toks, :].astype(F32)
            levels.append(
                side[:, :local_heads]
                + side[:, local_heads : 2 * local_heads]
                + side[:, 2 * local_heads : 3 * local_heads]
            )
        top = levels[0]
        for one in levels[1:]:
            top = jnp.maximum(top, one)
        shares = [jnp.exp(one - top) for one in levels]
        total = shares[0]
        for one in shares[1:]:
            total = total + one
        shares = [one / total for one in shares]
        for h in range(local_heads):
            acc = None
            for share, ref in zip(shares, ins):
                term = share[:, h : h + 1] * ref[h * toks : (h + 1) * toks, :].astype(F32)
                acc = term if acc is None else acc + term
            out[:, h * head_size : (h + 1) * head_size] = acc.astype(BF)

    (attn,) = kernel(
        combine,
        "combine",
        [sds((toks, local_heads * head_size), BF)],
        [VM] * blks + [ANY],
        notes + [proj_near],
    )
    other = hop(attn, "rows", 2, 1)
    across = (((1,), (1,)), ((), ()))

    def project_own(own_ref, weight_ref, out_ref):
        out_ref[...] = lax.dot_general(
            own_ref[...], weight_ref[...], across, preferred_element_type=F32
        )

    (proj_own,) = kernel(
        project_own,
        "project_own",
        [sds((toks, width), F32)],
        [VM, VM],
        [attn, proj_near],
        flops=2 * toks * width * attn.shape[1],
    )

    def project(place_ref, own_ref, other_ref, weight_ref, out_ref):
        first = place_ref[0] == 0
        own = own_ref[...]
        other = lax.dot_general(
            other_ref[...], weight_ref[...], across, preferred_element_type=F32
        )
        out_ref[:toks] = jnp.where(first, own, other).astype(BF)
        out_ref[toks:] = jnp.where(first, other, own).astype(BF)

    (proj,) = kernel(
        project,
        "project",
        [sds((tokens, width), BF)],
        [SM, VM, VM, VM],
        [place, proj_own, other, proj_near],
    )
    proj_other = hop(proj, "heads", 2, 1)
    (gate_near,) = fetch(proj, [gate_weight], "fetch_gate")

    def inner(value):
        value = value.reshape((blks, 2, tok_dev) + value.shape[1:])
        return jnp.swapaxes(value, 0, 1).reshape((tokens,) + value.shape[3:])

    valid_tok, masked_tok = token_masks(cand_lengths, masked_pos, tokens)
    base_state = inner(jnp.where(masked_tok[:, None], mask_embed[None, :], dec_state))
    keep_mask = valid_tok.astype(F32)
    keep_inner = inner(keep_mask)[:, None]
    lanes = -(-(width + 2) // 128) * 128

    def middle(base_ref, keep_ref, gain_ref, own_ref, other_ref, near_ref, stream_ref, note_ref):
        mid = base_ref[...].astype(F32) + (own_ref[...].astype(F32) + other_ref[...].astype(F32))
        stream_ref[...] = (mid * keep_ref[...]).astype(BF)
        note_ref[:, :width] = (mid * gain_ref[...].astype(F32)).astype(BF)
        squares = jnp.sum(mid * mid, axis=1, keepdims=True)
        high, low = split_in(squares, 2)
        lane = lax.broadcasted_iota(jnp.int32, (tokens, lanes - width), 1)
        note_ref[:, width:] = jnp.where(
            lane == 0, high.astype(F32), jnp.where(lane == 1, low.astype(F32), 0.0)
        ).astype(BF)

    stream, note = kernel(
        middle,
        "middle",
        [sds((tokens, width), BF), sds((tokens, lanes), BF)],
        [VM] * 5 + [ANY],
        [base_state, keep_inner, norm_gain[None, :], proj, proj_other, gate_near],
    )

    far_pairs, near_pairs = [], []
    for b in range(blks):
        for h in range(head_parts):
            far_pairs.append((b * head_parts + h, (b ^ 3) * head_parts + h))
            to = (b ^ 1, h) if b // half == h else (b ^ 2, 1 - h)
            near_pairs.append((b * head_parts + h, to[0] * head_parts + to[1]))
    far = lax.ppermute(note, ("blk", "heads"), far_pairs)
    near = lax.ppermute(note, ("blk", "heads"), near_pairs)
    (up_near,) = fetch(note, [up_weight], "fetch_up")
    lanes_all = note.shape[1]

    def pick(place_ref, own_ref, near_ref, far_ref, gate_ref, up_ref, out_ref):
        at = place_ref[1]
        inside = at // half == place_ref[2]
        odd = at % 2 == 1
        own, near_tile, far_tile = own_ref[...], near_ref[...], far_ref[...]
        same = jnp.where(inside, own, near_tile)
        pair = jnp.where(inside, near_tile, far_tile)
        out_ref[0] = jnp.where(odd, pair, same)
        out_ref[1] = jnp.where(odd, same, pair)

    (mine,) = kernel(
        pick,
        "pick",
        [sds((half, tokens, lanes_all), BF)],
        [SM, VM, VM, VM, ANY, ANY],
        [place, note, near, far, gate_near, up_near],
    )
    theirs = hop(mine, "rows", 2, 1)
    rows_in = gate_weight.shape[0]

    def tile_products(tiles_ref, weight_ref, row_at):
        total = None
        for k in range(half):
            start = pl.multiple_of((k * 2 + row_at) * width, 16)
            term = jnp.dot(
                tiles_ref[k, :, :width],
                weight_ref[pl.ds(start, width), :],
                preferred_element_type=F32,
            )
            total = term if total is None else total + term
        return total

    def inner_products(place_ref, mine_ref, gate_ref, up_ref, gate_out, up_out):
        gate_out[...] = tile_products(mine_ref, gate_ref, place_ref[0])
        up_out[...] = tile_products(mine_ref, up_ref, place_ref[0])

    gate_own, up_own = kernel(
        inner_products,
        "inner_products",
        [sds((tokens, hidden_width), F32)] * 2,
        [SM, VM, VM, VM],
        [place, mine, gate_near, up_near],
        flops=2 * tokens * rows_in * hidden_width,
    )

    def gates(place_ref, mine_ref, theirs_ref, own_ref, weight_ref, out_ref, note_ref):
        squares = None
        for k in range(half):
            for ref in (mine_ref, theirs_ref):
                here = ref[k, :, width : width + 2].astype(F32)
                squares = here if squares is None else squares + here
        squares = squares[:, 0:1] + squares[:, 1:2]
        gate = own_ref[...] + tile_products(theirs_ref, weight_ref, 1 - place_ref[0])
        out_ref[:, :hidden_width] = gate
        note_ref[:, :hidden_width] = gate.astype(BF)
        high, low = split_in(squares, 2)
        lane = lax.broadcasted_iota(jnp.int32, (tokens, 128), 1)
        out_ref[:, hidden_width:] = jnp.where(lane == 0, squares, 0.0)
        note_ref[:, hidden_width:] = jnp.where(
            lane == 0, high.astype(F32), jnp.where(lane == 1, low.astype(F32), 0.0)
        ).astype(BF)

    long_width = hidden_width + 128
    gate, gate_note = kernel(
        gates,
        "gates",
        [sds((tokens, long_width), F32), sds((tokens, long_width), BF)],
        [SM, VM, VM, VM, VM],
        [place, mine, theirs, gate_own, gate_near],
    )
    gate_other = hop(gate_note, "heads", 2, 1)

    def ups(place_ref, theirs_ref, own_ref, weight_ref, out_ref, note_ref):
        up = own_ref[...] + tile_products(theirs_ref, weight_ref, 1 - place_ref[0])
        out_ref[...] = up
        note_ref[...] = up.astype(BF)

    up, up_note = kernel(
        ups,
        "ups",
        [sds((tokens, hidden_width), F32), sds((tokens, hidden_width), BF)],
        [SM, VM, VM, VM],
        [place, theirs, up_own, up_near],
        flops=tokens * rows_in * hidden_width,
    )
    up_other = hop(up_note, "heads", 2, 1)
    (down_near,) = fetch(up_note, [down_weight], "fetch_down")

    def downs(
        place_ref, gate_ref, gate_other_ref, up_ref, up_other_ref, weight_ref, keep_ref, away_ref
    ):
        other = gate_other_ref[:, hidden_width:].astype(F32)
        squares = gate_ref[:, hidden_width : hidden_width + 1] + other[:, 0:1] + other[:, 1:2]
        inv_rms = lax.rsqrt(squares / features + EPS)
        gate = (gate_ref[:, :hidden_width] + gate_other_ref[:, :hidden_width].astype(F32)) * inv_rms
        up = (up_ref[...] + up_other_ref[...].astype(F32)) * inv_rms
        hidden = (jax.nn.gelu(gate, approximate=True) * up).astype(BF)
        down = jnp.dot(hidden, weight_ref[...], preferred_element_type=F32)
        first = place_ref[0] == 0
        keep_ref[...] = jnp.where(first, down[:toks], down[toks:])
        away_ref[...] = jnp.where(first, down[toks:], down[:toks]).astype(BF)

    keep, away = kernel(
        downs,
        "downs",
        [sds((toks, out_width), F32), sds((toks, out_width), BF)],
        [SM] + [VM] * 5,
        [place, gate, gate_other, up, up_other, down_near],
        limit=12,
    )
    back = hop(away, "rows", 2, 1)

    def owners(place_ref, keep_ref, back_ref, own_ref, *piece_refs):
        total = keep_ref[...] + back_ref[...].astype(F32)
        blocks = [total[k * tok_dev : (k + 1) * tok_dev] for k in range(blks)]
        at = place_ref[1]
        for s, ref in enumerate((own_ref,) + piece_refs):
            value = blocks[0]
            for k in range(1, blks):
                value = jnp.where(at == (k ^ s), blocks[k], value)
            ref[...] = value.astype(ref.dtype)

    own, *sends = kernel(
        owners,
        "owners",
        [sds((tok_dev, out_width), F32)] + [sds((tok_dev, out_width), BF)] * (blks - 1),
        [SM, VM, VM],
        [place, keep, back],
    )
    for s in range(1, blks):
        own = own + hop(sends[s - 1], "blk", blks, s).astype(F32)
    keep_own = lax.dynamic_slice_in_dim(keep_mask, (blk * 2 + row) * tok_dev, tok_dev, 0)
    branch = (own * keep_own[:, None]).astype(BF)
    stream = stream.reshape(2, blks, tok_dev, width).swapaxes(0, 1).reshape(tokens, width)
    return (stream, branch)


def solution(mesh):
    size = dict(mesh.shape)
    direct = size["blk"] == 4 and size["heads"] == 2 and size["rows"] == 2
    placed = (
        P(("groups", "blk", "rows"), "heads", None),
        P(("groups", "blk"), "heads", None),
        P(("groups", "blk"), "heads", None),
        P("groups", ("blk", "rows")),
        P(("blk", "rows")),
        P("heads", ("blk", "rows")),
        P(("blk", "rows")),
        P("heads", ("blk", "rows")),
        P("heads", ("blk", "rows")),
        P(("blk", "rows"), "heads"),
        P("groups"),
        P("groups", None),
    )
    return jax.shard_map(
        shards_direct if direct else shards_any,
        mesh=mesh,
        in_specs=placed,
        out_specs=(P("groups", ("blk", "rows")), P(("groups", "blk", "rows"), "heads")),
        check_vma=False,
    )
```

```python
import jax
import jax.numpy as jnp
from jax import lax
from jax.experimental import pallas as pl
from jax.experimental.pallas import tpu as pltpu
from jax.sharding import PartitionSpec as P

LEN = 128
EPS = 1e-06
BF = jnp.bfloat16
F32 = jnp.float32


def token_masks(cand_lengths, masked_pos, tokens):
    positions = jnp.arange(tokens, dtype=jnp.int32) % LEN
    length_tok = jnp.repeat(cand_lengths, LEN)[:tokens]
    valid_tok = positions < length_tok
    slots = jnp.arange(LEN, dtype=jnp.int32)
    masked_tok = jnp.any(masked_pos[:, :, None] == slots[None, None, :], axis=1).reshape(-1)[
        :tokens
    ]
    return (valid_tok, masked_tok)


def shards_any(
    queries,
    src_keys,
    src_values,
    dec_state,
    mask_embed,
    out_weight,
    norm_gain,
    gate_weight,
    up_weight,
    down_weight,
    cand_lengths,
    masked_pos,
):
    tok_dev, local_heads, head_size = queries.shape
    kv_local = src_keys.shape[1]
    group_size = local_heads // kv_local
    score_scale = head_size ** (-0.5)
    features = dec_state.shape[1] * lax.axis_size("blk") * lax.axis_size("rows")
    queries_all = lax.all_gather(queries, "blk", axis=0, tiled=True)
    gathered_rows = queries_all.shape[0]
    grouped = queries_all.reshape(gathered_rows, kv_local, group_size, head_size)
    scores = (
        jnp.einsum("tgjd,kgd->tgjk", grouped, src_keys, preferred_element_type=F32) * score_scale
    )
    local_peak = jnp.max(scores, axis=3)
    weights = jnp.exp(scores - local_peak[..., None])
    totals = jnp.sum(weights, axis=3)
    numerator = jnp.einsum(
        "tgjk,kgd->tgjd", weights.astype(BF), src_values, preferred_element_type=F32
    )
    highest = lax.pmax(local_peak, "blk")
    factor = jnp.exp(local_peak - highest)
    numer_own, totals_own = (
        lax.psum_scatter(
            (numerator * factor[..., None]).astype(BF), "blk", scatter_dimension=0, tiled=True
        ).astype(F32),
        lax.psum_scatter(
            (totals * factor).astype(BF), "blk", scatter_dimension=0, tiled=True
        ).astype(F32),
    )
    attn_own = (
        (numer_own / totals_own[..., None]).astype(BF).reshape(tok_dev, local_heads * head_size)
    )
    attn_all = lax.all_gather(attn_own, ("blk", "rows"), axis=0, tiled=True)
    tokens = attn_all.shape[0]
    projected = lax.psum(
        jnp.dot(attn_all, out_weight, preferred_element_type=F32).astype(BF), "heads"
    ).astype(F32)
    valid_tok, masked_tok = token_masks(cand_lengths, masked_pos, tokens)
    base_state = jnp.where(masked_tok[:, None], mask_embed[None, :], dec_state).astype(F32)
    stream_mid = base_state + projected
    squares = lax.psum(jnp.sum(stream_mid * stream_mid, axis=1), ("blk", "rows"))
    inv_rms = lax.rsqrt(squares / features + EPS)[:, None]
    normed = (stream_mid * inv_rms * norm_gain.astype(F32)).astype(BF)
    keep_mask = valid_tok.astype(F32)[:, None]
    stream = (stream_mid * keep_mask).astype(BF)
    normed_full = lax.all_gather(normed, ("blk", "rows"), axis=1, tiled=True)
    feature_width = gate_weight.shape[0]
    column_block = lax.dynamic_slice_in_dim(
        normed_full, lax.axis_index("heads") * feature_width, feature_width, 1
    )
    gate_part = jnp.dot(column_block, gate_weight, preferred_element_type=F32)
    up_part = jnp.dot(column_block, up_weight, preferred_element_type=F32)
    gate_rows, up_rows = (
        lax.psum(gate_part.astype(BF), "heads").astype(F32),
        lax.psum(up_part.astype(BF), "heads").astype(F32),
    )
    hidden = (jax.nn.gelu(gate_rows, approximate=True) * up_rows).astype(BF)
    down_out = lax.psum_scatter(
        jnp.dot(hidden, down_weight, preferred_element_type=F32),
        ("blk", "rows"),
        scatter_dimension=0,
        tiled=True,
    )
    own_start = (lax.axis_index("blk") * lax.axis_size("rows") + lax.axis_index("rows")) * tok_dev
    keep_own = lax.dynamic_slice_in_dim(keep_mask, own_start, tok_dev, 0)
    return (stream, (down_out * keep_own).astype(BF))


VM = pl.BlockSpec(memory_space=pltpu.VMEM)
ANY = pl.BlockSpec(memory_space=pl.ANY)
MIB = 1 << 20


def hop(value, axis, size, step):
    return lax.ppermute(value, axis, [(i, i ^ step) for i in range(size)])


def by_index(pieces, at):
    return [lax.select_n(at ^ k, *pieces) for k in range(len(pieces))]


def kernel(body, name, outs, specs, args, limit=8, flops=0, aliases=None):
    near = [a for a, spec in zip(args, specs) if spec is VM]
    size = sum(a.size * a.dtype.itemsize for a in near + list(outs))
    return pl.pallas_call(
        body,
        out_shape=outs,
        in_specs=specs,
        out_specs=[VM] * len(outs),
        input_output_aliases=aliases or {},
        compiler_params=pltpu.CompilerParams(vmem_limit_bytes=limit * MIB),
        cost_estimate=pl.CostEstimate(flops=flops, bytes_accessed=size, transcendentals=0),
        name=name,
    )(*args)


def fetch(after, arrays, name):
    n, skip = len(arrays), len(after)

    def body(*refs):
        refs = refs[skip:]
        sources, targets, sems = refs[:n], refs[n : 2 * n], refs[2 * n]
        copies = [
            pltpu.make_async_copy(sources[i], targets[i], sems.at[i]) for i in range(n)
        ]
        for copy in copies:
            copy.start()
        for copy in copies:
            copy.wait()

    size = sum(a.size * a.dtype.itemsize for a in arrays)
    return pl.pallas_call(
        body,
        out_shape=[jax.ShapeDtypeStruct(a.shape, a.dtype) for a in arrays],
        in_specs=[ANY] * (skip + n),
        out_specs=[VM] * n,
        scratch_shapes=[pltpu.SemaphoreType.DMA((n,))],
        compiler_params=pltpu.CompilerParams(vmem_limit_bytes=MIB),
        cost_estimate=pl.CostEstimate(flops=0, bytes_accessed=2 * size, transcendentals=0),
        name=name,
    )(*after, *[pltpu.with_memory_space_constraint(a, pltpu.HBM) for a in arrays])


def parts_of(value, count):
    out = []
    for _ in range(count):
        part = lax.reduce_precision(value, 8, 7)
        out.append(part.astype(BF))
        value = value - part
    return out


def split_in(value, count):
    out = []
    for _ in range(count):
        part = value.astype(BF)
        out.append(part)
        value = value - part.astype(F32)
    return out


def shards_direct(
    queries,
    src_keys,
    src_values,
    dec_state,
    mask_embed,
    out_weight,
    norm_gain,
    gate_weight,
    up_weight,
    down_weight,
    cand_lengths,
    masked_pos,
):
    blks, head_parts = lax.axis_size("blk"), lax.axis_size("heads")
    blk, head, row = (lax.axis_index(name) for name in ("blk", "heads", "rows"))
    tok_dev, local_heads, head_size = queries.shape
    kv_local = src_keys.shape[1]
    group_size = local_heads // kv_local
    score_scale = head_size ** (-0.5)
    width = dec_state.shape[1]
    features = width * blks * 2
    half = blks // head_parts
    hidden_width, out_width = gate_weight.shape[1], down_weight.shape[1]
    toks = tok_dev * blks
    tokens = toks * 2
    sds = jax.ShapeDtypeStruct

    def inner(value):
        value = value.reshape((blks, 2, tok_dev) + value.shape[1:])
        return jnp.swapaxes(value, 0, 1).reshape((tokens,) + value.shape[3:])

    valid_tok, masked_tok = token_masks(cand_lengths, masked_pos, tokens)
    base_state = inner(jnp.where(masked_tok[:, None], mask_embed[None, :], dec_state))
    keep_mask = valid_tok.astype(F32)
    keep_inner = inner(keep_mask)[:, None]
    own_start = (blk * 2 + row) * tok_dev
    keep_own = lax.dynamic_slice_in_dim(keep_mask, own_start, tok_dev, 0)[:, None]
    gain = norm_gain[None, :]

    (queries_near,) = fetch([], [queries], "fetch_queries")
    pieces = [queries_near] + [hop(queries, "blk", blks, s) for s in range(1, blks)]
    q_all = jnp.concatenate(by_index(pieces, blk), axis=0)
    q_all, base_state, keep_inner, keep_own, gain = lax.optimization_barrier(
        (q_all, base_state, keep_inner, keep_own, gain)
    )
    grouped = q_all.reshape(toks, kv_local, group_size, head_size)
    scores = (
        jnp.einsum("tgjd,kgd->tgjk", grouped, src_keys, preferred_element_type=F32) * score_scale
    )
    peak = jnp.max(scores, axis=3)
    weights = jnp.exp(scores - peak[..., None])
    totals = jnp.sum(weights, axis=3)
    numerator = jnp.einsum(
        "tgjk,kgd->tgjd", weights.astype(BF), src_values, preferred_element_type=F32
    )
    partial = (numerator / totals[..., None]).astype(BF)
    partial = partial.transpose(1, 2, 0, 3).reshape(local_heads * toks, head_size)
    partial, peak, totals = lax.optimization_barrier((partial, peak, totals))
    level = (peak + jnp.log(totals)).reshape(toks, local_heads)
    side = jnp.concatenate(parts_of(level, 3), axis=1)
    side = jnp.pad(side, ((0, 0), (0, head_size - side.shape[1])))
    note = jnp.concatenate([partial, side], axis=0)
    notes = [note] + [hop(note, "blk", blks, s) for s in range(1, blks)]
    (proj_near,) = fetch([note], [out_weight.T], "fetch_proj")

    def combine(*refs):
        ins, out = refs[:blks], refs[-2]
        base = local_heads * toks
        levels = []
        for ref in ins:
            side = ref[base : base + toks, :].astype(F32)
            levels.append(
                side[:, :local_heads]
                + side[:, local_heads : 2 * local_heads]
                + side[:, 2 * local_heads : 3 * local_heads]
            )
        top = levels[0]
        for one in levels[1:]:
            top = jnp.maximum(top, one)
        shares = [jnp.exp(one - top) for one in levels]
        total = shares[0]
        for one in shares[1:]:
            total = total + one
        shares = [one / total for one in shares]
        for h in range(local_heads):
            acc = None
            for share, ref in zip(shares, ins):
                term = share[:, h : h + 1] * ref[h * toks : (h + 1) * toks, :].astype(F32)
                acc = term if acc is None else acc + term
            out[:, h * head_size : (h + 1) * head_size] = acc.astype(BF)

    attn, proj_near = kernel(
        combine,
        "combine",
        [sds((toks, local_heads * head_size), BF), sds(proj_near.shape, BF)],
        [VM] * (blks + 1),
        notes + [proj_near],
        aliases={blks: 1},
    )
    other = hop(attn, "rows", 2, 1)
    across = (((1,), (1,)), ((), ()))

    def project_own(own_ref, weight_ref, out_ref):
        out_ref[...] = lax.dot_general(
            own_ref[...], weight_ref[...], across, preferred_element_type=F32
        )

    (proj_own,) = kernel(
        project_own,
        "project_own",
        [sds((toks, width), F32)],
        [VM, VM],
        [attn, proj_near],
        flops=2 * toks * width * attn.shape[1],
    )

    def project(own_ref, other_ref, weight_ref, out_ref):
        first = lax.axis_index("rows") == 0
        own = own_ref[...]
        other = lax.dot_general(
            other_ref[...], weight_ref[...], across, preferred_element_type=F32
        )
        out_ref[:toks] = jnp.where(first, own, other).astype(BF)
        out_ref[toks:] = jnp.where(first, other, own).astype(BF)

    (proj,) = kernel(
        project,
        "project",
        [sds((tokens, width), BF)],
        [VM, VM, VM],
        [proj_own, other, proj_near],
    )
    proj_other = hop(proj, "heads", 2, 1)
    (gate_near,) = fetch([proj], [gate_weight], "fetch_gate")

    lanes = -(-(width + 2) // 128) * 128

    def middle(base_ref, keep_ref, gain_ref, own_ref, other_ref, near_ref, stream_ref, note_ref):
        mid = base_ref[...].astype(F32) + (own_ref[...].astype(F32) + other_ref[...].astype(F32))
        stream_ref[...] = (mid * keep_ref[...]).astype(BF)
        note_ref[:, :width] = (mid * gain_ref[...].astype(F32)).astype(BF)
        squares = jnp.sum(mid * mid, axis=1, keepdims=True)
        high, low = split_in(squares, 2)
        lane = lax.broadcasted_iota(jnp.int32, (tokens, lanes - width), 1)
        note_ref[:, width:] = jnp.where(
            lane == 0, high.astype(F32), jnp.where(lane == 1, low.astype(F32), 0.0)
        ).astype(BF)

    stream, note = kernel(
        middle,
        "middle",
        [sds((tokens, width), BF), sds((tokens, lanes), BF)],
        [VM] * 5 + [ANY],
        [base_state, keep_inner, gain, proj, proj_other, gate_near],
    )

    far_pairs, near_pairs = [], []
    for b in range(blks):
        for h in range(head_parts):
            far_pairs.append((b * head_parts + h, (b ^ 3) * head_parts + h))
            to = (b ^ 1, h) if b // half == h else (b ^ 2, 1 - h)
            near_pairs.append((b * head_parts + h, to[0] * head_parts + to[1]))
    far = lax.ppermute(note, ("blk", "heads"), far_pairs)
    near = lax.ppermute(note, ("blk", "heads"), near_pairs)
    (up_near,) = fetch([note], [up_weight], "fetch_up")
    lanes_all = note.shape[1]

    def pick(own_ref, near_ref, far_ref, gate_ref, up_ref, out_ref):
        at = lax.axis_index("blk")
        inside = at // half == lax.axis_index("heads")
        odd = at % 2 == 1
        own, near_tile, far_tile = own_ref[...], near_ref[...], far_ref[...]
        same = jnp.where(inside, own, near_tile)
        pair = jnp.where(inside, near_tile, far_tile)
        out_ref[0] = jnp.where(odd, pair, same)
        out_ref[1] = jnp.where(odd, same, pair)

    (mine,) = kernel(
        pick,
        "pick",
        [sds((half, tokens, lanes_all), BF)],
        [VM, VM, VM, ANY, ANY],
        [note, near, far, gate_near, up_near],
    )
    theirs = hop(mine, "rows", 2, 1)
    rows_in = gate_weight.shape[0]

    def tile_products(tiles_ref, weight_ref, row_at):
        total = None
        for k in range(half):
            start = pl.multiple_of((k * 2 + row_at) * width, 16)
            term = jnp.dot(
                tiles_ref[k, :, :width],
                weight_ref[pl.ds(start, width), :],
                preferred_element_type=F32,
            )
            total = term if total is None else total + term
        return total

    def inner_products(mine_ref, gate_ref, up_ref, gate_out, up_out):
        gate_out[...] = tile_products(mine_ref, gate_ref, lax.axis_index("rows"))
        up_out[...] = tile_products(mine_ref, up_ref, lax.axis_index("rows"))

    gate_own, up_own = kernel(
        inner_products,
        "inner_products",
        [sds((tokens, hidden_width), F32)] * 2,
        [VM, VM, VM],
        [mine, gate_near, up_near],
        flops=2 * tokens * rows_in * hidden_width,
    )

    cut = -(-hidden_width // 512) * 256
    pieces_at = [(0, cut), (cut, hidden_width)]

    def gate_up(lo, hi, with_squares):
        span = hi - lo

        def body(*refs):
            theirs_ref, gate_in, up_in, gate_w, up_w = refs[:5]
            out_ref, note_ref = refs[-2:]
            row_at = 1 - lax.axis_index("rows")
            for k, (own, weight) in enumerate(((gate_in, gate_w), (up_in, up_w))):
                value = own[:, lo:hi] + tile_products(theirs_ref, weight.at[:, lo:hi], row_at)
                out_ref[:, k * span : (k + 1) * span] = value
                note_ref[:, k * span : (k + 1) * span] = value.astype(BF)
            if with_squares:
                squares = None
                for k in range(half):
                    for ref in (refs[5], theirs_ref):
                        here = ref[k, :, width : width + 2].astype(F32)
                        squares = here if squares is None else squares + here
                squares = squares[:, 0:1] + squares[:, 1:2]
                high, low = split_in(squares, 2)
                lane = lax.broadcasted_iota(jnp.int32, (tokens, 128), 1)
                out_ref[:, 2 * span :] = jnp.where(lane == 0, squares, 0.0)
                note_ref[:, 2 * span :] = jnp.where(
                    lane == 0, high.astype(F32), jnp.where(lane == 1, low.astype(F32), 0.0)
                ).astype(BF)

        return body

    sums, sum_notes = [], []
    for c, (lo, hi) in enumerate(pieces_at):
        operands = [theirs, gate_own, up_own, gate_near, up_near] + [mine] * (c == 0)
        long_width = 2 * (hi - lo) + 128 * (c == 0)
        value, value_note = kernel(
            gate_up(lo, hi, c == 0),
            f"gate_up_{c}",
            [sds((tokens, long_width), F32), sds((tokens, long_width), BF)],
            [VM] * len(operands),
            operands,
            flops=tokens * rows_in * hidden_width,
        )
        sums.append(value)
        sum_notes.append(value_note)
    sum_others = [hop(value, "heads", 2, 1) for value in sum_notes]
    (down_near,) = fetch([sum_notes[-1]], [down_weight], "fetch_down")

    def down_piece(c, own_ref, other_ref, first_ref, first_other_ref, weight_ref):
        lo, hi = pieces_at[c]
        span, at = hi - lo, 2 * cut
        other = first_other_ref[:, at:].astype(F32)
        squares = first_ref[:, at : at + 1] + other[:, 0:1] + other[:, 1:2]
        inv_rms = lax.rsqrt(squares / features + EPS)
        gate, up = [
            (
                own_ref[:, k * span : (k + 1) * span]
                + other_ref[:, k * span : (k + 1) * span].astype(F32)
            )
            * inv_rms
            for k in range(2)
        ]
        hidden = (jax.nn.gelu(gate, approximate=True) * up).astype(BF)
        return jnp.dot(hidden, weight_ref[lo:hi, :], preferred_element_type=F32)

    def down_first(own_ref, other_ref, weight_ref, out_ref):
        out_ref[...] = down_piece(0, own_ref, other_ref, own_ref, other_ref, weight_ref)

    (down_part,) = kernel(
        down_first,
        "down_first",
        [sds((tokens, out_width), F32)],
        [VM] * 3,
        [sums[0], sum_others[0], down_near],
        flops=tokens * hidden_width * out_width,
    )

    def down_last(
        own_ref, other_ref, first_ref, first_other_ref, part_ref, weight_ref, keep_ref, away_ref
    ):
        down = part_ref[...] + down_piece(
            1, own_ref, other_ref, first_ref, first_other_ref, weight_ref
        )
        first = lax.axis_index("rows") == 0
        keep_ref[...] = jnp.where(first, down[:toks], down[toks:])
        away_ref[...] = jnp.where(first, down[toks:], down[:toks]).astype(BF)

    keep, away = kernel(
        down_last,
        "down_last",
        [sds((toks, out_width), F32), sds((toks, out_width), BF)],
        [VM] * 6,
        [sums[1], sum_others[1], sums[0], sum_others[0], down_part, down_near],
        limit=12,
    )
    back = hop(away, "rows", 2, 1)

    def owners(keep_ref, back_ref, own_ref, *piece_refs):
        total = keep_ref[...] + back_ref[...].astype(F32)
        blocks = [total[k * tok_dev : (k + 1) * tok_dev] for k in range(blks)]
        at = lax.axis_index("blk")
        for s, ref in enumerate((own_ref,) + piece_refs):
            value = blocks[0]
            for k in range(1, blks):
                value = jnp.where(at == (k ^ s), blocks[k], value)
            ref[...] = value.astype(ref.dtype)

    own, *sends = kernel(
        owners,
        "owners",
        [sds((tok_dev, out_width), F32)] + [sds((tok_dev, out_width), BF)] * (blks - 1),
        [VM, VM],
        [keep, back],
    )
    for s in range(1, blks):
        own = own + hop(sends[s - 1], "blk", blks, s).astype(F32)
    branch = (own * keep_own).astype(BF)
    stream = stream.reshape(2, blks, tok_dev, width).swapaxes(0, 1).reshape(tokens, width)
    return (stream, branch)


def solution(mesh):
    size = dict(mesh.shape)
    direct = size["blk"] == 4 and size["heads"] == 2 and size["rows"] == 2
    placed = (
        P(("groups", "blk", "rows"), "heads", None),
        P(("groups", "blk"), "heads", None),
        P(("groups", "blk"), "heads", None),
        P("groups", ("blk", "rows")),
        P(("blk", "rows")),
        P("heads", ("blk", "rows")),
        P(("blk", "rows")),
        P("heads", ("blk", "rows")),
        P("heads", ("blk", "rows")),
        P(("blk", "rows"), "heads"),
        P("groups"),
        P("groups", None),
    )
    return jax.shard_map(
        shards_direct if direct else shards_any,
        mesh=mesh,
        in_specs=placed,
        out_specs=(P("groups", ("blk", "rows")), P(("groups", "blk", "rows"), "heads")),
        check_vma=False,
    )
```

```python
import jax
import jax.numpy as jnp
from jax import lax
from jax.experimental import pallas as pl
from jax.experimental.pallas import tpu as pltpu
from jax.sharding import PartitionSpec as P

LEN = 128
EPS = 1e-06
BF = jnp.bfloat16
F32 = jnp.float32


def token_masks(cand_lengths, masked_pos, tokens):
    positions = jnp.arange(tokens, dtype=jnp.int32) % LEN
    length_tok = jnp.repeat(cand_lengths, LEN)[:tokens]
    valid_tok = positions < length_tok
    slots = jnp.arange(LEN, dtype=jnp.int32)
    masked_tok = jnp.any(masked_pos[:, :, None] == slots[None, None, :], axis=1).reshape(-1)[
        :tokens
    ]
    return (valid_tok, masked_tok)


def shards_any(
    queries,
    src_keys,
    src_values,
    dec_state,
    mask_embed,
    out_weight,
    norm_gain,
    gate_weight,
    up_weight,
    down_weight,
    cand_lengths,
    masked_pos,
):
    tok_dev, local_heads, head_size = queries.shape
    kv_local = src_keys.shape[1]
    group_size = local_heads // kv_local
    score_scale = head_size ** (-0.5)
    features = dec_state.shape[1] * lax.axis_size("blk") * lax.axis_size("rows")
    queries_all = lax.all_gather(queries, "blk", axis=0, tiled=True)
    gathered_rows = queries_all.shape[0]
    grouped = queries_all.reshape(gathered_rows, kv_local, group_size, head_size)
    scores = (
        jnp.einsum("tgjd,kgd->tgjk", grouped, src_keys, preferred_element_type=F32) * score_scale
    )
    local_peak = jnp.max(scores, axis=3)
    weights = jnp.exp(scores - local_peak[..., None])
    totals = jnp.sum(weights, axis=3)
    numerator = jnp.einsum(
        "tgjk,kgd->tgjd", weights.astype(BF), src_values, preferred_element_type=F32
    )
    highest = lax.pmax(local_peak, "blk")
    factor = jnp.exp(local_peak - highest)
    numer_own, totals_own = (
        lax.psum_scatter(
            (numerator * factor[..., None]).astype(BF), "blk", scatter_dimension=0, tiled=True
        ).astype(F32),
        lax.psum_scatter(
            (totals * factor).astype(BF), "blk", scatter_dimension=0, tiled=True
        ).astype(F32),
    )
    attn_own = (
        (numer_own / totals_own[..., None]).astype(BF).reshape(tok_dev, local_heads * head_size)
    )
    attn_all = lax.all_gather(attn_own, ("blk", "rows"), axis=0, tiled=True)
    tokens = attn_all.shape[0]
    projected = lax.psum(
        jnp.dot(attn_all, out_weight, preferred_element_type=F32).astype(BF), "heads"
    ).astype(F32)
    valid_tok, masked_tok = token_masks(cand_lengths, masked_pos, tokens)
    base_state = jnp.where(masked_tok[:, None], mask_embed[None, :], dec_state).astype(F32)
    stream_mid = base_state + projected
    squares = lax.psum(jnp.sum(stream_mid * stream_mid, axis=1), ("blk", "rows"))
    inv_rms = lax.rsqrt(squares / features + EPS)[:, None]
    normed = (stream_mid * inv_rms * norm_gain.astype(F32)).astype(BF)
    keep_mask = valid_tok.astype(F32)[:, None]
    stream = (stream_mid * keep_mask).astype(BF)
    normed_full = lax.all_gather(normed, ("blk", "rows"), axis=1, tiled=True)
    feature_width = gate_weight.shape[0]
    column_block = lax.dynamic_slice_in_dim(
        normed_full, lax.axis_index("heads") * feature_width, feature_width, 1
    )
    gate_part = jnp.dot(column_block, gate_weight, preferred_element_type=F32)
    up_part = jnp.dot(column_block, up_weight, preferred_element_type=F32)
    gate_rows, up_rows = (
        lax.psum(gate_part.astype(BF), "heads").astype(F32),
        lax.psum(up_part.astype(BF), "heads").astype(F32),
    )
    hidden = (jax.nn.gelu(gate_rows, approximate=True) * up_rows).astype(BF)
    down_out = lax.psum_scatter(
        jnp.dot(hidden, down_weight, preferred_element_type=F32),
        ("blk", "rows"),
        scatter_dimension=0,
        tiled=True,
    )
    own_start = (lax.axis_index("blk") * lax.axis_size("rows") + lax.axis_index("rows")) * tok_dev
    keep_own = lax.dynamic_slice_in_dim(keep_mask, own_start, tok_dev, 0)
    return (stream, (down_out * keep_own).astype(BF))


VM = pl.BlockSpec(memory_space=pltpu.VMEM)
ANY = pl.BlockSpec(memory_space=pl.ANY)
MIB = 1 << 20


def hop(value, axis, size, step):
    return lax.ppermute(value, axis, [(i, i ^ step) for i in range(size)])


def kernel(body, name, outs, specs, args, limit=8, flops=0, aliases=None):
    near = [a for a, spec in zip(args, specs) if spec is VM]
    size = sum(a.size * a.dtype.itemsize for a in near + list(outs))
    return pl.pallas_call(
        body,
        out_shape=outs,
        in_specs=specs,
        out_specs=[VM] * len(outs),
        input_output_aliases=aliases or {},
        compiler_params=pltpu.CompilerParams(vmem_limit_bytes=limit * MIB),
        cost_estimate=pl.CostEstimate(flops=flops, bytes_accessed=size, transcendentals=0),
        name=name,
    )(*args)


def fetch(after, arrays, name):
    n, skip = len(arrays), len(after)

    def body(*refs):
        refs = refs[skip:]
        sources, targets, sems = refs[:n], refs[n : 2 * n], refs[2 * n]
        copies = [
            pltpu.make_async_copy(sources[i], targets[i], sems.at[i]) for i in range(n)
        ]
        for copy in copies:
            copy.start()
        for copy in copies:
            copy.wait()

    size = sum(a.size * a.dtype.itemsize for a in arrays)
    return pl.pallas_call(
        body,
        out_shape=[jax.ShapeDtypeStruct(a.shape, a.dtype) for a in arrays],
        in_specs=[ANY] * (skip + n),
        out_specs=[VM] * n,
        scratch_shapes=[pltpu.SemaphoreType.DMA((n,))],
        compiler_params=pltpu.CompilerParams(vmem_limit_bytes=MIB),
        cost_estimate=pl.CostEstimate(flops=0, bytes_accessed=2 * size, transcendentals=0),
        name=name,
    )(*after, *[pltpu.with_memory_space_constraint(a, pltpu.HBM) for a in arrays])


def parts_of(value, count):
    out = []
    for _ in range(count):
        part = lax.reduce_precision(value, 8, 7)
        out.append(part.astype(BF))
        value = value - part
    return out


def split_in(value, count):
    out = []
    for _ in range(count):
        part = value.astype(BF)
        out.append(part)
        value = value - part.astype(F32)
    return out


def shards_direct(
    queries,
    src_keys,
    src_values,
    dec_state,
    mask_embed,
    out_weight,
    norm_gain,
    gate_weight,
    up_weight,
    down_weight,
    cand_lengths,
    masked_pos,
):
    blks, head_parts = lax.axis_size("blk"), lax.axis_size("heads")
    blk, head, row = (lax.axis_index(name) for name in ("blk", "heads", "rows"))
    tok_dev, local_heads, head_size = queries.shape
    kv_local = src_keys.shape[1]
    group_size = local_heads // kv_local
    score_scale = head_size ** (-0.5)
    width = dec_state.shape[1]
    features = width * blks * 2
    half = blks // head_parts
    hidden_width, out_width = gate_weight.shape[1], down_weight.shape[1]
    toks = tok_dev * blks
    tokens = toks * 2
    sds = jax.ShapeDtypeStruct

    def inner(value):
        value = value.reshape((blks, 2, tok_dev) + value.shape[1:])
        return jnp.swapaxes(value, 0, 1).reshape((tokens,) + value.shape[3:])

    valid_tok, masked_tok = token_masks(cand_lengths, masked_pos, tokens)
    base_state = inner(jnp.where(masked_tok[:, None], mask_embed[None, :], dec_state))
    keep_mask = valid_tok.astype(F32)
    keep_inner = inner(keep_mask)[:, None]
    own_start = (blk * 2 + row) * tok_dev
    keep_own = lax.dynamic_slice_in_dim(keep_mask, own_start, tok_dev, 0)[:, None]
    gain = norm_gain[None, :]

    (queries_near,) = fetch([], [queries], "fetch_queries")
    blocks = [queries_near] * blks
    for s in [1] + list(reversed(range(2, blks))):
        piece = hop(queries, "blk", blks, s)
        blocks = [jnp.where(blk == (k ^ s), piece, block) for k, block in enumerate(blocks)]
        blocks = list(lax.optimization_barrier(tuple(blocks)))
    q_all = jnp.concatenate(blocks, axis=0)
    q_all, base_state, keep_inner, keep_own, gain = lax.optimization_barrier(
        (q_all, base_state, keep_inner, keep_own, gain)
    )
    grouped = q_all.reshape(toks, kv_local, group_size, head_size)
    scores = (
        jnp.einsum("tgjd,kgd->tgjk", grouped, src_keys, preferred_element_type=F32) * score_scale
    )
    peak = jnp.max(scores, axis=3)
    weights = jnp.exp(scores - peak[..., None])
    totals = jnp.sum(weights, axis=3)
    numerator = jnp.einsum(
        "tgjk,kgd->tgjd", weights.astype(BF), src_values, preferred_element_type=F32
    )
    partial = (numerator / totals[..., None]).astype(BF)
    partial = partial.transpose(1, 2, 0, 3).reshape(local_heads * toks, head_size)
    partial, peak, totals = lax.optimization_barrier((partial, peak, totals))
    level = (peak + jnp.log(totals)).reshape(toks, local_heads)
    side = jnp.concatenate(parts_of(level, 3), axis=1)
    side = jnp.pad(side, ((0, 0), (0, head_size - side.shape[1])))
    note = jnp.concatenate([partial, side], axis=0)
    notes = [note] + [hop(note, "blk", blks, s) for s in range(1, blks)]
    (proj_near,) = fetch([note], [out_weight.T], "fetch_proj")

    def combine(*refs):
        ins, out = refs[:blks], refs[-2]
        base = local_heads * toks
        levels = []
        for ref in ins:
            side = ref[base : base + toks, :].astype(F32)
            levels.append(
                side[:, :local_heads]
                + side[:, local_heads : 2 * local_heads]
                + side[:, 2 * local_heads : 3 * local_heads]
            )
        top = levels[0]
        for one in levels[1:]:
            top = jnp.maximum(top, one)
        shares = [jnp.exp(one - top) for one in levels]
        total = shares[0]
        for one in shares[1:]:
            total = total + one
        shares = [one / total for one in shares]
        for h in range(local_heads):
            acc = None
            for share, ref in zip(shares, ins):
                term = share[:, h : h + 1] * ref[h * toks : (h + 1) * toks, :].astype(F32)
                acc = term if acc is None else acc + term
            out[:, h * head_size : (h + 1) * head_size] = acc.astype(BF)

    attn, proj_near = kernel(
        combine,
        "combine",
        [sds((toks, local_heads * head_size), BF), sds(proj_near.shape, BF)],
        [VM] * (blks + 1),
        notes + [proj_near],
        aliases={blks: 1},
    )
    other = hop(attn, "rows", 2, 1)
    across = (((1,), (1,)), ((), ()))

    gate_cut = gate_weight.shape[0] // 64 * 16

    def project_own(own_ref, weight_ref, gate_ref, out_ref, near_ref, sem):
        copy = pltpu.make_async_copy(
            gate_ref.at[pl.ds(0, gate_cut)], near_ref.at[pl.ds(0, gate_cut)], sem
        )
        copy.start()
        out_ref[...] = lax.dot_general(
            own_ref[...], weight_ref[...], across, preferred_element_type=F32
        )
        copy.wait()

    gate_far = pltpu.with_memory_space_constraint(gate_weight, pltpu.HBM)
    proj_own, gate_near = pl.pallas_call(
        project_own,
        out_shape=[sds((toks, width), F32), sds(gate_weight.shape, BF)],
        in_specs=[VM, VM, ANY],
        out_specs=[VM] * 2,
        scratch_shapes=[pltpu.SemaphoreType.DMA],
        compiler_params=pltpu.CompilerParams(vmem_limit_bytes=8 * MIB),
        cost_estimate=pl.CostEstimate(
            flops=2 * toks * width * attn.shape[1],
            bytes_accessed=2 * gate_cut * gate_weight.shape[1] * 2,
            transcendentals=0,
        ),
        name="project_own",
    )(attn, proj_near, gate_far)

    def project(own_ref, other_ref, weight_ref, out_ref):
        first = lax.axis_index("rows") == 0
        own = own_ref[...]
        other = lax.dot_general(
            other_ref[...], weight_ref[...], across, preferred_element_type=F32
        )
        out_ref[:toks] = jnp.where(first, own, other).astype(BF)
        out_ref[toks:] = jnp.where(first, other, own).astype(BF)

    (proj,) = kernel(
        project,
        "project",
        [sds((tokens, width), BF)],
        [VM, VM, VM],
        [proj_own, other, proj_near],
    )
    proj_other = hop(proj, "heads", 2, 1)

    def fetch_gate(proj_ref, gate_ref, part_ref, near_ref, sem):
        rest = pl.ds(gate_cut, gate_weight.shape[0] - gate_cut)
        copy = pltpu.make_async_copy(gate_ref.at[rest], near_ref.at[rest], sem)
        copy.start()
        copy.wait()

    gate_near = pl.pallas_call(
        fetch_gate,
        out_shape=sds(gate_weight.shape, BF),
        in_specs=[ANY, ANY, VM],
        out_specs=VM,
        input_output_aliases={2: 0},
        scratch_shapes=[pltpu.SemaphoreType.DMA],
        compiler_params=pltpu.CompilerParams(vmem_limit_bytes=MIB),
        cost_estimate=pl.CostEstimate(
            flops=0, bytes_accessed=2 * gate_weight.size * 2, transcendentals=0
        ),
        name="fetch_gate",
    )(proj, gate_far, gate_near)
    lanes = -(-(width + 2) // 128) * 128

    def middle(base_ref, keep_ref, gain_ref, own_ref, other_ref, near_ref, stream_ref, note_ref):
        mid = base_ref[...].astype(F32) + (own_ref[...].astype(F32) + other_ref[...].astype(F32))
        stream_ref[...] = (mid * keep_ref[...]).astype(BF)
        note_ref[:, :width] = (mid * gain_ref[...].astype(F32)).astype(BF)
        squares = jnp.sum(mid * mid, axis=1, keepdims=True)
        high, low = split_in(squares, 2)
        lane = lax.broadcasted_iota(jnp.int32, (tokens, lanes - width), 1)
        note_ref[:, width:] = jnp.where(
            lane == 0, high.astype(F32), jnp.where(lane == 1, low.astype(F32), 0.0)
        ).astype(BF)

    stream, note = kernel(
        middle,
        "middle",
        [sds((tokens, width), BF), sds((tokens, lanes), BF)],
        [VM] * 5 + [ANY],
        [base_state, keep_inner, gain, proj, proj_other, gate_near],
    )

    far_pairs, near_pairs = [], []
    for b in range(blks):
        for h in range(head_parts):
            far_pairs.append((b * head_parts + h, (b ^ 2) * head_parts + h))
            to = (b ^ 1, h) if b // half == h else (b ^ 3, 1 - h)
            near_pairs.append((b * head_parts + h, to[0] * head_parts + to[1]))
    near = lax.ppermute(note, ("blk", "heads"), near_pairs)
    far = lax.ppermute(note, ("blk", "heads"), far_pairs)
    (up_near,) = fetch([note], [up_weight], "fetch_up")
    lanes_all = note.shape[1]

    def pick(own_ref, near_ref, far_ref, gate_ref, up_ref, out_ref):
        at = lax.axis_index("blk")
        inside = at // half == lax.axis_index("heads")
        odd = at % 2 == 1
        same = jnp.where(inside, own_ref[...], far_ref[...])
        pair = near_ref[...]
        out_ref[0] = jnp.where(odd, pair, same)
        out_ref[1] = jnp.where(odd, same, pair)

    (mine,) = kernel(
        pick,
        "pick",
        [sds((half, tokens, lanes_all), BF)],
        [VM, VM, VM, ANY, ANY],
        [note, near, far, gate_near, up_near],
    )
    theirs = hop(mine, "rows", 2, 1)
    rows_in = gate_weight.shape[0]

    def tile_products(tiles_ref, weight_ref, row_at):
        total = None
        for k in range(half):
            start = pl.multiple_of((k * 2 + row_at) * width, 16)
            term = jnp.dot(
                tiles_ref[k, :, :width],
                weight_ref[pl.ds(start, width), :],
                preferred_element_type=F32,
            )
            total = term if total is None else total + term
        return total

    def inner_products(mine_ref, gate_ref, up_ref, gate_out, up_out):
        gate_out[...] = tile_products(mine_ref, gate_ref, lax.axis_index("rows"))
        up_out[...] = tile_products(mine_ref, up_ref, lax.axis_index("rows"))

    gate_own, up_own = kernel(
        inner_products,
        "inner_products",
        [sds((tokens, hidden_width), F32)] * 2,
        [VM, VM, VM],
        [mine, gate_near, up_near],
        flops=2 * tokens * rows_in * hidden_width,
    )

    cut = -(-hidden_width // 512) * 256
    pieces_at = [(0, cut), (cut, hidden_width)]

    def gate_up(lo, hi, with_squares):
        span = hi - lo

        def body(*refs):
            theirs_ref, gate_in, up_in, gate_w, up_w = refs[:5]
            out_ref, note_ref = refs[-2:]
            row_at = 1 - lax.axis_index("rows")
            for k, (own, weight) in enumerate(((gate_in, gate_w), (up_in, up_w))):
                value = own[:, lo:hi] + tile_products(theirs_ref, weight.at[:, lo:hi], row_at)
                out_ref[:, k * span : (k + 1) * span] = value
                note_ref[:, k * span : (k + 1) * span] = value.astype(BF)
            if with_squares:
                squares = None
                for k in range(half):
                    for ref in (refs[5], theirs_ref):
                        here = ref[k, :, width : width + 2].astype(F32)
                        squares = here if squares is None else squares + here
                squares = squares[:, 0:1] + squares[:, 1:2]
                high, low = split_in(squares, 2)
                lane = lax.broadcasted_iota(jnp.int32, (tokens, 128), 1)
                out_ref[:, 2 * span :] = jnp.where(lane == 0, squares, 0.0)
                note_ref[:, 2 * span :] = jnp.where(
                    lane == 0, high.astype(F32), jnp.where(lane == 1, low.astype(F32), 0.0)
                ).astype(BF)

        return body

    sums, sum_notes = [], []
    for c, (lo, hi) in enumerate(pieces_at):
        operands = [theirs, gate_own, up_own, gate_near, up_near] + [mine] * (c == 0)
        long_width = 2 * (hi - lo) + 128 * (c == 0)
        value, value_note = kernel(
            gate_up(lo, hi, c == 0),
            f"gate_up_{c}",
            [sds((tokens, long_width), F32), sds((tokens, long_width), BF)],
            [VM] * len(operands),
            operands,
            flops=tokens * rows_in * hidden_width,
        )
        sums.append(value)
        sum_notes.append(value_note)
    sum_others = [hop(value, "heads", 2, 1) for value in sum_notes]
    (down_near,) = fetch([sum_notes[-1]], [down_weight], "fetch_down")

    def down_piece(c, own_ref, other_ref, first_ref, first_other_ref, weight_ref):
        lo, hi = pieces_at[c]
        span, at = hi - lo, 2 * cut
        other = first_other_ref[:, at:].astype(F32)
        squares = first_ref[:, at : at + 1] + other[:, 0:1] + other[:, 1:2]
        inv_rms = lax.rsqrt(squares / features + EPS)
        gate, up = [
            (
                own_ref[:, k * span : (k + 1) * span]
                + other_ref[:, k * span : (k + 1) * span].astype(F32)
            )
            * inv_rms
            for k in range(2)
        ]
        hidden = (jax.nn.gelu(gate, approximate=True) * up).astype(BF)
        return jnp.dot(hidden, weight_ref[lo:hi, :], preferred_element_type=F32)

    def down_first(own_ref, other_ref, weight_ref, out_ref):
        out_ref[...] = down_piece(0, own_ref, other_ref, own_ref, other_ref, weight_ref)

    (down_part,) = kernel(
        down_first,
        "down_first",
        [sds((tokens, out_width), F32)],
        [VM] * 3,
        [sums[0], sum_others[0], down_near],
        flops=tokens * hidden_width * out_width,
    )

    def down_last(
        own_ref, other_ref, first_ref, first_other_ref, part_ref, weight_ref, keep_ref, away_ref
    ):
        down = part_ref[...] + down_piece(
            1, own_ref, other_ref, first_ref, first_other_ref, weight_ref
        )
        first = lax.axis_index("rows") == 0
        keep_ref[...] = jnp.where(first, down[:toks], down[toks:])
        away_ref[...] = jnp.where(first, down[toks:], down[:toks]).astype(BF)

    keep, away = kernel(
        down_last,
        "down_last",
        [sds((toks, out_width), F32), sds((toks, out_width), BF)],
        [VM] * 6,
        [sums[1], sum_others[1], sums[0], sum_others[0], down_part, down_near],
        limit=12,
    )
    back = hop(away, "rows", 2, 1)

    def owners(keep_ref, back_ref, own_ref, *piece_refs):
        total = keep_ref[...] + back_ref[...].astype(F32)
        blocks = [total[k * tok_dev : (k + 1) * tok_dev] for k in range(blks)]
        at = lax.axis_index("blk")
        for s, ref in enumerate((own_ref,) + piece_refs):
            value = blocks[0]
            for k in range(1, blks):
                value = jnp.where(at == (k ^ s), blocks[k], value)
            ref[...] = value.astype(ref.dtype)

    own, *sends = kernel(
        owners,
        "owners",
        [sds((tok_dev, out_width), F32)] + [sds((tok_dev, out_width), BF)] * (blks - 1),
        [VM, VM],
        [keep, back],
    )
    for s in reversed(range(1, blks)):
        own = own + hop(sends[s - 1], "blk", blks, s).astype(F32)
    branch = (own * keep_own).astype(BF)
    stream = stream.reshape(2, blks, tok_dev, width).swapaxes(0, 1).reshape(tokens, width)
    return (stream, branch)


def solution(mesh):
    size = dict(mesh.shape)
    direct = size["blk"] == 4 and size["heads"] == 2 and size["rows"] == 2
    placed = (
        P(("groups", "blk", "rows"), "heads", None),
        P(("groups", "blk"), "heads", None),
        P(("groups", "blk"), "heads", None),
        P("groups", ("blk", "rows")),
        P(("blk", "rows")),
        P("heads", ("blk", "rows")),
        P(("blk", "rows")),
        P("heads", ("blk", "rows")),
        P("heads", ("blk", "rows")),
        P(("blk", "rows"), "heads"),
        P("groups"),
        P("groups", None),
    )
    return jax.shard_map(
        shards_direct if direct else shards_any,
        mesh=mesh,
        in_specs=placed,
        out_specs=(P("groups", ("blk", "rows")), P(("groups", "blk", "rows"), "heads")),
        check_vma=False,
    )
```

```python
import jax
import jax.numpy as jnp
from jax import lax
from jax.experimental import pallas as pl
from jax.experimental.pallas import tpu as pltpu
from jax.sharding import PartitionSpec as P

LEN = 128
EPS = 1e-06
BF = jnp.bfloat16
F32 = jnp.float32


def token_masks(cand_lengths, masked_pos, tokens):
    positions = jnp.arange(tokens, dtype=jnp.int32) % LEN
    length_tok = jnp.repeat(cand_lengths, LEN)[:tokens]
    valid_tok = positions < length_tok
    slots = jnp.arange(LEN, dtype=jnp.int32)
    masked_tok = jnp.any(masked_pos[:, :, None] == slots[None, None, :], axis=1).reshape(-1)[
        :tokens
    ]
    return (valid_tok, masked_tok)


def shards_any(
    queries,
    src_keys,
    src_values,
    dec_state,
    mask_embed,
    out_weight,
    norm_gain,
    gate_weight,
    up_weight,
    down_weight,
    cand_lengths,
    masked_pos,
):
    tok_dev, local_heads, head_size = queries.shape
    kv_local = src_keys.shape[1]
    group_size = local_heads // kv_local
    score_scale = head_size ** (-0.5)
    features = dec_state.shape[1] * lax.axis_size("blk") * lax.axis_size("rows")
    queries_all = lax.all_gather(queries, "blk", axis=0, tiled=True)
    gathered_rows = queries_all.shape[0]
    grouped = queries_all.reshape(gathered_rows, kv_local, group_size, head_size)
    scores = (
        jnp.einsum("tgjd,kgd->tgjk", grouped, src_keys, preferred_element_type=F32) * score_scale
    )
    local_peak = jnp.max(scores, axis=3)
    weights = jnp.exp(scores - local_peak[..., None])
    totals = jnp.sum(weights, axis=3)
    numerator = jnp.einsum(
        "tgjk,kgd->tgjd", weights.astype(BF), src_values, preferred_element_type=F32
    )
    highest = lax.pmax(local_peak, "blk")
    factor = jnp.exp(local_peak - highest)
    numer_own, totals_own = (
        lax.psum_scatter(
            (numerator * factor[..., None]).astype(BF), "blk", scatter_dimension=0, tiled=True
        ).astype(F32),
        lax.psum_scatter(
            (totals * factor).astype(BF), "blk", scatter_dimension=0, tiled=True
        ).astype(F32),
    )
    attn_own = (
        (numer_own / totals_own[..., None]).astype(BF).reshape(tok_dev, local_heads * head_size)
    )
    attn_all = lax.all_gather(attn_own, ("blk", "rows"), axis=0, tiled=True)
    tokens = attn_all.shape[0]
    projected = lax.psum(
        jnp.dot(attn_all, out_weight, preferred_element_type=F32).astype(BF), "heads"
    ).astype(F32)
    valid_tok, masked_tok = token_masks(cand_lengths, masked_pos, tokens)
    base_state = jnp.where(masked_tok[:, None], mask_embed[None, :], dec_state).astype(F32)
    stream_mid = base_state + projected
    squares = lax.psum(jnp.sum(stream_mid * stream_mid, axis=1), ("blk", "rows"))
    inv_rms = lax.rsqrt(squares / features + EPS)[:, None]
    normed = (stream_mid * inv_rms * norm_gain.astype(F32)).astype(BF)
    keep_mask = valid_tok.astype(F32)[:, None]
    stream = (stream_mid * keep_mask).astype(BF)
    normed_full = lax.all_gather(normed, ("blk", "rows"), axis=1, tiled=True)
    feature_width = gate_weight.shape[0]
    column_block = lax.dynamic_slice_in_dim(
        normed_full, lax.axis_index("heads") * feature_width, feature_width, 1
    )
    gate_part = jnp.dot(column_block, gate_weight, preferred_element_type=F32)
    up_part = jnp.dot(column_block, up_weight, preferred_element_type=F32)
    gate_rows, up_rows = (
        lax.psum(gate_part.astype(BF), "heads").astype(F32),
        lax.psum(up_part.astype(BF), "heads").astype(F32),
    )
    hidden = (jax.nn.gelu(gate_rows, approximate=True) * up_rows).astype(BF)
    down_out = lax.psum_scatter(
        jnp.dot(hidden, down_weight, preferred_element_type=F32),
        ("blk", "rows"),
        scatter_dimension=0,
        tiled=True,
    )
    own_start = (lax.axis_index("blk") * lax.axis_size("rows") + lax.axis_index("rows")) * tok_dev
    keep_own = lax.dynamic_slice_in_dim(keep_mask, own_start, tok_dev, 0)
    return (stream, (down_out * keep_own).astype(BF))


VM = pl.BlockSpec(memory_space=pltpu.VMEM)
ANY = pl.BlockSpec(memory_space=pl.ANY)
MIB = 1 << 20


def hop(value, axis, size, step):
    return lax.ppermute(value, axis, [(i, i ^ step) for i in range(size)])


def kernel(body, name, outs, specs, args, limit=8, flops=0, aliases=None):
    near = [a for a, spec in zip(args, specs) if spec is VM]
    size = sum(a.size * a.dtype.itemsize for a in near + list(outs))
    return pl.pallas_call(
        body,
        out_shape=outs,
        in_specs=specs,
        out_specs=[VM] * len(outs),
        input_output_aliases=aliases or {},
        compiler_params=pltpu.CompilerParams(vmem_limit_bytes=limit * MIB),
        cost_estimate=pl.CostEstimate(flops=flops, bytes_accessed=size, transcendentals=0),
        name=name,
    )(*args)


def fetch(after, arrays, name, rows=None, into=None):
    n, skip = len(arrays), len(after)
    begun = list(into or [])

    def body(*refs):
        sources = refs[skip : skip + n]
        targets, sems = refs[-1 - n : -1], refs[-1]
        copies = []
        for i, (source, target) in enumerate(zip(sources, targets)):
            if rows is not None:
                source, target = source.at[pl.ds(*rows)], target.at[pl.ds(*rows)]
            copies.append(pltpu.make_async_copy(source, target, sems.at[i]))
        for copy in copies:
            copy.start()
        for copy in copies:
            copy.wait()

    size = sum(a.size * a.dtype.itemsize for a in arrays)
    return pl.pallas_call(
        body,
        out_shape=[jax.ShapeDtypeStruct(a.shape, a.dtype) for a in arrays],
        in_specs=[ANY] * (skip + n) + [VM] * len(begun),
        out_specs=[VM] * n,
        input_output_aliases={skip + n + i: i for i in range(len(begun))},
        scratch_shapes=[pltpu.SemaphoreType.DMA((n,))],
        compiler_params=pltpu.CompilerParams(vmem_limit_bytes=MIB),
        cost_estimate=pl.CostEstimate(flops=0, bytes_accessed=2 * size, transcendentals=0),
        name=name,
    )(*after, *[pltpu.with_memory_space_constraint(a, pltpu.HBM) for a in arrays], *begun)


def parts_of(value, count):
    out = []
    for _ in range(count):
        part = lax.reduce_precision(value, 8, 7)
        out.append(part.astype(BF))
        value = value - part
    return out


def split_in(value, count):
    out = []
    for _ in range(count):
        part = value.astype(BF)
        out.append(part)
        value = value - part.astype(F32)
    return out


def shards_direct(
    queries,
    src_keys,
    src_values,
    dec_state,
    mask_embed,
    out_weight,
    norm_gain,
    gate_weight,
    up_weight,
    down_weight,
    cand_lengths,
    masked_pos,
):
    blks, head_parts = lax.axis_size("blk"), lax.axis_size("heads")
    blk, head, row = (lax.axis_index(name) for name in ("blk", "heads", "rows"))
    tok_dev, local_heads, head_size = queries.shape
    kv_local = src_keys.shape[1]
    group_size = local_heads // kv_local
    score_scale = head_size ** (-0.5)
    width = dec_state.shape[1]
    features = width * blks * 2
    half = blks // head_parts
    hidden_width, out_width = gate_weight.shape[1], down_weight.shape[1]
    toks = tok_dev * blks
    tokens = toks * 2
    sds = jax.ShapeDtypeStruct

    def inner(value):
        value = value.reshape((blks, 2, tok_dev) + value.shape[1:])
        return jnp.swapaxes(value, 0, 1).reshape((tokens,) + value.shape[3:])

    valid_tok, masked_tok = token_masks(cand_lengths, masked_pos, tokens)
    base_state = inner(jnp.where(masked_tok[:, None], mask_embed[None, :], dec_state))
    keep_mask = valid_tok.astype(F32)
    keep_inner = inner(keep_mask)[:, None]
    own_start = (blk * 2 + row) * tok_dev
    keep_own = lax.dynamic_slice_in_dim(keep_mask, own_start, tok_dev, 0)[:, None]
    gain = norm_gain[None, :]

    (queries_near,) = fetch([], [queries], "fetch_queries")
    blocks = [queries_near] * blks
    for s in [1] + list(reversed(range(2, blks))):
        piece = hop(queries, "blk", blks, s)
        blocks = [jnp.where(blk == (k ^ s), piece, block) for k, block in enumerate(blocks)]
        blocks = list(lax.optimization_barrier(tuple(blocks)))
    q_all = jnp.concatenate(blocks, axis=0)
    q_all, base_state, keep_inner, keep_own, gain = lax.optimization_barrier(
        (q_all, base_state, keep_inner, keep_own, gain)
    )
    grouped = q_all.reshape(toks, kv_local, group_size, head_size)
    scores = (
        jnp.einsum("tgjd,kgd->tgjk", grouped, src_keys, preferred_element_type=F32) * score_scale
    )
    peak = jnp.max(scores, axis=3)
    weights = jnp.exp(scores - peak[..., None])
    totals = jnp.sum(weights, axis=3)
    numerator = jnp.einsum(
        "tgjk,kgd->tgjd", weights.astype(BF), src_values, preferred_element_type=F32
    )
    partial = (numerator / totals[..., None]).astype(BF)
    partial = partial.transpose(1, 2, 0, 3).reshape(local_heads * toks, head_size)
    partial, peak, totals = lax.optimization_barrier((partial, peak, totals))
    level = (peak + jnp.log(totals)).reshape(toks, local_heads)
    side = jnp.concatenate(parts_of(level, 3), axis=1)
    side = jnp.pad(side, ((0, 0), (0, head_size - side.shape[1])))
    note = jnp.concatenate([partial, side], axis=0)
    notes = [note] + [hop(note, "blk", blks, s) for s in range(1, blks)]
    proj_near, gate_near = fetch([note], [out_weight.T, gate_weight], "fetch_proj_gate")

    def combine(*refs):
        ins, out = refs[:blks], refs[blks + 2]
        base = local_heads * toks
        levels = []
        for ref in ins:
            side = ref[base : base + toks, :].astype(F32)
            levels.append(
                side[:, :local_heads]
                + side[:, local_heads : 2 * local_heads]
                + side[:, 2 * local_heads : 3 * local_heads]
            )
        top = levels[0]
        for one in levels[1:]:
            top = jnp.maximum(top, one)
        shares = [jnp.exp(one - top) for one in levels]
        total = shares[0]
        for one in shares[1:]:
            total = total + one
        shares = [one / total for one in shares]
        for h in range(local_heads):
            acc = None
            for share, ref in zip(shares, ins):
                term = share[:, h : h + 1] * ref[h * toks : (h + 1) * toks, :].astype(F32)
                acc = term if acc is None else acc + term
            out[:, h * head_size : (h + 1) * head_size] = acc.astype(BF)

    attn, proj_near, gate_near = kernel(
        combine,
        "combine",
        [sds((toks, local_heads * head_size), BF), sds(proj_near.shape, BF), sds(gate_near.shape, BF)],
        [VM] * (blks + 2),
        notes + [proj_near, gate_near],
        aliases={blks: 1, blks + 1: 2},
    )
    other = hop(attn, "rows", 2, 1)
    across = (((1,), (1,)), ((), ()))

    def project_own(own_ref, weight_ref, gate_ref, out_ref, gate_out):
        out_ref[...] = lax.dot_general(
            own_ref[...], weight_ref[...], across, preferred_element_type=F32
        )

    proj_own, gate_near = kernel(
        project_own,
        "project_own",
        [sds((toks, width), F32), sds(gate_near.shape, BF)],
        [VM] * 3,
        [attn, proj_near, gate_near],
        aliases={2: 1},
    )

    def project(own_ref, other_ref, weight_ref, gate_ref, out_ref, gate_out):
        first = lax.axis_index("rows") == 0
        own = own_ref[...]
        other = lax.dot_general(
            other_ref[...], weight_ref[...], across, preferred_element_type=F32
        )
        out_ref[:toks] = jnp.where(first, own, other).astype(BF)
        out_ref[toks:] = jnp.where(first, other, own).astype(BF)

    proj, gate_near = kernel(
        project,
        "project",
        [sds((tokens, width), BF), sds(gate_near.shape, BF)],
        [VM] * 4,
        [proj_own, other, proj_near, gate_near],
        aliases={3: 1},
    )
    proj_other = hop(proj, "heads", 2, 1)
    up_cut = up_weight.shape[0] // 32 * 16
    (up_near,) = fetch([proj], [up_weight], "fetch_up_first", rows=(0, up_cut))

    lanes = -(-(width + 2) // 128) * 128

    def middle(
        base_ref, keep_ref, gain_ref, own_ref, other_ref, gate_ref, up_ref, stream_ref, note_ref, *_
    ):
        mid = base_ref[...].astype(F32) + (own_ref[...].astype(F32) + other_ref[...].astype(F32))
        stream_ref[...] = (mid * keep_ref[...]).astype(BF)
        note_ref[:, :width] = (mid * gain_ref[...].astype(F32)).astype(BF)
        squares = jnp.sum(mid * mid, axis=1, keepdims=True)
        high, low = split_in(squares, 2)
        lane = lax.broadcasted_iota(jnp.int32, (tokens, lanes - width), 1)
        note_ref[:, width:] = jnp.where(
            lane == 0, high.astype(F32), jnp.where(lane == 1, low.astype(F32), 0.0)
        ).astype(BF)

    stream, note, gate_near, up_near = kernel(
        middle,
        "middle",
        [
            sds((tokens, width), BF),
            sds((tokens, lanes), BF),
            sds(gate_near.shape, BF),
            sds(up_near.shape, BF),
        ],
        [VM] * 7,
        [base_state, keep_inner, gain, proj, proj_other, gate_near, up_near],
        aliases={5: 2, 6: 3},
    )

    far_pairs, near_pairs = [], []
    for b in range(blks):
        for h in range(head_parts):
            far_pairs.append((b * head_parts + h, (b ^ 3) * head_parts + h))
            to = (b ^ 1, h) if b // half == h else (b ^ 2, 1 - h)
            near_pairs.append((b * head_parts + h, to[0] * head_parts + to[1]))
    near = lax.ppermute(note, ("blk", "heads"), near_pairs)
    far = lax.ppermute(note, ("blk", "heads"), far_pairs)
    (up_near,) = fetch(
        [note],
        [up_weight],
        "fetch_up_last",
        rows=(up_cut, up_weight.shape[0] - up_cut),
        into=[up_near],
    )
    lanes_all = note.shape[1]

    def pick(own_ref, near_ref, far_ref, gate_ref, up_ref, out_ref):
        at = lax.axis_index("blk")
        inside = at // half == lax.axis_index("heads")
        odd = at % 2 == 1
        same = jnp.where(inside, own_ref[...], near_ref[...])
        pair = jnp.where(inside, near_ref[...], far_ref[...])
        out_ref[0] = jnp.where(odd, pair, same)
        out_ref[1] = jnp.where(odd, same, pair)

    (mine,) = kernel(
        pick,
        "pick",
        [sds((half, tokens, lanes_all), BF)],
        [VM, VM, VM, ANY, ANY],
        [note, near, far, gate_near, up_near],
    )
    theirs = hop(mine, "rows", 2, 1)
    rows_in = gate_weight.shape[0]

    def tile_products(tiles_ref, weight_ref, row_at):
        total = None
        for k in range(half):
            start = pl.multiple_of((k * 2 + row_at) * width, 16)
            term = jnp.dot(
                tiles_ref[k, :, :width],
                weight_ref[pl.ds(start, width), :],
                preferred_element_type=F32,
            )
            total = term if total is None else total + term
        return total

    def inner_products(mine_ref, gate_ref, up_ref, gate_out, up_out):
        gate_out[...] = tile_products(mine_ref, gate_ref, lax.axis_index("rows"))
        up_out[...] = tile_products(mine_ref, up_ref, lax.axis_index("rows"))

    gate_own, up_own = kernel(
        inner_products,
        "inner_products",
        [sds((tokens, hidden_width), F32)] * 2,
        [VM, VM, VM],
        [mine, gate_near, up_near],
        flops=2 * tokens * rows_in * hidden_width,
    )

    cut = -(-hidden_width // 512) * 256
    pieces_at = [(0, cut), (cut, hidden_width)]

    def gate_up(lo, hi, with_squares):
        span = hi - lo

        def body(*refs):
            theirs_ref, gate_in, up_in, gate_w, up_w = refs[:5]
            out_ref, note_ref = refs[-2:]
            row_at = 1 - lax.axis_index("rows")
            for k, (own, weight) in enumerate(((gate_in, gate_w), (up_in, up_w))):
                value = own[:, lo:hi] + tile_products(theirs_ref, weight.at[:, lo:hi], row_at)
                out_ref[:, k * span : (k + 1) * span] = value
                note_ref[:, k * span : (k + 1) * span] = value.astype(BF)
            if with_squares:
                squares = None
                for k in range(half):
                    for ref in (refs[5], theirs_ref):
                        here = ref[k, :, width : width + 2].astype(F32)
                        squares = here if squares is None else squares + here
                squares = squares[:, 0:1] + squares[:, 1:2]
                high, low = split_in(squares, 2)
                lane = lax.broadcasted_iota(jnp.int32, (tokens, 128), 1)
                out_ref[:, 2 * span :] = jnp.where(lane == 0, squares, 0.0)
                note_ref[:, 2 * span :] = jnp.where(
                    lane == 0, high.astype(F32), jnp.where(lane == 1, low.astype(F32), 0.0)
                ).astype(BF)

        return body

    sums, sum_notes = [], []
    for c, (lo, hi) in enumerate(pieces_at):
        operands = [theirs, gate_own, up_own, gate_near, up_near] + [mine] * (c == 0)
        long_width = 2 * (hi - lo) + 128 * (c == 0)
        value, value_note = kernel(
            gate_up(lo, hi, c == 0),
            f"gate_up_{c}",
            [sds((tokens, long_width), F32), sds((tokens, long_width), BF)],
            [VM] * len(operands),
            operands,
            flops=tokens * rows_in * hidden_width,
        )
        sums.append(value)
        sum_notes.append(value_note)
    sum_others = [hop(value, "heads", 2, 1) for value in sum_notes]
    (down_near,) = fetch([sum_notes[-1]], [down_weight], "fetch_down")

    def down_piece(c, own_ref, other_ref, first_ref, first_other_ref, weight_ref):
        lo, hi = pieces_at[c]
        span, at = hi - lo, 2 * cut
        other = first_other_ref[:, at:].astype(F32)
        squares = first_ref[:, at : at + 1] + other[:, 0:1] + other[:, 1:2]
        inv_rms = lax.rsqrt(squares / features + EPS)
        gate, up = [
            (
                own_ref[:, k * span : (k + 1) * span]
                + other_ref[:, k * span : (k + 1) * span].astype(F32)
            )
            * inv_rms
            for k in range(2)
        ]
        hidden = (jax.nn.gelu(gate, approximate=True) * up).astype(BF)
        return jnp.dot(hidden, weight_ref[lo:hi, :], preferred_element_type=F32)

    def down_first(own_ref, other_ref, weight_ref, out_ref):
        out_ref[...] = down_piece(0, own_ref, other_ref, own_ref, other_ref, weight_ref)

    (down_part,) = kernel(
        down_first,
        "down_first",
        [sds((tokens, out_width), F32)],
        [VM] * 3,
        [sums[0], sum_others[0], down_near],
        flops=tokens * hidden_width * out_width,
    )

    def down_last(
        own_ref, other_ref, first_ref, first_other_ref, part_ref, weight_ref, keep_ref, away_ref
    ):
        down = part_ref[...] + down_piece(
            1, own_ref, other_ref, first_ref, first_other_ref, weight_ref
        )
        first = lax.axis_index("rows") == 0
        keep_ref[...] = jnp.where(first, down[:toks], down[toks:])
        away_ref[...] = jnp.where(first, down[toks:], down[:toks]).astype(BF)

    keep, away = kernel(
        down_last,
        "down_last",
        [sds((toks, out_width), F32), sds((toks, out_width), BF)],
        [VM] * 6,
        [sums[1], sum_others[1], sums[0], sum_others[0], down_part, down_near],
        limit=12,
    )
    back = hop(away, "rows", 2, 1)

    def owners(keep_ref, back_ref, own_ref, *piece_refs):
        total = keep_ref[...] + back_ref[...].astype(F32)
        blocks = [total[k * tok_dev : (k + 1) * tok_dev] for k in range(blks)]
        at = lax.axis_index("blk")
        for s, ref in enumerate((own_ref,) + piece_refs):
            value = blocks[0]
            for k in range(1, blks):
                value = jnp.where(at == (k ^ s), blocks[k], value)
            ref[...] = value.astype(ref.dtype)

    own, *sends = kernel(
        owners,
        "owners",
        [sds((tok_dev, out_width), F32)] + [sds((tok_dev, out_width), BF)] * (blks - 1),
        [VM, VM],
        [keep, back],
    )
    for s in reversed(range(1, blks)):
        own = own + hop(sends[s - 1], "blk", blks, s).astype(F32)
    branch = (own * keep_own).astype(BF)
    stream = stream.reshape(2, blks, tok_dev, width).swapaxes(0, 1).reshape(tokens, width)
    return (stream, branch)


def solution(mesh):
    size = dict(mesh.shape)
    direct = size["blk"] == 4 and size["heads"] == 2 and size["rows"] == 2
    placed = (
        P(("groups", "blk", "rows"), "heads", None),
        P(("groups", "blk"), "heads", None),
        P(("groups", "blk"), "heads", None),
        P("groups", ("blk", "rows")),
        P(("blk", "rows")),
        P("heads", ("blk", "rows")),
        P(("blk", "rows")),
        P("heads", ("blk", "rows")),
        P("heads", ("blk", "rows")),
        P(("blk", "rows"), "heads"),
        P("groups"),
        P("groups", None),
    )
    return jax.shard_map(
        shards_direct if direct else shards_any,
        mesh=mesh,
        in_specs=placed,
        out_specs=(P("groups", ("blk", "rows")), P(("groups", "blk", "rows"), "heads")),
        check_vma=False,
    )
```

```python
import jax
import jax.numpy as jnp
from jax import lax
from jax.experimental import pallas as pl
from jax.experimental.pallas import tpu as pltpu
from jax.sharding import PartitionSpec as P

LEN = 128
EPS = 1e-06
BF = jnp.bfloat16
F32 = jnp.float32


def token_masks(cand_lengths, masked_pos, tokens):
    positions = jnp.arange(tokens, dtype=jnp.int32) % LEN
    length_tok = jnp.repeat(cand_lengths, LEN)[:tokens]
    valid_tok = positions < length_tok
    slots = jnp.arange(LEN, dtype=jnp.int32)
    masked_tok = jnp.any(masked_pos[:, :, None] == slots[None, None, :], axis=1).reshape(-1)[
        :tokens
    ]
    return (valid_tok, masked_tok)


def shards_any(
    queries,
    src_keys,
    src_values,
    dec_state,
    mask_embed,
    out_weight,
    norm_gain,
    gate_weight,
    up_weight,
    down_weight,
    cand_lengths,
    masked_pos,
):
    tok_dev, local_heads, head_size = queries.shape
    kv_local = src_keys.shape[1]
    group_size = local_heads // kv_local
    score_scale = head_size ** (-0.5)
    features = dec_state.shape[1] * lax.axis_size("blk") * lax.axis_size("rows")
    queries_all = lax.all_gather(queries, "blk", axis=0, tiled=True)
    gathered_rows = queries_all.shape[0]
    grouped = queries_all.reshape(gathered_rows, kv_local, group_size, head_size)
    scores = (
        jnp.einsum("tgjd,kgd->tgjk", grouped, src_keys, preferred_element_type=F32) * score_scale
    )
    local_peak = jnp.max(scores, axis=3)
    weights = jnp.exp(scores - local_peak[..., None])
    totals = jnp.sum(weights, axis=3)
    numerator = jnp.einsum(
        "tgjk,kgd->tgjd", weights.astype(BF), src_values, preferred_element_type=F32
    )
    highest = lax.pmax(local_peak, "blk")
    factor = jnp.exp(local_peak - highest)
    numer_own, totals_own = (
        lax.psum_scatter(
            (numerator * factor[..., None]).astype(BF), "blk", scatter_dimension=0, tiled=True
        ).astype(F32),
        lax.psum_scatter(
            (totals * factor).astype(BF), "blk", scatter_dimension=0, tiled=True
        ).astype(F32),
    )
    attn_own = (
        (numer_own / totals_own[..., None]).astype(BF).reshape(tok_dev, local_heads * head_size)
    )
    attn_all = lax.all_gather(attn_own, ("blk", "rows"), axis=0, tiled=True)
    tokens = attn_all.shape[0]
    projected = lax.psum(
        jnp.dot(attn_all, out_weight, preferred_element_type=F32).astype(BF), "heads"
    ).astype(F32)
    valid_tok, masked_tok = token_masks(cand_lengths, masked_pos, tokens)
    base_state = jnp.where(masked_tok[:, None], mask_embed[None, :], dec_state).astype(F32)
    stream_mid = base_state + projected
    squares = lax.psum(jnp.sum(stream_mid * stream_mid, axis=1), ("blk", "rows"))
    inv_rms = lax.rsqrt(squares / features + EPS)[:, None]
    normed = (stream_mid * inv_rms * norm_gain.astype(F32)).astype(BF)
    keep_mask = valid_tok.astype(F32)[:, None]
    stream = (stream_mid * keep_mask).astype(BF)
    normed_full = lax.all_gather(normed, ("blk", "rows"), axis=1, tiled=True)
    feature_width = gate_weight.shape[0]
    column_block = lax.dynamic_slice_in_dim(
        normed_full, lax.axis_index("heads") * feature_width, feature_width, 1
    )
    gate_part = jnp.dot(column_block, gate_weight, preferred_element_type=F32)
    up_part = jnp.dot(column_block, up_weight, preferred_element_type=F32)
    gate_rows, up_rows = (
        lax.psum(gate_part.astype(BF), "heads").astype(F32),
        lax.psum(up_part.astype(BF), "heads").astype(F32),
    )
    hidden = (jax.nn.gelu(gate_rows, approximate=True) * up_rows).astype(BF)
    down_out = lax.psum_scatter(
        jnp.dot(hidden, down_weight, preferred_element_type=F32),
        ("blk", "rows"),
        scatter_dimension=0,
        tiled=True,
    )
    own_start = (lax.axis_index("blk") * lax.axis_size("rows") + lax.axis_index("rows")) * tok_dev
    keep_own = lax.dynamic_slice_in_dim(keep_mask, own_start, tok_dev, 0)
    return (stream, (down_out * keep_own).astype(BF))


VM = pl.BlockSpec(memory_space=pltpu.VMEM)
ANY = pl.BlockSpec(memory_space=pl.ANY)
MIB = 1 << 20


def hop(value, axis, size, step):
    return lax.ppermute(value, axis, [(i, i ^ step) for i in range(size)])


def kernel(body, name, outs, specs, args, limit=8, flops=0, aliases=None, scratch=()):
    near = [a for a, spec in zip(args, specs) if spec is VM]
    size = sum(a.size * a.dtype.itemsize for a in near + list(outs))
    return pl.pallas_call(
        body,
        out_shape=outs,
        in_specs=specs,
        out_specs=[VM] * len(outs),
        input_output_aliases=aliases or {},
        scratch_shapes=list(scratch),
        compiler_params=pltpu.CompilerParams(vmem_limit_bytes=limit * MIB),
        cost_estimate=pl.CostEstimate(flops=flops, bytes_accessed=size, transcendentals=0),
        name=name,
    )(*args)


def fetch(after, arrays, name, rows=None, into=None):
    n, skip = len(arrays), len(after)
    begun = list(into or [])

    def body(*refs):
        sources = refs[skip : skip + n]
        targets, sems = refs[-1 - n : -1], refs[-1]
        copies = []
        for i, (source, target) in enumerate(zip(sources, targets)):
            if rows is not None:
                source, target = source.at[pl.ds(*rows)], target.at[pl.ds(*rows)]
            copies.append(pltpu.make_async_copy(source, target, sems.at[i]))
        for copy in copies:
            copy.start()
        for copy in copies:
            copy.wait()

    size = sum(a.size * a.dtype.itemsize for a in arrays)
    return pl.pallas_call(
        body,
        out_shape=[jax.ShapeDtypeStruct(a.shape, a.dtype) for a in arrays],
        in_specs=[ANY] * (skip + n) + [VM] * len(begun),
        out_specs=[VM] * n,
        input_output_aliases={skip + n + i: i for i in range(len(begun))},
        scratch_shapes=[pltpu.SemaphoreType.DMA((n,))],
        compiler_params=pltpu.CompilerParams(vmem_limit_bytes=MIB),
        cost_estimate=pl.CostEstimate(flops=0, bytes_accessed=2 * size, transcendentals=0),
        name=name,
    )(*after, *[pltpu.with_memory_space_constraint(a, pltpu.HBM) for a in arrays], *begun)


def parts_of(value, count):
    out = []
    for _ in range(count):
        part = lax.reduce_precision(value, 8, 7)
        out.append(part.astype(BF))
        value = value - part
    return out


def split_in(value, count):
    out = []
    for _ in range(count):
        part = value.astype(BF)
        out.append(part)
        value = value - part.astype(F32)
    return out


def shards_direct(
    queries,
    src_keys,
    src_values,
    dec_state,
    mask_embed,
    out_weight,
    norm_gain,
    gate_weight,
    up_weight,
    down_weight,
    cand_lengths,
    masked_pos,
):
    blks, head_parts = lax.axis_size("blk"), lax.axis_size("heads")
    blk, head, row = (lax.axis_index(name) for name in ("blk", "heads", "rows"))
    tok_dev, local_heads, head_size = queries.shape
    kv_local = src_keys.shape[1]
    group_size = local_heads // kv_local
    score_scale = head_size ** (-0.5)
    width = dec_state.shape[1]
    features = width * blks * 2
    half = blks // head_parts
    hidden_width, out_width = gate_weight.shape[1], down_weight.shape[1]
    toks = tok_dev * blks
    tokens = toks * 2
    sds = jax.ShapeDtypeStruct

    queries_near, dec_state, mask_embed, norm_gain, masked_pos = fetch(
        [], [queries, dec_state, mask_embed, norm_gain, masked_pos], "fetch_small"
    )
    blocks = [queries_near] * blks
    for s in reversed(range(1, blks)):
        piece = hop(queries, "blk", blks, s)
        blocks = [jnp.where(blk == (k ^ s), piece, block) for k, block in enumerate(blocks)]
        blocks = list(lax.optimization_barrier(tuple(blocks)))
    q_all = jnp.concatenate(blocks, axis=0)
    grouped = q_all.reshape(toks, kv_local, group_size, head_size)
    scores = (
        jnp.einsum("tgjd,kgd->tgjk", grouped, src_keys, preferred_element_type=F32) * score_scale
    )
    peak = jnp.max(scores, axis=3)
    weights = jnp.exp(scores - peak[..., None])
    totals = jnp.sum(weights, axis=3)
    numerator = jnp.einsum(
        "tgjk,kgd->tgjd", weights.astype(BF), src_values, preferred_element_type=F32
    )
    partial = (numerator / totals[..., None]).astype(BF)
    partial = partial.transpose(1, 2, 0, 3).reshape(local_heads * toks, head_size)
    partial, peak, totals = lax.optimization_barrier((partial, peak, totals))
    level = (peak + jnp.log(totals)).reshape(toks, local_heads)
    side = jnp.concatenate(parts_of(level, 3), axis=1)
    side = jnp.pad(side, ((0, 0), (0, head_size - side.shape[1])))
    note = jnp.concatenate([partial, side], axis=0)
    notes = [note] + [hop(note, "blk", blks, s) for s in reversed(range(1, blks))]
    proj_near, gate_near = fetch([note], [out_weight.T, gate_weight], "fetch_proj_gate")

    def combine(*refs):
        ins, out = refs[:blks], refs[blks + 2]
        base = local_heads * toks
        levels = []
        for ref in ins:
            side = ref[base : base + toks, :].astype(F32)
            levels.append(
                side[:, :local_heads]
                + side[:, local_heads : 2 * local_heads]
                + side[:, 2 * local_heads : 3 * local_heads]
            )
        top = levels[0]
        for one in levels[1:]:
            top = jnp.maximum(top, one)
        shares = [jnp.exp(one - top) for one in levels]
        total = shares[0]
        for one in shares[1:]:
            total = total + one
        shares = [one / total for one in shares]
        for h in range(local_heads):
            acc = None
            for share, ref in zip(shares, ins):
                term = share[:, h : h + 1] * ref[h * toks : (h + 1) * toks, :].astype(F32)
                acc = term if acc is None else acc + term
            out[:, h * head_size : (h + 1) * head_size] = acc.astype(BF)

    attn, proj_near, gate_near = kernel(
        combine,
        "combine",
        [sds((toks, local_heads * head_size), BF), sds(proj_near.shape, BF), sds(gate_near.shape, BF)],
        [VM] * (blks + 2),
        notes + [proj_near, gate_near],
        aliases={blks: 1, blks + 1: 2},
    )
    other = hop(attn, "rows", 2, 1)
    across = (((1,), (1,)), ((), ()))

    def project_own(own_ref, weight_ref, gate_ref, out_ref, gate_out):
        out_ref[...] = lax.dot_general(
            own_ref[...], weight_ref[...], across, preferred_element_type=F32
        )

    proj_own, gate_near = kernel(
        project_own,
        "project_own",
        [sds((toks, width), F32), sds(gate_near.shape, BF)],
        [VM] * 3,
        [attn, proj_near, gate_near],
        aliases={2: 1},
    )

    def project(own_ref, other_ref, weight_ref, gate_ref, out_ref, gate_out):
        first = lax.axis_index("rows") == 0
        own = own_ref[...]
        other = lax.dot_general(
            other_ref[...], weight_ref[...], across, preferred_element_type=F32
        )
        out_ref[:toks] = jnp.where(first, own, other).astype(BF)
        out_ref[toks:] = jnp.where(first, other, own).astype(BF)

    proj, gate_near = kernel(
        project,
        "project",
        [sds((tokens, width), BF), sds(gate_near.shape, BF)],
        [VM] * 4,
        [proj_own, other, proj_near, gate_near],
        aliases={3: 1},
    )
    proj_other = hop(proj, "heads", 2, 1)
    up_cut = up_weight.shape[0] // 32 * 16
    (up_near,) = fetch([proj], [up_weight], "fetch_up_first", rows=(0, up_cut))

    lanes = -(-(width + 2) // 128) * 128

    inner = [b * 2 + r for r in range(2) for b in range(blks)]
    outer = [r * blks + b for b in range(blks) for r in range(2)]

    def shuffled(value, order, scratch):
        for at, k in enumerate(order):
            scratch[at * tok_dev : (at + 1) * tok_dev] = value[k * tok_dev : (k + 1) * tok_dev]
        return scratch[...]

    def middle(
        dec_ref,
        embed_ref,
        gain_ref,
        masked_ref,
        own_ref,
        other_ref,
        gate_ref,
        up_ref,
        mid_ref,
        note_ref,
        gate_out,
        up_out,
        base_ref,
    ):
        slots = lax.broadcasted_iota(jnp.int32, (tokens, 1), 0)
        hits = jnp.where(slots == masked_ref[...], 1.0, 0.0)
        masked = jnp.max(hits, axis=1, keepdims=True) > 0.0
        base = jnp.where(masked, embed_ref[...].astype(F32), dec_ref[...].astype(F32))
        mid = shuffled(base, inner, base_ref) + (
            own_ref[...].astype(F32) + other_ref[...].astype(F32)
        )
        mid_ref[...] = mid
        note_ref[:, :width] = (mid * gain_ref[...].astype(F32)).astype(BF)
        squares = jnp.sum(mid * mid, axis=1, keepdims=True)
        high, low = split_in(squares, 2)
        lane = lax.broadcasted_iota(jnp.int32, (tokens, lanes - width), 1)
        note_ref[:, width:] = jnp.where(
            lane == 0, high.astype(F32), jnp.where(lane == 1, low.astype(F32), 0.0)
        ).astype(BF)

    mid, note, gate_near, up_near = kernel(
        middle,
        "middle",
        [
            sds((tokens, width), F32),
            sds((tokens, lanes), BF),
            sds(gate_near.shape, BF),
            sds(up_near.shape, BF),
        ],
        [VM] * 8,
        [
            dec_state,
            mask_embed[None, :],
            norm_gain[None, :],
            masked_pos,
            proj,
            proj_other,
            gate_near,
            up_near,
        ],
        aliases={6: 2, 7: 3},
        scratch=[pltpu.VMEM((tokens, width), F32)],
    )

    def residual(mid_ref, length_ref, stream_ref, keep_ref, order_ref):
        slots = lax.broadcasted_iota(jnp.int32, (tokens, 1), 0)
        keep = jnp.where(slots < length_ref[...], 1.0, 0.0)
        stream_ref[...] = (shuffled(mid_ref[...], outer, order_ref) * keep).astype(BF)
        first = (lax.axis_index("blk") * 2 + lax.axis_index("rows")) * tok_dev
        owned = first + lax.broadcasted_iota(jnp.int32, (tok_dev, 1), 0)
        keep_ref[...] = jnp.where(owned < length_ref[...], 1.0, 0.0)

    stream, keep_own = kernel(
        residual,
        "residual",
        [sds((tokens, width), BF), sds((tok_dev, 1), F32)],
        [VM] * 2,
        [mid, cand_lengths[None, :]],
        scratch=[pltpu.VMEM((tokens, width), F32)],
    )

    far_pairs, near_pairs = [], []
    for b in range(blks):
        for h in range(head_parts):
            far_pairs.append((b * head_parts + h, (b ^ 3) * head_parts + h))
            to = (b ^ 1, h) if b // half == h else (b ^ 2, 1 - h)
            near_pairs.append((b * head_parts + h, to[0] * head_parts + to[1]))
    near = lax.ppermute(note, ("blk", "heads"), near_pairs)
    far = lax.ppermute(note, ("blk", "heads"), far_pairs)
    (up_near,) = fetch(
        [note],
        [up_weight],
        "fetch_up_last",
        rows=(up_cut, up_weight.shape[0] - up_cut),
        into=[up_near],
    )
    lanes_all = note.shape[1]

    def pick(own_ref, far_ref, near_ref, gate_ref, up_ref, out_ref):
        at = lax.axis_index("blk")
        inside = at // half == lax.axis_index("heads")
        odd = at % 2 == 1
        same = jnp.where(inside, own_ref[...], near_ref[...])
        pair = jnp.where(inside, near_ref[...], far_ref[...])
        out_ref[0] = jnp.where(odd, pair, same)
        out_ref[1] = jnp.where(odd, same, pair)

    (mine,) = kernel(
        pick,
        "pick",
        [sds((half, tokens, lanes_all), BF)],
        [VM, VM, VM, ANY, ANY],
        [note, far, near, gate_near, up_near],
    )
    theirs = hop(mine, "rows", 2, 1)
    rows_in = gate_weight.shape[0]

    def tile_products(tiles_ref, weight_ref, row_at):
        total = None
        for k in range(half):
            start = pl.multiple_of((k * 2 + row_at) * width, 16)
            term = jnp.dot(
                tiles_ref[k, :, :width],
                weight_ref[pl.ds(start, width), :],
                preferred_element_type=F32,
            )
            total = term if total is None else total + term
        return total

    def inner_products(mine_ref, gate_ref, up_ref, gate_out, up_out):
        gate_out[...] = tile_products(mine_ref, gate_ref, lax.axis_index("rows"))
        up_out[...] = tile_products(mine_ref, up_ref, lax.axis_index("rows"))

    gate_own, up_own = kernel(
        inner_products,
        "inner_products",
        [sds((tokens, hidden_width), F32)] * 2,
        [VM, VM, VM],
        [mine, gate_near, up_near],
        flops=2 * tokens * rows_in * hidden_width,
    )

    cut = -(-hidden_width // 512) * 256
    pieces_at = [(0, cut), (cut, hidden_width)]

    def gate_up(lo, hi, with_squares):
        span = hi - lo

        def body(*refs):
            theirs_ref, gate_in, up_in, gate_w, up_w = refs[:5]
            out_ref, note_ref = refs[-2:]
            row_at = 1 - lax.axis_index("rows")
            for k, (own, weight) in enumerate(((gate_in, gate_w), (up_in, up_w))):
                value = own[:, lo:hi] + tile_products(theirs_ref, weight.at[:, lo:hi], row_at)
                out_ref[:, k * span : (k + 1) * span] = value
                note_ref[:, k * span : (k + 1) * span] = value.astype(BF)
            if with_squares:
                squares = None
                for k in range(half):
                    for ref in (refs[5], theirs_ref):
                        here = ref[k, :, width : width + 2].astype(F32)
                        squares = here if squares is None else squares + here
                squares = squares[:, 0:1] + squares[:, 1:2]
                high, low = split_in(squares, 2)
                lane = lax.broadcasted_iota(jnp.int32, (tokens, 128), 1)
                out_ref[:, 2 * span :] = jnp.where(lane == 0, squares, 0.0)
                note_ref[:, 2 * span :] = jnp.where(
                    lane == 0, high.astype(F32), jnp.where(lane == 1, low.astype(F32), 0.0)
                ).astype(BF)

        return body

    sums, sum_notes = [], []
    for c, (lo, hi) in enumerate(pieces_at):
        operands = [theirs, gate_own, up_own, gate_near, up_near] + [mine] * (c == 0)
        long_width = 2 * (hi - lo) + 128 * (c == 0)
        value, value_note = kernel(
            gate_up(lo, hi, c == 0),
            f"gate_up_{c}",
            [sds((tokens, long_width), F32), sds((tokens, long_width), BF)],
            [VM] * len(operands),
            operands,
            flops=tokens * rows_in * hidden_width,
        )
        sums.append(value)
        sum_notes.append(value_note)
    sum_others = [hop(value, "heads", 2, 1) for value in sum_notes]
    (down_near,) = fetch([sum_notes[-1]], [down_weight], "fetch_down")

    def down_piece(c, own_ref, other_ref, first_ref, first_other_ref, weight_ref):
        lo, hi = pieces_at[c]
        span, at = hi - lo, 2 * cut
        other = first_other_ref[:, at:].astype(F32)
        squares = first_ref[:, at : at + 1] + other[:, 0:1] + other[:, 1:2]
        inv_rms = lax.rsqrt(squares / features + EPS)
        gate, up = [
            (
                own_ref[:, k * span : (k + 1) * span]
                + other_ref[:, k * span : (k + 1) * span].astype(F32)
            )
            * inv_rms
            for k in range(2)
        ]
        hidden = (jax.nn.gelu(gate, approximate=True) * up).astype(BF)
        return jnp.dot(hidden, weight_ref[lo:hi, :], preferred_element_type=F32)

    def down_first(own_ref, other_ref, weight_ref, out_ref):
        out_ref[...] = down_piece(0, own_ref, other_ref, own_ref, other_ref, weight_ref)

    (down_part,) = kernel(
        down_first,
        "down_first",
        [sds((tokens, out_width), F32)],
        [VM] * 3,
        [sums[0], sum_others[0], down_near],
        flops=tokens * hidden_width * out_width,
    )

    def down_last(
        own_ref, other_ref, first_ref, first_other_ref, part_ref, weight_ref, keep_ref, away_ref
    ):
        down = part_ref[...] + down_piece(
            1, own_ref, other_ref, first_ref, first_other_ref, weight_ref
        )
        first = lax.axis_index("rows") == 0
        keep_ref[...] = jnp.where(first, down[:toks], down[toks:])
        away_ref[...] = jnp.where(first, down[toks:], down[:toks]).astype(BF)

    keep, away = kernel(
        down_last,
        "down_last",
        [sds((toks, out_width), F32), sds((toks, out_width), BF)],
        [VM] * 6,
        [sums[1], sum_others[1], sums[0], sum_others[0], down_part, down_near],
        limit=12,
    )
    back = hop(away, "rows", 2, 1)

    def owners(keep_ref, back_ref, own_ref, *piece_refs):
        total = keep_ref[...] + back_ref[...].astype(F32)
        blocks = [total[k * tok_dev : (k + 1) * tok_dev] for k in range(blks)]
        at = lax.axis_index("blk")
        for s, ref in enumerate((own_ref,) + piece_refs):
            value = blocks[0]
            for k in range(1, blks):
                value = jnp.where(at == (k ^ s), blocks[k], value)
            ref[...] = value.astype(ref.dtype)

    own, *sends = kernel(
        owners,
        "owners",
        [sds((tok_dev, out_width), F32)] + [sds((tok_dev, out_width), BF)] * (blks - 1),
        [VM, VM],
        [keep, back],
    )
    for s in reversed(range(1, blks)):
        own = own + hop(sends[s - 1], "blk", blks, s).astype(F32)
    branch = (own * keep_own).astype(BF)
    return (stream, branch)


def solution(mesh):
    size = dict(mesh.shape)
    few = size["blk"] == 4 and size["heads"] == 2 and size["rows"] == 2

    def shards(*args):
        queries, cand_lengths = args[0], args[-2]
        toks = queries.shape[0] * size["blk"]
        direct = few and toks % 16 == 0 and toks * 2 <= LEN and cand_lengths.shape[0] == 1
        return (shards_direct if direct else shards_any)(*args)

    placed = (
        P(("groups", "blk", "rows"), "heads", None),
        P(("groups", "blk"), "heads", None),
        P(("groups", "blk"), "heads", None),
        P("groups", ("blk", "rows")),
        P(("blk", "rows")),
        P("heads", ("blk", "rows")),
        P(("blk", "rows")),
        P("heads", ("blk", "rows")),
        P("heads", ("blk", "rows")),
        P(("blk", "rows"), "heads"),
        P("groups"),
        P("groups", None),
    )
    return jax.shard_map(
        shards,
        mesh=mesh,
        in_specs=placed,
        out_specs=(P("groups", ("blk", "rows")), P(("groups", "blk", "rows"), "heads")),
        check_vma=False,
    )
```

```python
import jax
import jax.numpy as jnp
from jax import lax
from jax.experimental import pallas as pl
from jax.experimental.pallas import tpu as pltpu
from jax.sharding import PartitionSpec as P

LEN = 128
EPS = 1e-06
BF = jnp.bfloat16
F32 = jnp.float32


def token_masks(cand_lengths, masked_pos, tokens):
    positions = jnp.arange(tokens, dtype=jnp.int32) % LEN
    length_tok = jnp.repeat(cand_lengths, LEN)[:tokens]
    valid_tok = positions < length_tok
    slots = jnp.arange(LEN, dtype=jnp.int32)
    masked_tok = jnp.any(masked_pos[:, :, None] == slots[None, None, :], axis=1).reshape(-1)[
        :tokens
    ]
    return (valid_tok, masked_tok)


def shards_any(
    queries,
    src_keys,
    src_values,
    dec_state,
    mask_embed,
    out_weight,
    norm_gain,
    gate_weight,
    up_weight,
    down_weight,
    cand_lengths,
    masked_pos,
):
    tok_dev, local_heads, head_size = queries.shape
    kv_local = src_keys.shape[1]
    group_size = local_heads // kv_local
    score_scale = head_size ** (-0.5)
    features = dec_state.shape[1] * lax.axis_size("blk") * lax.axis_size("rows")
    queries_all = lax.all_gather(queries, "blk", axis=0, tiled=True)
    gathered_rows = queries_all.shape[0]
    grouped = queries_all.reshape(gathered_rows, kv_local, group_size, head_size)
    scores = (
        jnp.einsum("tgjd,kgd->tgjk", grouped, src_keys, preferred_element_type=F32) * score_scale
    )
    local_peak = jnp.max(scores, axis=3)
    weights = jnp.exp(scores - local_peak[..., None])
    totals = jnp.sum(weights, axis=3)
    numerator = jnp.einsum(
        "tgjk,kgd->tgjd", weights.astype(BF), src_values, preferred_element_type=F32
    )
    highest = lax.pmax(local_peak, "blk")
    factor = jnp.exp(local_peak - highest)
    numer_own, totals_own = (
        lax.psum_scatter(
            (numerator * factor[..., None]).astype(BF), "blk", scatter_dimension=0, tiled=True
        ).astype(F32),
        lax.psum_scatter(
            (totals * factor).astype(BF), "blk", scatter_dimension=0, tiled=True
        ).astype(F32),
    )
    attn_own = (
        (numer_own / totals_own[..., None]).astype(BF).reshape(tok_dev, local_heads * head_size)
    )
    attn_all = lax.all_gather(attn_own, ("blk", "rows"), axis=0, tiled=True)
    tokens = attn_all.shape[0]
    projected = lax.psum(
        jnp.dot(attn_all, out_weight, preferred_element_type=F32).astype(BF), "heads"
    ).astype(F32)
    valid_tok, masked_tok = token_masks(cand_lengths, masked_pos, tokens)
    base_state = jnp.where(masked_tok[:, None], mask_embed[None, :], dec_state).astype(F32)
    stream_mid = base_state + projected
    squares = lax.psum(jnp.sum(stream_mid * stream_mid, axis=1), ("blk", "rows"))
    inv_rms = lax.rsqrt(squares / features + EPS)[:, None]
    normed = (stream_mid * inv_rms * norm_gain.astype(F32)).astype(BF)
    keep_mask = valid_tok.astype(F32)[:, None]
    stream = (stream_mid * keep_mask).astype(BF)
    normed_full = lax.all_gather(normed, ("blk", "rows"), axis=1, tiled=True)
    feature_width = gate_weight.shape[0]
    column_block = lax.dynamic_slice_in_dim(
        normed_full, lax.axis_index("heads") * feature_width, feature_width, 1
    )
    gate_part = jnp.dot(column_block, gate_weight, preferred_element_type=F32)
    up_part = jnp.dot(column_block, up_weight, preferred_element_type=F32)
    gate_rows, up_rows = (
        lax.psum(gate_part.astype(BF), "heads").astype(F32),
        lax.psum(up_part.astype(BF), "heads").astype(F32),
    )
    hidden = (jax.nn.gelu(gate_rows, approximate=True) * up_rows).astype(BF)
    down_out = lax.psum_scatter(
        jnp.dot(hidden, down_weight, preferred_element_type=F32),
        ("blk", "rows"),
        scatter_dimension=0,
        tiled=True,
    )
    own_start = (lax.axis_index("blk") * lax.axis_size("rows") + lax.axis_index("rows")) * tok_dev
    keep_own = lax.dynamic_slice_in_dim(keep_mask, own_start, tok_dev, 0)
    return (stream, (down_out * keep_own).astype(BF))


VM = pl.BlockSpec(memory_space=pltpu.VMEM)
ANY = pl.BlockSpec(memory_space=pl.ANY)
MIB = 1 << 20


def hop(value, axis, size, step):
    return lax.ppermute(value, axis, [(i, i ^ step) for i in range(size)])


def kernel(body, name, outs, specs, args, limit=8, flops=0, aliases=None, scratch=()):
    near = [a for a, spec in zip(args, specs) if spec is VM]
    size = sum(a.size * a.dtype.itemsize for a in near + list(outs))
    return pl.pallas_call(
        body,
        out_shape=outs,
        in_specs=specs,
        out_specs=[VM] * len(outs),
        input_output_aliases=aliases or {},
        scratch_shapes=list(scratch),
        compiler_params=pltpu.CompilerParams(vmem_limit_bytes=limit * MIB),
        cost_estimate=pl.CostEstimate(flops=flops, bytes_accessed=size, transcendentals=0),
        name=name,
    )(*args)


def fetch(after, arrays, name, rows=None, into=None):
    n, skip = len(arrays), len(after)
    begun = list(into or [])

    def body(*refs):
        sources = refs[skip : skip + n]
        targets, sems = refs[-1 - n : -1], refs[-1]
        copies = []
        for i, (source, target) in enumerate(zip(sources, targets)):
            if rows is not None and rows[i] is not None:
                source, target = source.at[pl.ds(*rows[i])], target.at[pl.ds(*rows[i])]
            copies.append(pltpu.make_async_copy(source, target, sems.at[i]))
        for copy in copies:
            copy.start()
        for copy in copies:
            copy.wait()

    size = sum(a.size * a.dtype.itemsize for a in arrays)
    return pl.pallas_call(
        body,
        out_shape=[jax.ShapeDtypeStruct(a.shape, a.dtype) for a in arrays],
        in_specs=[ANY] * (skip + n) + [VM] * len(begun),
        out_specs=[VM] * n,
        input_output_aliases={skip + n + i: i for i in range(len(begun))},
        scratch_shapes=[pltpu.SemaphoreType.DMA((n,))],
        compiler_params=pltpu.CompilerParams(vmem_limit_bytes=MIB),
        cost_estimate=pl.CostEstimate(flops=0, bytes_accessed=2 * size, transcendentals=0),
        name=name,
    )(*after, *[pltpu.with_memory_space_constraint(a, pltpu.HBM) for a in arrays], *begun)


def parts_of(value, count):
    out = []
    for _ in range(count):
        part = lax.reduce_precision(value, 8, 7)
        out.append(part.astype(BF))
        value = value - part
    return out


def split_in(value, count):
    out = []
    for _ in range(count):
        part = value.astype(BF)
        out.append(part)
        value = value - part.astype(F32)
    return out


def shards_direct(
    queries,
    src_keys,
    src_values,
    dec_state,
    mask_embed,
    out_weight,
    norm_gain,
    gate_weight,
    up_weight,
    down_weight,
    cand_lengths,
    masked_pos,
):
    blks, head_parts = lax.axis_size("blk"), lax.axis_size("heads")
    blk, head, row = (lax.axis_index(name) for name in ("blk", "heads", "rows"))
    tok_dev, local_heads, head_size = queries.shape
    kv_local = src_keys.shape[1]
    group_size = local_heads // kv_local
    score_scale = head_size ** (-0.5)
    width = dec_state.shape[1]
    features = width * blks * 2
    half = blks // head_parts
    hidden_width, out_width = gate_weight.shape[1], down_weight.shape[1]
    toks = tok_dev * blks
    tokens = toks * 2
    sds = jax.ShapeDtypeStruct

    queries_near, dec_state, mask_embed, norm_gain, masked_pos = fetch(
        [], [queries, dec_state, mask_embed, norm_gain, masked_pos], "fetch_small"
    )
    blocks = [queries_near] * blks
    for s in [blks - 1] + list(range(1, blks - 1)):
        piece = hop(queries, "blk", blks, s)
        blocks = [jnp.where(blk == (k ^ s), piece, block) for k, block in enumerate(blocks)]
        blocks = list(lax.optimization_barrier(tuple(blocks)))
    q_all = jnp.concatenate(blocks, axis=0)
    grouped = q_all.reshape(toks, kv_local, group_size, head_size)
    scores = (
        jnp.einsum("tgjd,kgd->tgjk", grouped, src_keys, preferred_element_type=F32) * score_scale
    )
    peak = jnp.max(scores, axis=3)
    weights = jnp.exp(scores - peak[..., None])
    totals = jnp.sum(weights, axis=3)
    numerator = jnp.einsum(
        "tgjk,kgd->tgjd", weights.astype(BF), src_values, preferred_element_type=F32
    )
    partial = (numerator / totals[..., None]).astype(BF)
    partial = partial.transpose(1, 2, 0, 3).reshape(local_heads * toks, head_size)
    partial, peak, totals = lax.optimization_barrier((partial, peak, totals))
    level = (peak + jnp.log(totals)).reshape(toks, local_heads)
    side = jnp.concatenate(parts_of(level, 3), axis=1)
    side = jnp.pad(side, ((0, 0), (0, head_size - side.shape[1])))
    note = jnp.concatenate([partial, side], axis=0)
    notes = [note] + [hop(note, "blk", blks, s) for s in reversed(range(1, blks))]
    gate_cut = gate_weight.shape[0] * 2 // 48 * 16
    proj_near, gate_near = fetch(
        [note], [out_weight.T, gate_weight], "fetch_proj_gate", rows=[None, (0, gate_cut)]
    )

    def combine(*refs):
        ins, out = refs[:blks], refs[blks + 2]
        base = local_heads * toks
        levels = []
        for ref in ins:
            side = ref[base : base + toks, :].astype(F32)
            levels.append(
                side[:, :local_heads]
                + side[:, local_heads : 2 * local_heads]
                + side[:, 2 * local_heads : 3 * local_heads]
            )
        top = levels[0]
        for one in levels[1:]:
            top = jnp.maximum(top, one)
        shares = [jnp.exp(one - top) for one in levels]
        total = shares[0]
        for one in shares[1:]:
            total = total + one
        shares = [one / total for one in shares]
        for h in range(local_heads):
            acc = None
            for share, ref in zip(shares, ins):
                term = share[:, h : h + 1] * ref[h * toks : (h + 1) * toks, :].astype(F32)
                acc = term if acc is None else acc + term
            out[:, h * head_size : (h + 1) * head_size] = acc.astype(BF)

    attn, proj_near, gate_near = kernel(
        combine,
        "combine",
        [sds((toks, local_heads * head_size), BF), sds(proj_near.shape, BF), sds(gate_near.shape, BF)],
        [VM] * (blks + 2),
        notes + [proj_near, gate_near],
        aliases={blks: 1, blks + 1: 2},
    )
    other = hop(attn, "rows", 2, 1)
    across = (((1,), (1,)), ((), ()))

    def project_own(own_ref, weight_ref, gate_ref, out_ref, gate_out):
        out_ref[...] = lax.dot_general(
            own_ref[...], weight_ref[...], across, preferred_element_type=F32
        )

    proj_own, gate_near = kernel(
        project_own,
        "project_own",
        [sds((toks, width), F32), sds(gate_near.shape, BF)],
        [VM] * 3,
        [attn, proj_near, gate_near],
        aliases={2: 1},
    )

    def project(own_ref, other_ref, weight_ref, gate_ref, out_ref, gate_out):
        first = lax.axis_index("rows") == 0
        own = own_ref[...]
        other = lax.dot_general(
            other_ref[...], weight_ref[...], across, preferred_element_type=F32
        )
        out_ref[:toks] = jnp.where(first, own, other).astype(BF)
        out_ref[toks:] = jnp.where(first, other, own).astype(BF)

    proj, gate_near = kernel(
        project,
        "project",
        [sds((tokens, width), BF), sds(gate_near.shape, BF)],
        [VM] * 4,
        [proj_own, other, proj_near, gate_near],
        aliases={3: 1},
    )
    proj_other = hop(proj, "heads", 2, 1)
    (gate_near,) = fetch(
        [proj],
        [gate_weight],
        "fetch_gate_last",
        rows=[(gate_cut, gate_weight.shape[0] - gate_cut)],
        into=[gate_near],
    )

    lanes = -(-(width + 2) // 128) * 128

    inner = [b * 2 + r for r in range(2) for b in range(blks)]
    outer = [r * blks + b for b in range(blks) for r in range(2)]

    def shuffled(value, order, scratch):
        for at, k in enumerate(order):
            scratch[at * tok_dev : (at + 1) * tok_dev] = value[k * tok_dev : (k + 1) * tok_dev]
        return scratch[...]

    def middle(
        dec_ref,
        embed_ref,
        gain_ref,
        masked_ref,
        own_ref,
        other_ref,
        gate_ref,
        mid_ref,
        note_ref,
        gate_out,
        base_ref,
    ):
        slots = lax.broadcasted_iota(jnp.int32, (tokens, 1), 0)
        hits = jnp.where(slots == masked_ref[...], 1.0, 0.0)
        masked = jnp.max(hits, axis=1, keepdims=True) > 0.0
        base = jnp.where(masked, embed_ref[...].astype(F32), dec_ref[...].astype(F32))
        mid = shuffled(base, inner, base_ref) + (
            own_ref[...].astype(F32) + other_ref[...].astype(F32)
        )
        mid_ref[...] = mid
        note_ref[:, :width] = (mid * gain_ref[...].astype(F32)).astype(BF)
        squares = jnp.sum(mid * mid, axis=1, keepdims=True)
        high, low = split_in(squares, 2)
        lane = lax.broadcasted_iota(jnp.int32, (tokens, lanes - width), 1)
        note_ref[:, width:] = jnp.where(
            lane == 0, high.astype(F32), jnp.where(lane == 1, low.astype(F32), 0.0)
        ).astype(BF)

    mid, note, gate_near = kernel(
        middle,
        "middle",
        [
            sds((tokens, width), F32),
            sds((tokens, lanes), BF),
            sds(gate_near.shape, BF),
        ],
        [VM] * 7,
        [
            dec_state,
            mask_embed[None, :],
            norm_gain[None, :],
            masked_pos,
            proj,
            proj_other,
            gate_near,
        ],
        aliases={6: 2},
        scratch=[pltpu.VMEM((tokens, width), F32)],
    )

    def residual(mid_ref, length_ref, stream_ref, keep_ref, order_ref):
        slots = lax.broadcasted_iota(jnp.int32, (tokens, 1), 0)
        keep = jnp.where(slots < length_ref[...], 1.0, 0.0)
        stream_ref[...] = (shuffled(mid_ref[...], outer, order_ref) * keep).astype(BF)
        first = (lax.axis_index("blk") * 2 + lax.axis_index("rows")) * tok_dev
        owned = first + lax.broadcasted_iota(jnp.int32, (tok_dev, 1), 0)
        keep_ref[...] = jnp.where(owned < length_ref[...], 1.0, 0.0)

    stream, keep_own = kernel(
        residual,
        "residual",
        [sds((tokens, width), BF), sds((tok_dev, 1), F32)],
        [VM] * 2,
        [mid, cand_lengths[None, :]],
        scratch=[pltpu.VMEM((tokens, width), F32)],
    )

    far_pairs, near_pairs = [], []
    for b in range(blks):
        for h in range(head_parts):
            far_pairs.append((b * head_parts + h, (b ^ 3) * head_parts + h))
            to = (b ^ 1, h) if b // half == h else (b ^ 2, 1 - h)
            near_pairs.append((b * head_parts + h, to[0] * head_parts + to[1]))
    near = lax.ppermute(note, ("blk", "heads"), near_pairs)
    far = lax.ppermute(note, ("blk", "heads"), far_pairs)
    (up_near,) = fetch([note], [up_weight], "fetch_up")
    lanes_all = note.shape[1]

    def pick(own_ref, far_ref, near_ref, gate_ref, up_ref, out_ref):
        at = lax.axis_index("blk")
        inside = at // half == lax.axis_index("heads")
        odd = at % 2 == 1
        same = jnp.where(inside, own_ref[...], near_ref[...])
        pair = jnp.where(inside, near_ref[...], far_ref[...])
        out_ref[0] = jnp.where(odd, pair, same)
        out_ref[1] = jnp.where(odd, same, pair)

    (mine,) = kernel(
        pick,
        "pick",
        [sds((half, tokens, lanes_all), BF)],
        [VM, VM, VM, ANY, ANY],
        [note, far, near, gate_near, up_near],
    )
    theirs = hop(mine, "rows", 2, 1)
    rows_in = gate_weight.shape[0]

    def tile_products(tiles_ref, weight_ref, row_at):
        total = None
        for k in range(half):
            start = pl.multiple_of((k * 2 + row_at) * width, 16)
            term = jnp.dot(
                tiles_ref[k, :, :width],
                weight_ref[pl.ds(start, width), :],
                preferred_element_type=F32,
            )
            total = term if total is None else total + term
        return total

    def inner_products(mine_ref, gate_ref, up_ref, gate_out, up_out):
        gate_out[...] = tile_products(mine_ref, gate_ref, lax.axis_index("rows"))
        up_out[...] = tile_products(mine_ref, up_ref, lax.axis_index("rows"))

    gate_own, up_own = kernel(
        inner_products,
        "inner_products",
        [sds((tokens, hidden_width), F32)] * 2,
        [VM, VM, VM],
        [mine, gate_near, up_near],
        flops=2 * tokens * rows_in * hidden_width,
    )

    cut = -(-hidden_width // 512) * 256
    pieces_at = [(0, cut), (cut, hidden_width)]

    def gate_up(lo, hi, with_squares):
        span = hi - lo

        def body(*refs):
            theirs_ref, gate_in, up_in, gate_w, up_w = refs[:5]
            out_ref, note_ref = refs[-2:]
            row_at = 1 - lax.axis_index("rows")
            for k, (own, weight) in enumerate(((gate_in, gate_w), (up_in, up_w))):
                value = own[:, lo:hi] + tile_products(theirs_ref, weight.at[:, lo:hi], row_at)
                out_ref[:, k * span : (k + 1) * span] = value
                note_ref[:, k * span : (k + 1) * span] = value.astype(BF)
            if with_squares:
                squares = None
                for k in range(half):
                    for ref in (refs[5], theirs_ref):
                        here = ref[k, :, width : width + 2].astype(F32)
                        squares = here if squares is None else squares + here
                squares = squares[:, 0:1] + squares[:, 1:2]
                high, low = split_in(squares, 2)
                lane = lax.broadcasted_iota(jnp.int32, (tokens, 128), 1)
                out_ref[:, 2 * span :] = jnp.where(lane == 0, squares, 0.0)
                note_ref[:, 2 * span :] = jnp.where(
                    lane == 0, high.astype(F32), jnp.where(lane == 1, low.astype(F32), 0.0)
                ).astype(BF)

        return body

    sums, sum_notes = [], []
    for c, (lo, hi) in enumerate(pieces_at):
        operands = [theirs, gate_own, up_own, gate_near, up_near] + [mine] * (c == 0)
        long_width = 2 * (hi - lo) + 128 * (c == 0)
        value, value_note = kernel(
            gate_up(lo, hi, c == 0),
            f"gate_up_{c}",
            [sds((tokens, long_width), F32), sds((tokens, long_width), BF)],
            [VM] * len(operands),
            operands,
            flops=tokens * rows_in * hidden_width,
        )
        sums.append(value)
        sum_notes.append(value_note)
    sum_others = [hop(value, "heads", 2, 1) for value in sum_notes]
    (down_near,) = fetch([sum_notes[-1]], [down_weight], "fetch_down")

    def down_piece(c, own_ref, other_ref, first_ref, first_other_ref, weight_ref):
        lo, hi = pieces_at[c]
        span, at = hi - lo, 2 * cut
        other = first_other_ref[:, at:].astype(F32)
        squares = first_ref[:, at : at + 1] + other[:, 0:1] + other[:, 1:2]
        inv_rms = lax.rsqrt(squares / features + EPS)
        gate, up = [
            (
                own_ref[:, k * span : (k + 1) * span]
                + other_ref[:, k * span : (k + 1) * span].astype(F32)
            )
            * inv_rms
            for k in range(2)
        ]
        hidden = (jax.nn.gelu(gate, approximate=True) * up).astype(BF)
        return jnp.dot(hidden, weight_ref[lo:hi, :], preferred_element_type=F32)

    def down_first(own_ref, other_ref, weight_ref, out_ref):
        out_ref[...] = down_piece(0, own_ref, other_ref, own_ref, other_ref, weight_ref)

    (down_part,) = kernel(
        down_first,
        "down_first",
        [sds((tokens, out_width), F32)],
        [VM] * 3,
        [sums[0], sum_others[0], down_near],
        flops=tokens * hidden_width * out_width,
    )

    def down_last(
        own_ref, other_ref, first_ref, first_other_ref, part_ref, weight_ref, keep_ref, away_ref
    ):
        down = part_ref[...] + down_piece(
            1, own_ref, other_ref, first_ref, first_other_ref, weight_ref
        )
        first = lax.axis_index("rows") == 0
        keep_ref[...] = jnp.where(first, down[:toks], down[toks:])
        away_ref[...] = jnp.where(first, down[toks:], down[:toks]).astype(BF)

    keep, away = kernel(
        down_last,
        "down_last",
        [sds((toks, out_width), F32), sds((toks, out_width), BF)],
        [VM] * 6,
        [sums[1], sum_others[1], sums[0], sum_others[0], down_part, down_near],
        limit=12,
    )
    back = hop(away, "rows", 2, 1)

    def owners(keep_ref, back_ref, own_ref, *piece_refs):
        total = keep_ref[...] + back_ref[...].astype(F32)
        blocks = [total[k * tok_dev : (k + 1) * tok_dev] for k in range(blks)]
        at = lax.axis_index("blk")
        for s, ref in enumerate((own_ref,) + piece_refs):
            value = blocks[0]
            for k in range(1, blks):
                value = jnp.where(at == (k ^ s), blocks[k], value)
            ref[...] = value.astype(ref.dtype)

    own, *sends = kernel(
        owners,
        "owners",
        [sds((tok_dev, out_width), F32)] + [sds((tok_dev, out_width), BF)] * (blks - 1),
        [VM, VM],
        [keep, back],
    )
    for s in range(1, blks):
        own = own + hop(sends[s - 1], "blk", blks, s).astype(F32)
    branch = (own * keep_own).astype(BF)
    return (stream, branch)


def solution(mesh):
    size = dict(mesh.shape)
    few = size["blk"] == 4 and size["heads"] == 2 and size["rows"] == 2

    def shards(*args):
        queries, cand_lengths = args[0], args[-2]
        toks = queries.shape[0] * size["blk"]
        direct = few and toks % 16 == 0 and toks * 2 <= LEN and cand_lengths.shape[0] == 1
        return (shards_direct if direct else shards_any)(*args)

    placed = (
        P(("groups", "blk", "rows"), "heads", None),
        P(("groups", "blk"), "heads", None),
        P(("groups", "blk"), "heads", None),
        P("groups", ("blk", "rows")),
        P(("blk", "rows")),
        P("heads", ("blk", "rows")),
        P(("blk", "rows")),
        P("heads", ("blk", "rows")),
        P("heads", ("blk", "rows")),
        P(("blk", "rows"), "heads"),
        P("groups"),
        P("groups", None),
    )
    return jax.shard_map(
        shards,
        mesh=mesh,
        in_specs=placed,
        out_specs=(P("groups", ("blk", "rows")), P(("groups", "blk", "rows"), "heads")),
        check_vma=False,
    )
```

```python
import jax
import jax.numpy as jnp
from jax import lax
from jax.experimental import pallas as pl
from jax.experimental.pallas import tpu as pltpu
from jax.sharding import PartitionSpec as P

LEN = 128
EPS = 1e-06
BF = jnp.bfloat16
F32 = jnp.float32


def token_masks(cand_lengths, masked_pos, tokens):
    positions = jnp.arange(tokens, dtype=jnp.int32) % LEN
    length_tok = jnp.repeat(cand_lengths, LEN)[:tokens]
    valid_tok = positions < length_tok
    slots = jnp.arange(LEN, dtype=jnp.int32)
    masked_tok = jnp.any(masked_pos[:, :, None] == slots[None, None, :], axis=1).reshape(-1)[
        :tokens
    ]
    return (valid_tok, masked_tok)


def shards_any(
    queries,
    src_keys,
    src_values,
    dec_state,
    mask_embed,
    out_weight,
    norm_gain,
    gate_weight,
    up_weight,
    down_weight,
    cand_lengths,
    masked_pos,
):
    tok_dev, local_heads, head_size = queries.shape
    kv_local = src_keys.shape[1]
    group_size = local_heads // kv_local
    score_scale = head_size ** (-0.5)
    features = dec_state.shape[1] * lax.axis_size("blk") * lax.axis_size("rows")
    queries_all = lax.all_gather(queries, "blk", axis=0, tiled=True)
    gathered_rows = queries_all.shape[0]
    grouped = queries_all.reshape(gathered_rows, kv_local, group_size, head_size)
    scores = (
        jnp.einsum("tgjd,kgd->tgjk", grouped, src_keys, preferred_element_type=F32) * score_scale
    )
    local_peak = jnp.max(scores, axis=3)
    weights = jnp.exp(scores - local_peak[..., None])
    totals = jnp.sum(weights, axis=3)
    numerator = jnp.einsum(
        "tgjk,kgd->tgjd", weights.astype(BF), src_values, preferred_element_type=F32
    )
    highest = lax.pmax(local_peak, "blk")
    factor = jnp.exp(local_peak - highest)
    numer_own, totals_own = (
        lax.psum_scatter(
            (numerator * factor[..., None]).astype(BF), "blk", scatter_dimension=0, tiled=True
        ).astype(F32),
        lax.psum_scatter(
            (totals * factor).astype(BF), "blk", scatter_dimension=0, tiled=True
        ).astype(F32),
    )
    attn_own = (
        (numer_own / totals_own[..., None]).astype(BF).reshape(tok_dev, local_heads * head_size)
    )
    attn_all = lax.all_gather(attn_own, ("blk", "rows"), axis=0, tiled=True)
    tokens = attn_all.shape[0]
    projected = lax.psum(
        jnp.dot(attn_all, out_weight, preferred_element_type=F32).astype(BF), "heads"
    ).astype(F32)
    valid_tok, masked_tok = token_masks(cand_lengths, masked_pos, tokens)
    base_state = jnp.where(masked_tok[:, None], mask_embed[None, :], dec_state).astype(F32)
    stream_mid = base_state + projected
    squares = lax.psum(jnp.sum(stream_mid * stream_mid, axis=1), ("blk", "rows"))
    inv_rms = lax.rsqrt(squares / features + EPS)[:, None]
    normed = (stream_mid * inv_rms * norm_gain.astype(F32)).astype(BF)
    keep_mask = valid_tok.astype(F32)[:, None]
    stream = (stream_mid * keep_mask).astype(BF)
    normed_full = lax.all_gather(normed, ("blk", "rows"), axis=1, tiled=True)
    feature_width = gate_weight.shape[0]
    column_block = lax.dynamic_slice_in_dim(
        normed_full, lax.axis_index("heads") * feature_width, feature_width, 1
    )
    gate_part = jnp.dot(column_block, gate_weight, preferred_element_type=F32)
    up_part = jnp.dot(column_block, up_weight, preferred_element_type=F32)
    gate_rows, up_rows = (
        lax.psum(gate_part.astype(BF), "heads").astype(F32),
        lax.psum(up_part.astype(BF), "heads").astype(F32),
    )
    hidden = (jax.nn.gelu(gate_rows, approximate=True) * up_rows).astype(BF)
    down_out = lax.psum_scatter(
        jnp.dot(hidden, down_weight, preferred_element_type=F32),
        ("blk", "rows"),
        scatter_dimension=0,
        tiled=True,
    )
    own_start = (lax.axis_index("blk") * lax.axis_size("rows") + lax.axis_index("rows")) * tok_dev
    keep_own = lax.dynamic_slice_in_dim(keep_mask, own_start, tok_dev, 0)
    return (stream, (down_out * keep_own).astype(BF))


VM = pl.BlockSpec(memory_space=pltpu.VMEM)
ANY = pl.BlockSpec(memory_space=pl.ANY)
MIB = 1 << 20


def hop(value, axis, size, step):
    return lax.ppermute(value, axis, [(i, i ^ step) for i in range(size)])


def kernel(body, name, outs, specs, args, limit=8, flops=0, aliases=None, scratch=()):
    near = [a for a, spec in zip(args, specs) if spec is VM]
    size = sum(a.size * a.dtype.itemsize for a in near + list(outs))
    return pl.pallas_call(
        body,
        out_shape=outs,
        in_specs=specs,
        out_specs=[VM] * len(outs),
        input_output_aliases=aliases or {},
        scratch_shapes=list(scratch),
        compiler_params=pltpu.CompilerParams(vmem_limit_bytes=limit * MIB),
        cost_estimate=pl.CostEstimate(flops=flops, bytes_accessed=size, transcendentals=0),
        name=name,
    )(*args)


def fetch(after, arrays, name, rows=None, into=None):
    n, skip = len(arrays), len(after)
    begun = list(into or [])

    def body(*refs):
        sources = refs[skip : skip + n]
        targets, sems = refs[-1 - n : -1], refs[-1]
        copies = []
        for i, (source, target) in enumerate(zip(sources, targets)):
            if rows is not None and rows[i] is not None:
                source, target = source.at[pl.ds(*rows[i])], target.at[pl.ds(*rows[i])]
            copies.append(pltpu.make_async_copy(source, target, sems.at[i]))
        for copy in copies:
            copy.start()
        for copy in copies:
            copy.wait()

    size = sum(a.size * a.dtype.itemsize for a in arrays)
    return pl.pallas_call(
        body,
        out_shape=[jax.ShapeDtypeStruct(a.shape, a.dtype) for a in arrays],
        in_specs=[ANY] * (skip + n) + [VM] * len(begun),
        out_specs=[VM] * n,
        input_output_aliases={skip + n + i: i for i in range(len(begun))},
        scratch_shapes=[pltpu.SemaphoreType.DMA((n,))],
        compiler_params=pltpu.CompilerParams(vmem_limit_bytes=MIB),
        cost_estimate=pl.CostEstimate(flops=0, bytes_accessed=2 * size, transcendentals=0),
        name=name,
    )(*after, *[pltpu.with_memory_space_constraint(a, pltpu.HBM) for a in arrays], *begun)


def parts_of(value, count):
    out = []
    for _ in range(count):
        part = lax.reduce_precision(value, 8, 7)
        out.append(part.astype(BF))
        value = value - part
    return out


def split_in(value, count):
    out = []
    for _ in range(count):
        part = value.astype(BF)
        out.append(part)
        value = value - part.astype(F32)
    return out


def shards_direct(
    queries,
    src_keys,
    src_values,
    dec_state,
    mask_embed,
    out_weight,
    norm_gain,
    gate_weight,
    up_weight,
    down_weight,
    cand_lengths,
    masked_pos,
):
    blks, head_parts = lax.axis_size("blk"), lax.axis_size("heads")
    blk, head, row = (lax.axis_index(name) for name in ("blk", "heads", "rows"))
    tok_dev, local_heads, head_size = queries.shape
    kv_local = src_keys.shape[1]
    group_size = local_heads // kv_local
    score_scale = head_size ** (-0.5)
    width = dec_state.shape[1]
    features = width * blks * 2
    half = blks // head_parts
    hidden_width, out_width = gate_weight.shape[1], down_weight.shape[1]
    toks = tok_dev * blks
    tokens = toks * 2
    sds = jax.ShapeDtypeStruct

    queries_near, dec_state, mask_embed, norm_gain, masked_pos = fetch(
        [], [queries, dec_state, mask_embed, norm_gain, masked_pos], "fetch_small"
    )
    blocks = [queries_near] * blks
    for s in [blks - 1] + list(range(1, blks - 1)):
        piece = hop(queries, "blk", blks, s)
        blocks = [jnp.where(blk == (k ^ s), piece, block) for k, block in enumerate(blocks)]
        blocks = list(lax.optimization_barrier(tuple(blocks)))
    q_all = jnp.concatenate(blocks, axis=0)
    grouped = q_all.reshape(toks, kv_local, group_size, head_size)
    scores = (
        jnp.einsum("tgjd,kgd->tgjk", grouped, src_keys, preferred_element_type=F32) * score_scale
    )
    peak = jnp.max(scores, axis=3)
    weights = jnp.exp(scores - peak[..., None])
    totals = jnp.sum(weights, axis=3)
    numerator = jnp.einsum(
        "tgjk,kgd->tgjd", weights.astype(BF), src_values, preferred_element_type=F32
    )
    partial = (numerator / totals[..., None]).astype(BF)
    partial = partial.transpose(1, 2, 0, 3).reshape(local_heads * toks, head_size)
    partial, peak, totals = lax.optimization_barrier((partial, peak, totals))
    level = (peak + jnp.log(totals)).reshape(toks, local_heads)
    side = jnp.concatenate(parts_of(level, 3), axis=1)
    side = jnp.pad(side, ((0, 0), (0, head_size - side.shape[1])))
    note = jnp.concatenate([partial, side], axis=0)
    notes = [note] + [hop(note, "blk", blks, s) for s in reversed(range(1, blks))]
    gate_cut = gate_weight.shape[0] * 2 // 48 * 16
    proj_near, gate_near = fetch(
        [note], [out_weight.T, gate_weight], "fetch_proj_gate", rows=[None, (0, gate_cut)]
    )

    def combine(*refs):
        ins, out = refs[:blks], refs[blks + 2]
        base = local_heads * toks
        levels = []
        for ref in ins:
            side = ref[base : base + toks, :].astype(F32)
            levels.append(
                side[:, :local_heads]
                + side[:, local_heads : 2 * local_heads]
                + side[:, 2 * local_heads : 3 * local_heads]
            )
        top = levels[0]
        for one in levels[1:]:
            top = jnp.maximum(top, one)
        shares = [jnp.exp(one - top) for one in levels]
        total = shares[0]
        for one in shares[1:]:
            total = total + one
        shares = [one / total for one in shares]
        for h in range(local_heads):
            acc = None
            for share, ref in zip(shares, ins):
                term = share[:, h : h + 1] * ref[h * toks : (h + 1) * toks, :].astype(F32)
                acc = term if acc is None else acc + term
            out[:, h * head_size : (h + 1) * head_size] = acc.astype(BF)

    attn, proj_near, gate_near = kernel(
        combine,
        "combine",
        [sds((toks, local_heads * head_size), BF), sds(proj_near.shape, BF), sds(gate_near.shape, BF)],
        [VM] * (blks + 2),
        notes + [proj_near, gate_near],
        aliases={blks: 1, blks + 1: 2},
    )
    other = hop(attn, "rows", 2, 1)
    across = (((1,), (1,)), ((), ()))

    def project_own(own_ref, weight_ref, gate_ref, out_ref, gate_out):
        out_ref[...] = lax.dot_general(
            own_ref[...], weight_ref[...], across, preferred_element_type=F32
        )

    proj_own, gate_near = kernel(
        project_own,
        "project_own",
        [sds((toks, width), F32), sds(gate_near.shape, BF)],
        [VM] * 3,
        [attn, proj_near, gate_near],
        aliases={2: 1},
    )

    def project(own_ref, other_ref, weight_ref, gate_ref, out_ref, gate_out):
        first = lax.axis_index("rows") == 0
        own = own_ref[...]
        other = lax.dot_general(
            other_ref[...], weight_ref[...], across, preferred_element_type=F32
        )
        out_ref[:toks] = jnp.where(first, own, other).astype(BF)
        out_ref[toks:] = jnp.where(first, other, own).astype(BF)

    proj, gate_near = kernel(
        project,
        "project",
        [sds((tokens, width), BF), sds(gate_near.shape, BF)],
        [VM] * 4,
        [proj_own, other, proj_near, gate_near],
        aliases={3: 1},
    )
    proj_other = hop(proj, "heads", 2, 1)
    (gate_near,) = fetch(
        [proj],
        [gate_weight],
        "fetch_gate_last",
        rows=[(gate_cut, gate_weight.shape[0] - gate_cut)],
        into=[gate_near],
    )

    lanes = -(-(width + 2) // 128) * 128

    inner = [b * 2 + r for r in range(2) for b in range(blks)]
    outer = [r * blks + b for b in range(blks) for r in range(2)]

    def shuffled(value, order, scratch):
        for at, k in enumerate(order):
            scratch[at * tok_dev : (at + 1) * tok_dev] = value[k * tok_dev : (k + 1) * tok_dev]
        return scratch[...]

    def middle(
        dec_ref,
        embed_ref,
        gain_ref,
        masked_ref,
        own_ref,
        other_ref,
        gate_ref,
        mid_ref,
        note_ref,
        gate_out,
        base_ref,
    ):
        slots = lax.broadcasted_iota(jnp.int32, (tokens, 1), 0)
        hits = jnp.where(slots == masked_ref[...], 1.0, 0.0)
        masked = jnp.max(hits, axis=1, keepdims=True) > 0.0
        base = jnp.where(masked, embed_ref[...].astype(F32), dec_ref[...].astype(F32))
        mid = shuffled(base, inner, base_ref) + (
            own_ref[...].astype(F32) + other_ref[...].astype(F32)
        )
        mid_ref[...] = mid
        note_ref[:, :width] = (mid * gain_ref[...].astype(F32)).astype(BF)
        squares = jnp.sum(mid * mid, axis=1, keepdims=True)
        high, low = split_in(squares, 2)
        lane = lax.broadcasted_iota(jnp.int32, (tokens, lanes - width), 1)
        note_ref[:, width:] = jnp.where(
            lane == 0, high.astype(F32), jnp.where(lane == 1, low.astype(F32), 0.0)
        ).astype(BF)

    mid, note, gate_near = kernel(
        middle,
        "middle",
        [
            sds((tokens, width), F32),
            sds((tokens, lanes), BF),
            sds(gate_near.shape, BF),
        ],
        [VM] * 7,
        [
            dec_state,
            mask_embed[None, :],
            norm_gain[None, :],
            masked_pos,
            proj,
            proj_other,
            gate_near,
        ],
        aliases={6: 2},
        scratch=[pltpu.VMEM((tokens, width), F32)],
    )

    def residual(mid_ref, length_ref, stream_ref, keep_ref, order_ref):
        slots = lax.broadcasted_iota(jnp.int32, (tokens, 1), 0)
        keep = jnp.where(slots < length_ref[...], 1.0, 0.0)
        stream_ref[...] = (shuffled(mid_ref[...], outer, order_ref) * keep).astype(BF)
        first = (lax.axis_index("blk") * 2 + lax.axis_index("rows")) * tok_dev
        owned = first + lax.broadcasted_iota(jnp.int32, (tok_dev, 1), 0)
        keep_ref[...] = jnp.where(owned < length_ref[...], 1.0, 0.0)

    stream, keep_own = kernel(
        residual,
        "residual",
        [sds((tokens, width), BF), sds((tok_dev, 1), F32)],
        [VM] * 2,
        [mid, cand_lengths[None, :]],
        scratch=[pltpu.VMEM((tokens, width), F32)],
    )

    far_pairs, near_pairs = [], []
    for b in range(blks):
        for h in range(head_parts):
            far_pairs.append((b * head_parts + h, (b ^ 3) * head_parts + h))
            to = (b ^ 2, h) if b // half == h else (b ^ 1, 1 - h)
            near_pairs.append((b * head_parts + h, to[0] * head_parts + to[1]))
    near = lax.ppermute(note, ("blk", "heads"), near_pairs)
    far = lax.ppermute(note, ("blk", "heads"), far_pairs)
    (up_near,) = fetch([note], [up_weight], "fetch_up")
    lanes_all = note.shape[1]

    def pick(own_ref, near_ref, far_ref, gate_ref, up_ref, kept_ref, out_ref):
        at = lax.axis_index("blk")
        inside = at // half == lax.axis_index("heads")
        odd = at % 2 == 1
        same = jnp.where(inside, own_ref[...], near_ref[...])
        pair = jnp.where(inside, near_ref[...], far_ref[...])
        out_ref[0] = jnp.where(odd, pair, same)
        out_ref[1] = jnp.where(odd, same, pair)

    (mine,) = kernel(
        pick,
        "pick",
        [sds((half, tokens, lanes_all), BF)],
        [VM, VM, VM, ANY, ANY, ANY],
        [note, near, far, gate_near, up_near, keep_own],
    )
    theirs = hop(mine, "rows", 2, 1)
    rows_in = gate_weight.shape[0]

    def tile_products(tiles_ref, weight_ref, row_at):
        total = None
        for k in range(half):
            start = pl.multiple_of((k * 2 + row_at) * width, 16)
            term = jnp.dot(
                tiles_ref[k, :, :width],
                weight_ref[pl.ds(start, width), :],
                preferred_element_type=F32,
            )
            total = term if total is None else total + term
        return total

    def inner_products(mine_ref, gate_ref, up_ref, gate_out, up_out):
        gate_out[...] = tile_products(mine_ref, gate_ref, lax.axis_index("rows"))
        up_out[...] = tile_products(mine_ref, up_ref, lax.axis_index("rows"))

    gate_own, up_own = kernel(
        inner_products,
        "inner_products",
        [sds((tokens, hidden_width), F32)] * 2,
        [VM, VM, VM],
        [mine, gate_near, up_near],
        flops=2 * tokens * rows_in * hidden_width,
    )

    cut = -(-hidden_width // 512) * 256
    pieces_at = [(0, cut), (cut, hidden_width)]

    def gate_up(lo, hi, with_squares):
        span = hi - lo

        def body(*refs):
            theirs_ref, gate_in, up_in, gate_w, up_w = refs[:5]
            out_ref, note_ref = refs[-2:]
            row_at = 1 - lax.axis_index("rows")
            for k, (own, weight) in enumerate(((gate_in, gate_w), (up_in, up_w))):
                value = own[:, lo:hi] + tile_products(theirs_ref, weight.at[:, lo:hi], row_at)
                out_ref[:, k * span : (k + 1) * span] = value
                note_ref[:, k * span : (k + 1) * span] = value.astype(BF)
            if with_squares:
                squares = None
                for k in range(half):
                    for ref in (refs[5], theirs_ref):
                        here = ref[k, :, width : width + 2].astype(F32)
                        squares = here if squares is None else squares + here
                squares = squares[:, 0:1] + squares[:, 1:2]
                high, low = split_in(squares, 2)
                lane = lax.broadcasted_iota(jnp.int32, (tokens, 128), 1)
                out_ref[:, 2 * span :] = jnp.where(lane == 0, squares, 0.0)
                note_ref[:, 2 * span :] = jnp.where(
                    lane == 0, high.astype(F32), jnp.where(lane == 1, low.astype(F32), 0.0)
                ).astype(BF)

        return body

    sums, sum_notes = [], []
    for c, (lo, hi) in enumerate(pieces_at):
        operands = [theirs, gate_own, up_own, gate_near, up_near] + [mine] * (c == 0)
        long_width = 2 * (hi - lo) + 128 * (c == 0)
        value, value_note = kernel(
            gate_up(lo, hi, c == 0),
            f"gate_up_{c}",
            [sds((tokens, long_width), F32), sds((tokens, long_width), BF)],
            [VM] * len(operands),
            operands,
            flops=tokens * rows_in * hidden_width,
        )
        sums.append(value)
        sum_notes.append(value_note)
    sum_others = [hop(value, "heads", 2, 1) for value in sum_notes]
    (down_near,) = fetch([sum_notes[-1]], [down_weight], "fetch_down")

    def down_piece(c, own_ref, other_ref, first_ref, first_other_ref, weight_ref):
        lo, hi = pieces_at[c]
        span, at = hi - lo, 2 * cut
        other = first_other_ref[:, at:].astype(F32)
        squares = first_ref[:, at : at + 1] + other[:, 0:1] + other[:, 1:2]
        inv_rms = lax.rsqrt(squares / features + EPS)
        gate, up = [
            (
                own_ref[:, k * span : (k + 1) * span]
                + other_ref[:, k * span : (k + 1) * span].astype(F32)
            )
            * inv_rms
            for k in range(2)
        ]
        hidden = (jax.nn.gelu(gate, approximate=True) * up).astype(BF)
        return jnp.dot(hidden, weight_ref[lo:hi, :], preferred_element_type=F32)

    def down_first(own_ref, other_ref, weight_ref, out_ref):
        out_ref[...] = down_piece(0, own_ref, other_ref, own_ref, other_ref, weight_ref)

    (down_part,) = kernel(
        down_first,
        "down_first",
        [sds((tokens, out_width), F32)],
        [VM] * 3,
        [sums[0], sum_others[0], down_near],
        flops=tokens * hidden_width * out_width,
    )

    def down_last(
        own_ref, other_ref, first_ref, first_other_ref, part_ref, weight_ref, keep_ref, away_ref
    ):
        down = part_ref[...] + down_piece(
            1, own_ref, other_ref, first_ref, first_other_ref, weight_ref
        )
        first = lax.axis_index("rows") == 0
        keep_ref[...] = jnp.where(first, down[:toks], down[toks:])
        away_ref[...] = jnp.where(first, down[toks:], down[:toks]).astype(BF)

    keep, away = kernel(
        down_last,
        "down_last",
        [sds((toks, out_width), F32), sds((toks, out_width), BF)],
        [VM] * 6,
        [sums[1], sum_others[1], sums[0], sum_others[0], down_part, down_near],
        limit=12,
    )
    back = hop(away, "rows", 2, 1)

    def owners(keep_ref, back_ref, own_ref, *piece_refs):
        total = keep_ref[...] + back_ref[...].astype(F32)
        blocks = [total[k * tok_dev : (k + 1) * tok_dev] for k in range(blks)]
        at = lax.axis_index("blk")
        for s, ref in enumerate((own_ref,) + piece_refs):
            value = blocks[0]
            for k in range(1, blks):
                value = jnp.where(at == (k ^ s), blocks[k], value)
            ref[...] = value.astype(ref.dtype)

    own, *sends = kernel(
        owners,
        "owners",
        [sds((tok_dev, out_width), F32)] + [sds((tok_dev, out_width), BF)] * (blks - 1),
        [VM, VM],
        [keep, back],
    )
    for s in range(1, blks):
        own = own + hop(sends[s - 1], "blk", blks, s).astype(F32)
    branch = (own * keep_own).astype(BF)
    return (stream, branch)


def solution(mesh):
    size = dict(mesh.shape)
    few = size["blk"] == 4 and size["heads"] == 2 and size["rows"] == 2

    def shards(*args):
        queries, cand_lengths = args[0], args[-2]
        toks = queries.shape[0] * size["blk"]
        direct = few and toks % 16 == 0 and toks * 2 <= LEN and cand_lengths.shape[0] == 1
        return (shards_direct if direct else shards_any)(*args)

    placed = (
        P(("groups", "blk", "rows"), "heads", None),
        P(("groups", "blk"), "heads", None),
        P(("groups", "blk"), "heads", None),
        P("groups", ("blk", "rows")),
        P(("blk", "rows")),
        P("heads", ("blk", "rows")),
        P(("blk", "rows")),
        P("heads", ("blk", "rows")),
        P("heads", ("blk", "rows")),
        P(("blk", "rows"), "heads"),
        P("groups"),
        P("groups", None),
    )
    return jax.shard_map(
        shards,
        mesh=mesh,
        in_specs=placed,
        out_specs=(P("groups", ("blk", "rows")), P(("groups", "blk", "rows"), "heads")),
        check_vma=False,
    )
```

```python
import jax
import jax.numpy as jnp
from jax import lax
from jax.experimental import pallas as pl
from jax.experimental.pallas import tpu as pltpu
from jax.sharding import PartitionSpec as P

LEN = 128
EPS = 1e-06
BF = jnp.bfloat16
F32 = jnp.float32


def token_masks(cand_lengths, masked_pos, tokens):
    positions = jnp.arange(tokens, dtype=jnp.int32) % LEN
    length_tok = jnp.repeat(cand_lengths, LEN)[:tokens]
    valid_tok = positions < length_tok
    slots = jnp.arange(LEN, dtype=jnp.int32)
    masked_tok = jnp.any(masked_pos[:, :, None] == slots[None, None, :], axis=1).reshape(-1)[
        :tokens
    ]
    return (valid_tok, masked_tok)


def shards_any(
    queries,
    src_keys,
    src_values,
    dec_state,
    mask_embed,
    out_weight,
    norm_gain,
    gate_weight,
    up_weight,
    down_weight,
    cand_lengths,
    masked_pos,
):
    tok_dev, local_heads, head_size = queries.shape
    kv_local = src_keys.shape[1]
    group_size = local_heads // kv_local
    score_scale = head_size ** (-0.5)
    features = dec_state.shape[1] * lax.axis_size("blk") * lax.axis_size("rows")
    queries_all = lax.all_gather(queries, "blk", axis=0, tiled=True)
    gathered_rows = queries_all.shape[0]
    grouped = queries_all.reshape(gathered_rows, kv_local, group_size, head_size)
    scores = (
        jnp.einsum("tgjd,kgd->tgjk", grouped, src_keys, preferred_element_type=F32) * score_scale
    )
    local_peak = jnp.max(scores, axis=3)
    weights = jnp.exp(scores - local_peak[..., None])
    totals = jnp.sum(weights, axis=3)
    numerator = jnp.einsum(
        "tgjk,kgd->tgjd", weights.astype(BF), src_values, preferred_element_type=F32
    )
    highest = lax.pmax(local_peak, "blk")
    factor = jnp.exp(local_peak - highest)
    numer_own, totals_own = (
        lax.psum_scatter(
            (numerator * factor[..., None]).astype(BF), "blk", scatter_dimension=0, tiled=True
        ).astype(F32),
        lax.psum_scatter(
            (totals * factor).astype(BF), "blk", scatter_dimension=0, tiled=True
        ).astype(F32),
    )
    attn_own = (
        (numer_own / totals_own[..., None]).astype(BF).reshape(tok_dev, local_heads * head_size)
    )
    attn_all = lax.all_gather(attn_own, ("blk", "rows"), axis=0, tiled=True)
    tokens = attn_all.shape[0]
    projected = lax.psum(
        jnp.dot(attn_all, out_weight, preferred_element_type=F32).astype(BF), "heads"
    ).astype(F32)
    valid_tok, masked_tok = token_masks(cand_lengths, masked_pos, tokens)
    base_state = jnp.where(masked_tok[:, None], mask_embed[None, :], dec_state).astype(F32)
    stream_mid = base_state + projected
    squares = lax.psum(jnp.sum(stream_mid * stream_mid, axis=1), ("blk", "rows"))
    inv_rms = lax.rsqrt(squares / features + EPS)[:, None]
    normed = (stream_mid * inv_rms * norm_gain.astype(F32)).astype(BF)
    keep_mask = valid_tok.astype(F32)[:, None]
    stream = (stream_mid * keep_mask).astype(BF)
    normed_full = lax.all_gather(normed, ("blk", "rows"), axis=1, tiled=True)
    feature_width = gate_weight.shape[0]
    column_block = lax.dynamic_slice_in_dim(
        normed_full, lax.axis_index("heads") * feature_width, feature_width, 1
    )
    gate_part = jnp.dot(column_block, gate_weight, preferred_element_type=F32)
    up_part = jnp.dot(column_block, up_weight, preferred_element_type=F32)
    gate_rows, up_rows = (
        lax.psum(gate_part.astype(BF), "heads").astype(F32),
        lax.psum(up_part.astype(BF), "heads").astype(F32),
    )
    hidden = (jax.nn.gelu(gate_rows, approximate=True) * up_rows).astype(BF)
    down_out = lax.psum_scatter(
        jnp.dot(hidden, down_weight, preferred_element_type=F32),
        ("blk", "rows"),
        scatter_dimension=0,
        tiled=True,
    )
    own_start = (lax.axis_index("blk") * lax.axis_size("rows") + lax.axis_index("rows")) * tok_dev
    keep_own = lax.dynamic_slice_in_dim(keep_mask, own_start, tok_dev, 0)
    return (stream, (down_out * keep_own).astype(BF))


VM = pl.BlockSpec(memory_space=pltpu.VMEM)
ANY = pl.BlockSpec(memory_space=pl.ANY)
MIB = 1 << 20


def hop(value, axis, size, step):
    return lax.ppermute(value, axis, [(i, i ^ step) for i in range(size)])


def kernel(body, name, outs, specs, args, limit=8, flops=0, aliases=None, scratch=()):
    near = [a for a, spec in zip(args, specs) if spec is VM]
    size = sum(a.size * a.dtype.itemsize for a in near + list(outs))
    return pl.pallas_call(
        body,
        out_shape=outs,
        in_specs=specs,
        out_specs=[VM] * len(outs),
        input_output_aliases=aliases or {},
        scratch_shapes=list(scratch),
        compiler_params=pltpu.CompilerParams(vmem_limit_bytes=limit * MIB),
        cost_estimate=pl.CostEstimate(flops=flops, bytes_accessed=size, transcendentals=0),
        name=name,
    )(*args)


def fetch(after, arrays, name, rows=None, into=None):
    n, skip = len(arrays), len(after)
    begun = list(into or [])

    def body(*refs):
        sources = refs[skip : skip + n]
        targets, sems = refs[-1 - n : -1], refs[-1]
        copies = []
        for i, (source, target) in enumerate(zip(sources, targets)):
            if rows is not None and rows[i] is not None:
                source, target = source.at[pl.ds(*rows[i])], target.at[pl.ds(*rows[i])]
            copies.append(pltpu.make_async_copy(source, target, sems.at[i]))
        for copy in copies:
            copy.start()
        for copy in copies:
            copy.wait()

    size = sum(a.size * a.dtype.itemsize for a in arrays)
    return pl.pallas_call(
        body,
        out_shape=[jax.ShapeDtypeStruct(a.shape, a.dtype) for a in arrays],
        in_specs=[ANY] * (skip + n) + [VM] * len(begun),
        out_specs=[VM] * n,
        input_output_aliases={skip + n + i: i for i in range(len(begun))},
        scratch_shapes=[pltpu.SemaphoreType.DMA((n,))],
        compiler_params=pltpu.CompilerParams(vmem_limit_bytes=MIB),
        cost_estimate=pl.CostEstimate(flops=0, bytes_accessed=2 * size, transcendentals=0),
        name=name,
    )(*after, *[pltpu.with_memory_space_constraint(a, pltpu.HBM) for a in arrays], *begun)


def parts_of(value, count):
    out = []
    for _ in range(count):
        part = lax.reduce_precision(value, 8, 7)
        out.append(part.astype(BF))
        value = value - part
    return out


def split_in(value, count):
    out = []
    for _ in range(count):
        part = value.astype(BF)
        out.append(part)
        value = value - part.astype(F32)
    return out


def shards_direct(
    queries,
    src_keys,
    src_values,
    dec_state,
    mask_embed,
    out_weight,
    norm_gain,
    gate_weight,
    up_weight,
    down_weight,
    cand_lengths,
    masked_pos,
):
    blks, head_parts = lax.axis_size("blk"), lax.axis_size("heads")
    blk, head, row = (lax.axis_index(name) for name in ("blk", "heads", "rows"))
    tok_dev, local_heads, head_size = queries.shape
    kv_local = src_keys.shape[1]
    group_size = local_heads // kv_local
    score_scale = head_size ** (-0.5)
    width = dec_state.shape[1]
    features = width * blks * 2
    half = blks // head_parts
    hidden_width, out_width = gate_weight.shape[1], down_weight.shape[1]
    toks = tok_dev * blks
    tokens = toks * 2
    sds = jax.ShapeDtypeStruct

    queries_near, dec_state, mask_embed, norm_gain, masked_pos = fetch(
        [], [queries, dec_state, mask_embed, norm_gain, masked_pos], "fetch_small"
    )
    blocks = [queries_near] * blks
    for s in [blks - 1] + list(range(1, blks - 1)):
        piece = hop(queries, "blk", blks, s)
        blocks = [jnp.where(blk == (k ^ s), piece, block) for k, block in enumerate(blocks)]
        blocks = list(lax.optimization_barrier(tuple(blocks)))
    q_all = jnp.concatenate(blocks, axis=0)
    grouped = q_all.reshape(toks, kv_local, group_size, head_size)
    scores = (
        jnp.einsum("tgjd,kgd->tgjk", grouped, src_keys, preferred_element_type=F32) * score_scale
    )
    peak = jnp.max(scores, axis=3)
    weights = jnp.exp(scores - peak[..., None])
    totals = jnp.sum(weights, axis=3)
    numerator = jnp.einsum(
        "tgjk,kgd->tgjd", weights.astype(BF), src_values, preferred_element_type=F32
    )
    partial = (numerator / totals[..., None]).astype(BF)
    partial = partial.transpose(1, 2, 0, 3).reshape(local_heads * toks, head_size)
    partial, peak, totals = lax.optimization_barrier((partial, peak, totals))
    level = (peak + jnp.log(totals)).reshape(toks, local_heads)
    side = jnp.concatenate(parts_of(level, 3), axis=1)
    side = jnp.pad(side, ((0, 0), (0, head_size - side.shape[1])))
    note = jnp.concatenate([partial, side], axis=0)
    notes = [note] + [hop(note, "blk", blks, s) for s in reversed(range(1, blks))]
    gate_cut = gate_weight.shape[0] * 2 // 48 * 16
    proj_near, gate_near = fetch(
        [note], [out_weight.T, gate_weight], "fetch_proj_gate", rows=[None, (0, gate_cut)]
    )

    def combine(*refs):
        ins, out = refs[:blks], refs[blks + 2]
        base = local_heads * toks
        levels = []
        for ref in ins:
            side = ref[base : base + toks, :].astype(F32)
            levels.append(
                side[:, :local_heads]
                + side[:, local_heads : 2 * local_heads]
                + side[:, 2 * local_heads : 3 * local_heads]
            )
        top = levels[0]
        for one in levels[1:]:
            top = jnp.maximum(top, one)
        shares = [jnp.exp(one - top) for one in levels]
        total = shares[0]
        for one in shares[1:]:
            total = total + one
        shares = [one / total for one in shares]
        for h in range(local_heads):
            acc = None
            for share, ref in zip(shares, ins):
                term = share[:, h : h + 1] * ref[h * toks : (h + 1) * toks, :].astype(F32)
                acc = term if acc is None else acc + term
            out[:, h * head_size : (h + 1) * head_size] = acc.astype(BF)

    attn, proj_near, gate_near = kernel(
        combine,
        "combine",
        [sds((toks, local_heads * head_size), BF), sds(proj_near.shape, BF), sds(gate_near.shape, BF)],
        [VM] * (blks + 2),
        notes + [proj_near, gate_near],
        aliases={blks: 1, blks + 1: 2},
    )
    other = hop(attn, "rows", 2, 1)
    across = (((1,), (1,)), ((), ()))

    def project_own(own_ref, weight_ref, gate_ref, out_ref, gate_out):
        out_ref[...] = lax.dot_general(
            own_ref[...], weight_ref[...], across, preferred_element_type=F32
        ).astype(BF)

    proj_own, gate_near = kernel(
        project_own,
        "project_own",
        [sds((toks, width), BF), sds(gate_near.shape, BF)],
        [VM] * 3,
        [attn, proj_near, gate_near],
        aliases={2: 1},
    )

    proj_own_across = hop(proj_own, "heads", 2, 1)

    def project(other_ref, weight_ref, gate_ref, out_ref, gate_out):
        out_ref[...] = lax.dot_general(
            other_ref[...], weight_ref[...], across, preferred_element_type=F32
        ).astype(BF)

    proj, gate_near = kernel(
        project,
        "project",
        [sds((toks, width), BF), sds(gate_near.shape, BF)],
        [VM] * 3,
        [other, proj_near, gate_near],
        aliases={2: 1},
    )
    proj_across = hop(proj, "heads", 2, 1)
    (gate_near,) = fetch(
        [proj],
        [gate_weight],
        "fetch_gate_last",
        rows=[(gate_cut, gate_weight.shape[0] - gate_cut)],
        into=[gate_near],
    )

    lanes = -(-(width + 2) // 128) * 128

    inner = [b * 2 + r for r in range(2) for b in range(blks)]
    outer = [r * blks + b for b in range(blks) for r in range(2)]

    def shuffled(value, order, scratch):
        for at, k in enumerate(order):
            scratch[at * tok_dev : (at + 1) * tok_dev] = value[k * tok_dev : (k + 1) * tok_dev]
        return scratch[...]

    def middle(
        dec_ref,
        embed_ref,
        gain_ref,
        masked_ref,
        own_ref,
        own_across_ref,
        other_ref,
        other_across_ref,
        gate_ref,
        mid_ref,
        note_ref,
        gate_out,
        base_ref,
    ):
        slots = lax.broadcasted_iota(jnp.int32, (tokens, 1), 0)
        hits = jnp.where(slots == masked_ref[...], 1.0, 0.0)
        masked = jnp.max(hits, axis=1, keepdims=True) > 0.0
        base = jnp.where(masked, embed_ref[...].astype(F32), dec_ref[...].astype(F32))
        base = shuffled(base, inner, base_ref)
        own = own_ref[...].astype(F32) + own_across_ref[...].astype(F32)
        other = other_ref[...].astype(F32) + other_across_ref[...].astype(F32)
        first = lax.axis_index("rows") == 0
        mid_ref[:toks] = base[:toks] + jnp.where(first, own, other)
        mid_ref[toks:] = base[toks:] + jnp.where(first, other, own)
        mid = mid_ref[...]
        note_ref[:, :width] = (mid * gain_ref[...].astype(F32)).astype(BF)
        squares = jnp.sum(mid * mid, axis=1, keepdims=True)
        high, low = split_in(squares, 2)
        lane = lax.broadcasted_iota(jnp.int32, (tokens, lanes - width), 1)
        note_ref[:, width:] = jnp.where(
            lane == 0, high.astype(F32), jnp.where(lane == 1, low.astype(F32), 0.0)
        ).astype(BF)

    mid, note, gate_near = kernel(
        middle,
        "middle",
        [
            sds((tokens, width), F32),
            sds((tokens, lanes), BF),
            sds(gate_near.shape, BF),
        ],
        [VM] * 9,
        [
            dec_state,
            mask_embed[None, :],
            norm_gain[None, :],
            masked_pos,
            proj_own,
            proj_own_across,
            proj,
            proj_across,
            gate_near,
        ],
        aliases={8: 2},
        scratch=[pltpu.VMEM((tokens, width), F32)],
    )

    def residual(mid_ref, length_ref, stream_ref, keep_ref, order_ref):
        slots = lax.broadcasted_iota(jnp.int32, (tokens, 1), 0)
        keep = jnp.where(slots < length_ref[...], 1.0, 0.0)
        stream_ref[...] = (shuffled(mid_ref[...], outer, order_ref) * keep).astype(BF)
        first = (lax.axis_index("blk") * 2 + lax.axis_index("rows")) * tok_dev
        owned = first + lax.broadcasted_iota(jnp.int32, (tok_dev, 1), 0)
        keep_ref[...] = jnp.where(owned < length_ref[...], 1.0, 0.0)

    stream, keep_own = kernel(
        residual,
        "residual",
        [sds((tokens, width), BF), sds((tok_dev, 1), F32)],
        [VM] * 2,
        [mid, cand_lengths[None, :]],
        scratch=[pltpu.VMEM((tokens, width), F32)],
    )

    far_pairs, near_pairs = [], []
    for b in range(blks):
        for h in range(head_parts):
            far_pairs.append((b * head_parts + h, (b ^ 3) * head_parts + h))
            to = (b ^ 2, h) if b // half == h else (b ^ 1, 1 - h)
            near_pairs.append((b * head_parts + h, to[0] * head_parts + to[1]))
    near = lax.ppermute(note, ("blk", "heads"), near_pairs)
    far = lax.ppermute(note, ("blk", "heads"), far_pairs)
    (up_near,) = fetch([note], [up_weight], "fetch_up")
    lanes_all = note.shape[1]

    def pick(own_ref, near_ref, far_ref, gate_ref, up_ref, kept_ref, out_ref):
        at = lax.axis_index("blk")
        inside = at // half == lax.axis_index("heads")
        odd = at % 2 == 1
        same = jnp.where(inside, own_ref[...], near_ref[...])
        pair = jnp.where(inside, near_ref[...], far_ref[...])
        out_ref[0] = jnp.where(odd, pair, same)
        out_ref[1] = jnp.where(odd, same, pair)

    (mine,) = kernel(
        pick,
        "pick",
        [sds((half, tokens, lanes_all), BF)],
        [VM, VM, VM, ANY, ANY, ANY],
        [note, near, far, gate_near, up_near, keep_own],
    )
    theirs = hop(mine, "rows", 2, 1)
    rows_in = gate_weight.shape[0]

    def tile_products(tiles_ref, weight_ref, row_at):
        total = None
        for k in range(half):
            start = pl.multiple_of((k * 2 + row_at) * width, 16)
            term = jnp.dot(
                tiles_ref[k, :, :width],
                weight_ref[pl.ds(start, width), :],
                preferred_element_type=F32,
            )
            total = term if total is None else total + term
        return total

    def inner_products(mine_ref, gate_ref, up_ref, gate_out, up_out):
        gate_out[...] = tile_products(mine_ref, gate_ref, lax.axis_index("rows"))
        up_out[...] = tile_products(mine_ref, up_ref, lax.axis_index("rows"))

    gate_own, up_own = kernel(
        inner_products,
        "inner_products",
        [sds((tokens, hidden_width), F32)] * 2,
        [VM, VM, VM],
        [mine, gate_near, up_near],
        flops=2 * tokens * rows_in * hidden_width,
    )

    cut = -(-hidden_width // 512) * 256
    pieces_at = [(0, cut), (cut, hidden_width)]

    def gate_up(lo, hi, with_squares):
        span = hi - lo

        def body(*refs):
            theirs_ref, gate_in, up_in, gate_w, up_w = refs[:5]
            out_ref, note_ref = refs[-2:]
            row_at = 1 - lax.axis_index("rows")
            for k, (own, weight) in enumerate(((gate_in, gate_w), (up_in, up_w))):
                value = own[:, lo:hi] + tile_products(theirs_ref, weight.at[:, lo:hi], row_at)
                out_ref[:, k * span : (k + 1) * span] = value
                note_ref[:, k * span : (k + 1) * span] = value.astype(BF)
            if with_squares:
                squares = None
                for k in range(half):
                    for ref in (refs[5], theirs_ref):
                        here = ref[k, :, width : width + 2].astype(F32)
                        squares = here if squares is None else squares + here
                squares = squares[:, 0:1] + squares[:, 1:2]
                high, low = split_in(squares, 2)
                lane = lax.broadcasted_iota(jnp.int32, (tokens, 128), 1)
                out_ref[:, 2 * span :] = jnp.where(lane == 0, squares, 0.0)
                note_ref[:, 2 * span :] = jnp.where(
                    lane == 0, high.astype(F32), jnp.where(lane == 1, low.astype(F32), 0.0)
                ).astype(BF)

        return body

    sums, sum_notes = [], []
    for c, (lo, hi) in enumerate(pieces_at):
        operands = [theirs, gate_own, up_own, gate_near, up_near] + [mine] * (c == 0)
        long_width = 2 * (hi - lo) + 128 * (c == 0)
        value, value_note = kernel(
            gate_up(lo, hi, c == 0),
            f"gate_up_{c}",
            [sds((tokens, long_width), F32), sds((tokens, long_width), BF)],
            [VM] * len(operands),
            operands,
            flops=tokens * rows_in * hidden_width,
        )
        sums.append(value)
        sum_notes.append(value_note)
    sum_others = [hop(value, "heads", 2, 1) for value in sum_notes]
    (down_near,) = fetch([sum_notes[-1]], [down_weight], "fetch_down")

    def down_piece(c, own_ref, other_ref, first_ref, first_other_ref, weight_ref):
        lo, hi = pieces_at[c]
        span, at = hi - lo, 2 * cut
        other = first_other_ref[:, at:].astype(F32)
        squares = first_ref[:, at : at + 1] + other[:, 0:1] + other[:, 1:2]
        inv_rms = lax.rsqrt(squares / features + EPS)
        gate, up = [
            (
                own_ref[:, k * span : (k + 1) * span]
                + other_ref[:, k * span : (k + 1) * span].astype(F32)
            )
            * inv_rms
            for k in range(2)
        ]
        hidden = (jax.nn.gelu(gate, approximate=True) * up).astype(BF)
        return jnp.dot(hidden, weight_ref[lo:hi, :], preferred_element_type=F32)

    def down_first(own_ref, other_ref, weight_ref, out_ref):
        out_ref[...] = down_piece(0, own_ref, other_ref, own_ref, other_ref, weight_ref)

    (down_part,) = kernel(
        down_first,
        "down_first",
        [sds((tokens, out_width), F32)],
        [VM] * 3,
        [sums[0], sum_others[0], down_near],
        flops=tokens * hidden_width * out_width,
    )

    def down_last(
        own_ref, other_ref, first_ref, first_other_ref, part_ref, weight_ref, keep_ref, away_ref
    ):
        down = part_ref[...] + down_piece(
            1, own_ref, other_ref, first_ref, first_other_ref, weight_ref
        )
        first = lax.axis_index("rows") == 0
        keep_ref[...] = jnp.where(first, down[:toks], down[toks:])
        away_ref[...] = jnp.where(first, down[toks:], down[:toks]).astype(BF)

    keep, away = kernel(
        down_last,
        "down_last",
        [sds((toks, out_width), F32), sds((toks, out_width), BF)],
        [VM] * 6,
        [sums[1], sum_others[1], sums[0], sum_others[0], down_part, down_near],
        limit=12,
    )
    back = hop(away, "rows", 2, 1)

    def owners(keep_ref, back_ref, own_ref, *piece_refs):
        total = keep_ref[...] + back_ref[...].astype(F32)
        blocks = [total[k * tok_dev : (k + 1) * tok_dev] for k in range(blks)]
        at = lax.axis_index("blk")
        for s, ref in enumerate((own_ref,) + piece_refs):
            value = blocks[0]
            for k in range(1, blks):
                value = jnp.where(at == (k ^ s), blocks[k], value)
            ref[...] = value.astype(ref.dtype)

    own, *sends = kernel(
        owners,
        "owners",
        [sds((tok_dev, out_width), F32)] + [sds((tok_dev, out_width), BF)] * (blks - 1),
        [VM, VM],
        [keep, back],
    )
    for s in range(1, blks):
        own = own + hop(sends[s - 1], "blk", blks, s).astype(F32)
    branch = (own * keep_own).astype(BF)
    return (stream, branch)


def solution(mesh):
    size = dict(mesh.shape)
    few = size["blk"] == 4 and size["heads"] == 2 and size["rows"] == 2

    def shards(*args):
        queries, cand_lengths = args[0], args[-2]
        toks = queries.shape[0] * size["blk"]
        direct = few and toks % 16 == 0 and toks * 2 <= LEN and cand_lengths.shape[0] == 1
        return (shards_direct if direct else shards_any)(*args)

    placed = (
        P(("groups", "blk", "rows"), "heads", None),
        P(("groups", "blk"), "heads", None),
        P(("groups", "blk"), "heads", None),
        P("groups", ("blk", "rows")),
        P(("blk", "rows")),
        P("heads", ("blk", "rows")),
        P(("blk", "rows")),
        P("heads", ("blk", "rows")),
        P("heads", ("blk", "rows")),
        P(("blk", "rows"), "heads"),
        P("groups"),
        P("groups", None),
    )
    return jax.shard_map(
        shards,
        mesh=mesh,
        in_specs=placed,
        out_specs=(P("groups", ("blk", "rows")), P(("groups", "blk", "rows"), "heads")),
        check_vma=False,
    )
```

```python
import jax
import jax.numpy as jnp
from jax import lax
from jax.experimental import pallas as pl
from jax.experimental.pallas import tpu as pltpu
from jax.sharding import PartitionSpec as P

LEN = 128
EPS = 1e-06
BF = jnp.bfloat16
F32 = jnp.float32


def token_masks(cand_lengths, masked_pos, tokens):
    positions = jnp.arange(tokens, dtype=jnp.int32) % LEN
    length_tok = jnp.repeat(cand_lengths, LEN)[:tokens]
    valid_tok = positions < length_tok
    slots = jnp.arange(LEN, dtype=jnp.int32)
    masked_tok = jnp.any(masked_pos[:, :, None] == slots[None, None, :], axis=1).reshape(-1)[
        :tokens
    ]
    return (valid_tok, masked_tok)


def shards_any(
    queries,
    src_keys,
    src_values,
    dec_state,
    mask_embed,
    out_weight,
    norm_gain,
    gate_weight,
    up_weight,
    down_weight,
    cand_lengths,
    masked_pos,
):
    tok_dev, local_heads, head_size = queries.shape
    kv_local = src_keys.shape[1]
    group_size = local_heads // kv_local
    score_scale = head_size ** (-0.5)
    features = dec_state.shape[1] * lax.axis_size("blk") * lax.axis_size("rows")
    queries_all = lax.all_gather(queries, "blk", axis=0, tiled=True)
    gathered_rows = queries_all.shape[0]
    grouped = queries_all.reshape(gathered_rows, kv_local, group_size, head_size)
    scores = (
        jnp.einsum("tgjd,kgd->tgjk", grouped, src_keys, preferred_element_type=F32) * score_scale
    )
    local_peak = jnp.max(scores, axis=3)
    weights = jnp.exp(scores - local_peak[..., None])
    totals = jnp.sum(weights, axis=3)
    numerator = jnp.einsum(
        "tgjk,kgd->tgjd", weights.astype(BF), src_values, preferred_element_type=F32
    )
    highest = lax.pmax(local_peak, "blk")
    factor = jnp.exp(local_peak - highest)
    numer_own, totals_own = (
        lax.psum_scatter(
            (numerator * factor[..., None]).astype(BF), "blk", scatter_dimension=0, tiled=True
        ).astype(F32),
        lax.psum_scatter(
            (totals * factor).astype(BF), "blk", scatter_dimension=0, tiled=True
        ).astype(F32),
    )
    attn_own = (
        (numer_own / totals_own[..., None]).astype(BF).reshape(tok_dev, local_heads * head_size)
    )
    attn_all = lax.all_gather(attn_own, ("blk", "rows"), axis=0, tiled=True)
    tokens = attn_all.shape[0]
    projected = lax.psum(
        jnp.dot(attn_all, out_weight, preferred_element_type=F32).astype(BF), "heads"
    ).astype(F32)
    valid_tok, masked_tok = token_masks(cand_lengths, masked_pos, tokens)
    base_state = jnp.where(masked_tok[:, None], mask_embed[None, :], dec_state).astype(F32)
    stream_mid = base_state + projected
    squares = lax.psum(jnp.sum(stream_mid * stream_mid, axis=1), ("blk", "rows"))
    inv_rms = lax.rsqrt(squares / features + EPS)[:, None]
    normed = (stream_mid * inv_rms * norm_gain.astype(F32)).astype(BF)
    keep_mask = valid_tok.astype(F32)[:, None]
    stream = (stream_mid * keep_mask).astype(BF)
    normed_full = lax.all_gather(normed, ("blk", "rows"), axis=1, tiled=True)
    feature_width = gate_weight.shape[0]
    column_block = lax.dynamic_slice_in_dim(
        normed_full, lax.axis_index("heads") * feature_width, feature_width, 1
    )
    gate_part = jnp.dot(column_block, gate_weight, preferred_element_type=F32)
    up_part = jnp.dot(column_block, up_weight, preferred_element_type=F32)
    gate_rows, up_rows = (
        lax.psum(gate_part.astype(BF), "heads").astype(F32),
        lax.psum(up_part.astype(BF), "heads").astype(F32),
    )
    hidden = (jax.nn.gelu(gate_rows, approximate=True) * up_rows).astype(BF)
    down_out = lax.psum_scatter(
        jnp.dot(hidden, down_weight, preferred_element_type=F32),
        ("blk", "rows"),
        scatter_dimension=0,
        tiled=True,
    )
    own_start = (lax.axis_index("blk") * lax.axis_size("rows") + lax.axis_index("rows")) * tok_dev
    keep_own = lax.dynamic_slice_in_dim(keep_mask, own_start, tok_dev, 0)
    return (stream, (down_out * keep_own).astype(BF))


VM = pl.BlockSpec(memory_space=pltpu.VMEM)
ANY = pl.BlockSpec(memory_space=pl.ANY)
MIB = 1 << 20


def hop(value, axis, size, step):
    return lax.ppermute(value, axis, [(i, i ^ step) for i in range(size)])


def kernel(body, name, outs, specs, args, limit=8, flops=0, aliases=None, scratch=()):
    near = [a for a, spec in zip(args, specs) if spec is VM]
    size = sum(a.size * a.dtype.itemsize for a in near + list(outs))
    return pl.pallas_call(
        body,
        out_shape=outs,
        in_specs=specs,
        out_specs=[VM] * len(outs),
        input_output_aliases=aliases or {},
        scratch_shapes=list(scratch),
        compiler_params=pltpu.CompilerParams(vmem_limit_bytes=limit * MIB),
        cost_estimate=pl.CostEstimate(flops=flops, bytes_accessed=size, transcendentals=0),
        name=name,
    )(*args)


def fetch(after, arrays, name, rows=None, into=None):
    n, skip = len(arrays), len(after)
    begun = list(into or [])

    def body(*refs):
        sources = refs[skip : skip + n]
        targets, sems = refs[-1 - n : -1], refs[-1]
        copies = []
        for i, (source, target) in enumerate(zip(sources, targets)):
            if rows is not None and rows[i] is not None:
                source, target = source.at[pl.ds(*rows[i])], target.at[pl.ds(*rows[i])]
            copies.append(pltpu.make_async_copy(source, target, sems.at[i]))
        for copy in copies:
            copy.start()
        for copy in copies:
            copy.wait()

    size = sum(a.size * a.dtype.itemsize for a in arrays)
    return pl.pallas_call(
        body,
        out_shape=[jax.ShapeDtypeStruct(a.shape, a.dtype) for a in arrays],
        in_specs=[ANY] * (skip + n) + [VM] * len(begun),
        out_specs=[VM] * n,
        input_output_aliases={skip + n + i: i for i in range(len(begun))},
        scratch_shapes=[pltpu.SemaphoreType.DMA((n,))],
        compiler_params=pltpu.CompilerParams(vmem_limit_bytes=MIB),
        cost_estimate=pl.CostEstimate(flops=0, bytes_accessed=2 * size, transcendentals=0),
        name=name,
    )(*after, *[pltpu.with_memory_space_constraint(a, pltpu.HBM) for a in arrays], *begun)


def parts_of(value, count):
    out = []
    for _ in range(count):
        part = lax.reduce_precision(value, 8, 7)
        out.append(part.astype(BF))
        value = value - part
    return out


def split_in(value, count):
    out = []
    for _ in range(count):
        part = value.astype(BF)
        out.append(part)
        value = value - part.astype(F32)
    return out


def shards_direct(
    queries,
    src_keys,
    src_values,
    dec_state,
    mask_embed,
    out_weight,
    norm_gain,
    gate_weight,
    up_weight,
    down_weight,
    cand_lengths,
    masked_pos,
):
    blks, head_parts = lax.axis_size("blk"), lax.axis_size("heads")
    blk, head, row = (lax.axis_index(name) for name in ("blk", "heads", "rows"))
    tok_dev, local_heads, head_size = queries.shape
    kv_local = src_keys.shape[1]
    group_size = local_heads // kv_local
    score_scale = head_size ** (-0.5)
    width = dec_state.shape[1]
    features = width * blks * 2
    half = blks // head_parts
    hidden_width, out_width = gate_weight.shape[1], down_weight.shape[1]
    toks = tok_dev * blks
    tokens = toks * 2
    sds = jax.ShapeDtypeStruct

    queries_near, dec_state, mask_embed, norm_gain, masked_pos = fetch(
        [], [queries, dec_state, mask_embed, norm_gain, masked_pos], "fetch_small"
    )
    blocks = [queries_near] * blks
    for s in [blks - 1] + list(range(1, blks - 1)):
        piece = hop(queries, "blk", blks, s)
        blocks = [jnp.where(blk == (k ^ s), piece, block) for k, block in enumerate(blocks)]
        blocks = list(lax.optimization_barrier(tuple(blocks)))
    q_all = jnp.concatenate(blocks, axis=0)
    grouped = q_all.reshape(toks, kv_local, group_size, head_size)
    scores = (
        jnp.einsum("tgjd,kgd->tgjk", grouped, src_keys, preferred_element_type=F32) * score_scale
    )
    peak = jnp.max(scores, axis=3)
    weights = jnp.exp(scores - peak[..., None])
    totals = jnp.sum(weights, axis=3)
    numerator = jnp.einsum(
        "tgjk,kgd->tgjd", weights.astype(BF), src_values, preferred_element_type=F32
    )
    partial = (numerator / totals[..., None]).astype(BF)
    partial = partial.transpose(1, 2, 0, 3).reshape(local_heads * toks, head_size)
    partial, peak, totals = lax.optimization_barrier((partial, peak, totals))
    level = (peak + jnp.log(totals)).reshape(toks, local_heads)
    side = jnp.concatenate(parts_of(level, 3), axis=1)
    side = jnp.pad(side, ((0, 0), (0, head_size - side.shape[1])))
    note = jnp.concatenate([partial, side], axis=0)
    notes = [note] + [hop(note, "blk", blks, s) for s in reversed(range(1, blks))]
    gate_cut = gate_weight.shape[0] * 2 // 48 * 16
    proj_near, gate_near = fetch(
        [note], [out_weight.T, gate_weight], "fetch_proj_gate", rows=[None, (0, gate_cut)]
    )

    def combine(*refs):
        ins, out = refs[:blks], refs[blks + 2]
        base = local_heads * toks
        levels = []
        for ref in ins:
            side = ref[base : base + toks, :].astype(F32)
            levels.append(
                side[:, :local_heads]
                + side[:, local_heads : 2 * local_heads]
                + side[:, 2 * local_heads : 3 * local_heads]
            )
        top = levels[0]
        for one in levels[1:]:
            top = jnp.maximum(top, one)
        shares = [jnp.exp(one - top) for one in levels]
        total = shares[0]
        for one in shares[1:]:
            total = total + one
        shares = [one / total for one in shares]
        for h in range(local_heads):
            acc = None
            for share, ref in zip(shares, ins):
                term = share[:, h : h + 1] * ref[h * toks : (h + 1) * toks, :].astype(F32)
                acc = term if acc is None else acc + term
            out[:, h * head_size : (h + 1) * head_size] = acc.astype(BF)

    attn, proj_near, gate_near = kernel(
        combine,
        "combine",
        [sds((toks, local_heads * head_size), BF), sds(proj_near.shape, BF), sds(gate_near.shape, BF)],
        [VM] * (blks + 2),
        notes + [proj_near, gate_near],
        aliases={blks: 1, blks + 1: 2},
    )
    other = hop(attn, "rows", 2, 1)
    across = (((1,), (1,)), ((), ()))

    def project_own(own_ref, weight_ref, gate_ref, out_ref, gate_out):
        out_ref[...] = lax.dot_general(
            own_ref[...], weight_ref[...], across, preferred_element_type=F32
        )

    proj_own, gate_near = kernel(
        project_own,
        "project_own",
        [sds((toks, width), F32), sds(gate_near.shape, BF)],
        [VM] * 3,
        [attn, proj_near, gate_near],
        aliases={2: 1},
    )

    def project(own_ref, other_ref, weight_ref, gate_ref, out_ref, gate_out):
        first = lax.axis_index("rows") == 0
        own = own_ref[...]
        other = lax.dot_general(
            other_ref[...], weight_ref[...], across, preferred_element_type=F32
        )
        out_ref[:toks] = jnp.where(first, own, other).astype(BF)
        out_ref[toks:] = jnp.where(first, other, own).astype(BF)

    proj, gate_near = kernel(
        project,
        "project",
        [sds((tokens, width), BF), sds(gate_near.shape, BF)],
        [VM] * 4,
        [proj_own, other, proj_near, gate_near],
        aliases={3: 1},
    )
    proj_other = hop(proj, "heads", 2, 1)
    (gate_near,) = fetch(
        [proj],
        [gate_weight],
        "fetch_gate_last",
        rows=[(gate_cut, gate_weight.shape[0] - gate_cut)],
        into=[gate_near],
    )

    lanes = -(-(width + 2) // 128) * 128

    inner = [b * 2 + r for r in range(2) for b in range(blks)]
    outer = [r * blks + b for b in range(blks) for r in range(2)]

    def shuffled(value, order, scratch):
        for at, k in enumerate(order):
            scratch[at * tok_dev : (at + 1) * tok_dev] = value[k * tok_dev : (k + 1) * tok_dev]
        return scratch[...]

    def middle(
        dec_ref,
        embed_ref,
        gain_ref,
        masked_ref,
        own_ref,
        other_ref,
        gate_ref,
        mid_ref,
        note_ref,
        gate_out,
        base_ref,
    ):
        slots = lax.broadcasted_iota(jnp.int32, (tokens, 1), 0)
        hits = jnp.where(slots == masked_ref[...], 1.0, 0.0)
        masked = jnp.max(hits, axis=1, keepdims=True) > 0.0
        base = jnp.where(masked, embed_ref[...].astype(F32), dec_ref[...].astype(F32))
        mid = shuffled(base, inner, base_ref) + (
            own_ref[...].astype(F32) + other_ref[...].astype(F32)
        )
        mid_ref[...] = mid
        note_ref[:, :width] = (mid * gain_ref[...].astype(F32)).astype(BF)
        squares = jnp.sum(mid * mid, axis=1, keepdims=True)
        high, low = split_in(squares, 2)
        lane = lax.broadcasted_iota(jnp.int32, (tokens, lanes - width), 1)
        note_ref[:, width:] = jnp.where(
            lane == 0, high.astype(F32), jnp.where(lane == 1, low.astype(F32), 0.0)
        ).astype(BF)

    mid, note, gate_near = kernel(
        middle,
        "middle",
        [
            sds((tokens, width), F32),
            sds((tokens, lanes), BF),
            sds(gate_near.shape, BF),
        ],
        [VM] * 7,
        [
            dec_state,
            mask_embed[None, :],
            norm_gain[None, :],
            masked_pos,
            proj,
            proj_other,
            gate_near,
        ],
        aliases={6: 2},
        scratch=[pltpu.VMEM((tokens, width), F32)],
    )

    def residual(mid_ref, length_ref, stream_ref, keep_ref, order_ref):
        slots = lax.broadcasted_iota(jnp.int32, (tokens, 1), 0)
        keep = jnp.where(slots < length_ref[...], 1.0, 0.0)
        stream_ref[...] = (shuffled(mid_ref[...], outer, order_ref) * keep).astype(BF)
        first = (lax.axis_index("blk") * 2 + lax.axis_index("rows")) * tok_dev
        owned = first + lax.broadcasted_iota(jnp.int32, (tok_dev, 1), 0)
        keep_ref[...] = jnp.where(owned < length_ref[...], 1.0, 0.0)

    stream, keep_own = kernel(
        residual,
        "residual",
        [sds((tokens, width), BF), sds((tok_dev, 1), F32)],
        [VM] * 2,
        [mid, cand_lengths[None, :]],
        scratch=[pltpu.VMEM((tokens, width), F32)],
    )

    far_pairs, near_pairs = [], []
    for b in range(blks):
        for h in range(head_parts):
            far_pairs.append((b * head_parts + h, (b ^ 3) * head_parts + h))
            to = (b ^ 2, h) if b // half == h else (b ^ 1, 1 - h)
            near_pairs.append((b * head_parts + h, to[0] * head_parts + to[1]))
    near = lax.ppermute(note, ("blk", "heads"), near_pairs)
    far = lax.ppermute(note, ("blk", "heads"), far_pairs)
    (up_near,) = fetch([note], [up_weight], "fetch_up")
    lanes_all = note.shape[1]

    def pick(own_ref, near_ref, far_ref, gate_ref, up_ref, kept_ref, out_ref):
        at = lax.axis_index("blk")
        inside = at // half == lax.axis_index("heads")
        odd = at % 2 == 1
        same = jnp.where(inside, own_ref[...], near_ref[...])
        pair = jnp.where(inside, near_ref[...], far_ref[...])
        out_ref[0] = jnp.where(odd, pair, same)
        out_ref[1] = jnp.where(odd, same, pair)

    (mine,) = kernel(
        pick,
        "pick",
        [sds((half, tokens, lanes_all), BF)],
        [VM, VM, VM, ANY, ANY, ANY],
        [note, near, far, gate_near, up_near, keep_own],
    )
    theirs = hop(mine, "rows", 2, 1)
    rows_in = gate_weight.shape[0]

    def tile_products(tiles_ref, weight_ref, row_at):
        total = None
        for k in range(half):
            start = pl.multiple_of((k * 2 + row_at) * width, 16)
            term = jnp.dot(
                tiles_ref[k, :, :width],
                weight_ref[pl.ds(start, width), :],
                preferred_element_type=F32,
            )
            total = term if total is None else total + term
        return total

    def inner_products(mine_ref, gate_ref, up_ref, gate_out, up_out):
        gate_out[...] = tile_products(mine_ref, gate_ref, lax.axis_index("rows"))
        up_out[...] = tile_products(mine_ref, up_ref, lax.axis_index("rows"))

    gate_own, up_own = kernel(
        inner_products,
        "inner_products",
        [sds((tokens, hidden_width), F32)] * 2,
        [VM, VM, VM],
        [mine, gate_near, up_near],
        flops=2 * tokens * rows_in * hidden_width,
    )

    cut, next_cut = 3 * hidden_width // 7, 5 * hidden_width // 7
    pieces_at = [(0, cut), (cut, next_cut), (next_cut, hidden_width)]

    def gate_up(lo, hi, with_squares):
        span = hi - lo

        def body(*refs):
            theirs_ref, gate_in, up_in, gate_w, up_w = refs[:5]
            out_ref, note_ref = refs[-2:]
            row_at = 1 - lax.axis_index("rows")
            for k, (own, weight) in enumerate(((gate_in, gate_w), (up_in, up_w))):
                value = own[:, lo:hi] + tile_products(theirs_ref, weight.at[:, lo:hi], row_at)
                out_ref[:, k * span : (k + 1) * span] = value
                note_ref[:, k * span : (k + 1) * span] = value.astype(BF)
            if with_squares:
                squares = None
                for k in range(half):
                    for ref in (refs[5], theirs_ref):
                        here = ref[k, :, width : width + 2].astype(F32)
                        squares = here if squares is None else squares + here
                squares = squares[:, 0:1] + squares[:, 1:2]
                high, low = split_in(squares, 2)
                lane = lax.broadcasted_iota(jnp.int32, (tokens, 128), 1)
                out_ref[:, 2 * span :] = jnp.where(lane == 0, squares, 0.0)
                note_ref[:, 2 * span :] = jnp.where(
                    lane == 0, high.astype(F32), jnp.where(lane == 1, low.astype(F32), 0.0)
                ).astype(BF)

        return body

    sums, sum_notes = [], []
    for c, (lo, hi) in enumerate(pieces_at):
        operands = [theirs, gate_own, up_own, gate_near, up_near] + [mine] * (c == 0)
        long_width = 2 * (hi - lo) + 128 * (c == 0)
        value, value_note = kernel(
            gate_up(lo, hi, c == 0),
            f"gate_up_{c}",
            [sds((tokens, long_width), F32), sds((tokens, long_width), BF)],
            [VM] * len(operands),
            operands,
            flops=tokens * rows_in * hidden_width,
        )
        sums.append(value)
        sum_notes.append(value_note)
    sum_others = [hop(value, "heads", 2, 1) for value in sum_notes]
    (down_near,) = fetch([sum_notes[-1]], [down_weight], "fetch_down")

    def down_piece(c, own_ref, other_ref, first_ref, first_other_ref, weight_ref):
        lo, hi = pieces_at[c]
        span, at = hi - lo, 2 * cut
        other = first_other_ref[:, at:].astype(F32)
        squares = first_ref[:, at : at + 1] + other[:, 0:1] + other[:, 1:2]
        inv_rms = lax.rsqrt(squares / features + EPS)
        gate, up = [
            (
                own_ref[:, k * span : (k + 1) * span]
                + other_ref[:, k * span : (k + 1) * span].astype(F32)
            )
            * inv_rms
            for k in range(2)
        ]
        hidden = (jax.nn.gelu(gate, approximate=True) * up).astype(BF)
        return jnp.dot(hidden, weight_ref[lo:hi, :], preferred_element_type=F32)

    def down_first(own_ref, other_ref, weight_ref, out_ref):
        out_ref[...] = down_piece(0, own_ref, other_ref, own_ref, other_ref, weight_ref)

    (down_part,) = kernel(
        down_first,
        "down_first",
        [sds((tokens, out_width), F32)],
        [VM] * 3,
        [sums[0], sum_others[0], down_near],
        flops=tokens * hidden_width * out_width,
    )

    def down_next(own_ref, other_ref, first_ref, first_other_ref, part_ref, weight_ref, out_ref):
        out_ref[...] = part_ref[...] + down_piece(
            1, own_ref, other_ref, first_ref, first_other_ref, weight_ref
        )

    (down_part,) = kernel(
        down_next,
        "down_next",
        [sds((tokens, out_width), F32)],
        [VM] * 6,
        [sums[1], sum_others[1], sums[0], sum_others[0], down_part, down_near],
        flops=tokens * hidden_width * out_width,
    )

    def down_last(
        own_ref, other_ref, first_ref, first_other_ref, part_ref, weight_ref, keep_ref, away_ref
    ):
        down = part_ref[...] + down_piece(
            2, own_ref, other_ref, first_ref, first_other_ref, weight_ref
        )
        first = lax.axis_index("rows") == 0
        keep_ref[...] = jnp.where(first, down[:toks], down[toks:])
        away_ref[...] = jnp.where(first, down[toks:], down[:toks]).astype(BF)

    keep, away = kernel(
        down_last,
        "down_last",
        [sds((toks, out_width), F32), sds((toks, out_width), BF)],
        [VM] * 6,
        [sums[2], sum_others[2], sums[0], sum_others[0], down_part, down_near],
        limit=12,
    )
    back = hop(away, "rows", 2, 1)

    def owners(keep_ref, back_ref, own_ref, *piece_refs):
        total = keep_ref[...] + back_ref[...].astype(F32)
        blocks = [total[k * tok_dev : (k + 1) * tok_dev] for k in range(blks)]
        at = lax.axis_index("blk")
        for s, ref in enumerate((own_ref,) + piece_refs):
            value = blocks[0]
            for k in range(1, blks):
                value = jnp.where(at == (k ^ s), blocks[k], value)
            ref[...] = value.astype(ref.dtype)

    own, *sends = kernel(
        owners,
        "owners",
        [sds((tok_dev, out_width), F32)] + [sds((tok_dev, out_width), BF)] * (blks - 1),
        [VM, VM],
        [keep, back],
    )
    for s in range(1, blks):
        own = own + hop(sends[s - 1], "blk", blks, s).astype(F32)
    branch = (own * keep_own).astype(BF)
    return (stream, branch)


def solution(mesh):
    size = dict(mesh.shape)
    few = size["blk"] == 4 and size["heads"] == 2 and size["rows"] == 2

    def shards(*args):
        queries, cand_lengths = args[0], args[-2]
        toks = queries.shape[0] * size["blk"]
        direct = few and toks % 16 == 0 and toks * 2 <= LEN and cand_lengths.shape[0] == 1
        return (shards_direct if direct else shards_any)(*args)

    placed = (
        P(("groups", "blk", "rows"), "heads", None),
        P(("groups", "blk"), "heads", None),
        P(("groups", "blk"), "heads", None),
        P("groups", ("blk", "rows")),
        P(("blk", "rows")),
        P("heads", ("blk", "rows")),
        P(("blk", "rows")),
        P("heads", ("blk", "rows")),
        P("heads", ("blk", "rows")),
        P(("blk", "rows"), "heads"),
        P("groups"),
        P("groups", None),
    )
    return jax.shard_map(
        shards,
        mesh=mesh,
        in_specs=placed,
        out_specs=(P("groups", ("blk", "rows")), P(("groups", "blk", "rows"), "heads")),
        check_vma=False,
    )
```
